32 devices in a mesh: group: 2 (over y), row: 4 (over x, core), col: 4 (over z).
Axes of the slice: x: 2, y: 2, z: 4, core: 2. Of those that a mesh axis runs over, the one named last changes fastest.
Arguments:
- hidden_in: bfloat16 [4096, 2048], P(('group', 'row'), 'col'), may hold values from -6 to 6
- segments: int32 [2, 2048], P('group'), may hold values from 0 to 7, never falling along the last dimension, each value on 1 to 1024 neighbouring positions
- attn_gain: float32 [2048], P('col'), may hold values from 0.5 to 1.5
- query_weight: bfloat16 [2048, 2048], P('col', 'row'), may hold values from -1.25 to 1.25
- key_matrix: bfloat16 [2048, 512], P('col', 'row'), may hold values from -1.25 to 1.25
- value_matrix: bfloat16 [2048, 512], P('col', 'row'), may hold values from -0.125 to 0.125
- out_weight: bfloat16 [2048, 2048], P('row', 'col'), may hold values from -4 to 4
- ffn_gain: float32 [2048], P('col'), may hold values from 0.5 to 1.5
- gate_weight: bfloat16 [2048, 8192], P('col', 'row'), may hold values from -0.125 to 0.125
- up_weight: bfloat16 [2048, 8192], P('col', 'row'), may hold values from -0.125 to 0.125
- down_weight: bfloat16 [8192, 2048], P('row', 'col'), may hold values from -1.25 to 1.25
- cotangent: bfloat16 [4096, 2048], P(('group', 'row'), 'col'), may hold values from -6 to 6
Outputs:
- layer_out: bfloat16 [4096, 2048], P(('group', 'row'), 'col')
- input_grad: float32 [4096, 2048], P(('group', 'row'), 'col')
- attn_gain_grad: float32 [2048], P('col')
- query_grad: float32 [2048, 2048], P('col', 'row')
- key_grad: float32 [2048, 512], P('col', 'row')
- value_grad: float32 [2048, 512], P('col', 'row')
- out_grad: float32 [2048, 2048], P('row', 'col')
- ffn_gain_grad: float32 [2048], P('col')
- gate_grad: float32 [2048, 8192], P('col', 'row')
- up_grad: float32 [2048, 8192], P('col', 'row')
- down_grad: float32 [8192, 2048], P('row', 'col')
The draws below stay inside these ranges and needn't reach their ends.
Inputs may be any that keep to these rules, and one draw needn't show every extreme that they name: `segments`: in each sequence the segment numbers start at 0, never fall and take every value up to 7; a document holds 1 to 1024 tokens, and one document of every sequence holds exactly 1024.
All inputs are finite; a program needn't handle non-finite values.
Results may differ from the reference program's by a relative error of at most 0.02.
Values may be sent and summed in bfloat16 or wider, within the bound.
A program may use at most 192 MiB of HBM per device.

```python
import math
import jax
import jax.numpy as jnp
import numpy as np
from jax import lax

MODEL_WIDTH = 2048
QUERY_HEADS = 32
KEY_VALUE_HEADS = 8
HEAD_SIZE = 64
FF = 8192
SEQUENCE_LENGTH = 2048
NSEQ = 2
TOKENS = 4096


def level_of(key, shape, cuts, smallest, high):
    def one(axis_at, blocks):
        heights = jax.random.uniform(jax.random.fold_in(jax.random.fold_in(key, 6), axis_at), (blocks,), jnp.float32, smallest / len(cuts), high / len(cuts))
        return jnp.repeat(jnp.exp(heights), shape[axis_at] // blocks).reshape((-1,) + (1,) * (len(shape) - axis_at - 1))

    factor_of = one(*cuts[0])
    for cut in cuts[1:]:
        factor_of = factor_of * one(*cut)
    return factor_of


def length_profile(amount, total, bound, slope):
    portions = [(1 << 20) // math.isqrt(grade ** slope) + 1 for grade in range(2, amount + 1)]
    spare, given = total - bound - (amount - 1), [1] * (amount - 1)
    while spare > 0:
        candidates = [i for i in range(amount - 1) if given[i] < bound]
        pool, budget = sum([portions[i] for i in candidates]), spare
        for i in candidates:
            addition = min(bound - given[i], max(1, budget * portions[i] // pool), spare)
            given[i] = given[i] + addition
            spare = spare - addition
    return np.array([bound] + given)


def ragged_sizes(own_key, amount, total, reach, skew):
    if amount == 2:
        one = jax.random.randint(own_key, (), max(1, total - reach), min(reach, total - 1) + 1)
        return jnp.stack([one, total - one])
    sizes = jnp.asarray(length_profile(amount, total, reach, skew), jnp.int32)
    twos = (amount - 1) // 2
    giver, sink = sizes[1:1 + 2 * twos:2], sizes[2:2 + 2 * twos:2]
    slack = jnp.minimum(giver - 1, reach - sink)
    shifted = jax.random.randint(jax.random.fold_in(own_key, 1), (twos,), 0, 1 << 20) % (slack + 1)
    sizes = sizes.at[1:1 + 2 * twos:2].set(giver - shifted).at[2:2 + 2 * twos:2].set(sink + shifted)
    return sizes[jax.random.permutation(jax.random.fold_in(own_key, 2), amount)]


def noise(own_key, extent, scale, most, split=(), held_as=jnp.bfloat16):
    entries = scale * jax.random.normal(own_key, extent, jnp.float32)
    if split:
        entries = entries * level_of(own_key, extent, split, -0.22, 0.18)
    return jnp.clip(entries, -most, most).astype(held_as)


def setup_inputs(seed: int = 0) -> dict:
    arg_keys = jax.random.split(jax.random.key(seed), 13)
    return {
        "hidden_in": noise(arg_keys[0], (TOKENS, MODEL_WIDTH), 1.0, 6.0, ((0, 8), (1, 4))),
        "segments": jax.vmap(lambda own: jnp.searchsorted(jnp.cumsum(ragged_sizes(own, 8, SEQUENCE_LENGTH, SEQUENCE_LENGTH // 2, 2)), jnp.arange(SEQUENCE_LENGTH), side="right"))(jax.random.split(arg_keys[1], NSEQ)).reshape((NSEQ, SEQUENCE_LENGTH)).astype(jnp.int32),
        "attn_gain": jnp.clip(1.0 + 0.1 * jax.random.normal(arg_keys[2], (MODEL_WIDTH,), jnp.float32), 0.5, 1.5),
        "query_weight": noise(arg_keys[3], (MODEL_WIDTH, QUERY_HEADS * HEAD_SIZE), 0.088, 1.25, ((0, 4), (1, 4))),
        "key_matrix": noise(arg_keys[4], (MODEL_WIDTH, KEY_VALUE_HEADS * HEAD_SIZE), 0.088, 1.25, ((0, 4), (1, 4))),
        "value_matrix": noise(arg_keys[5], (MODEL_WIDTH, KEY_VALUE_HEADS * HEAD_SIZE), MODEL_WIDTH ** -0.5, 0.125, ((0, 4), (1, 4))),
        "out_weight": noise(arg_keys[6], (QUERY_HEADS * HEAD_SIZE, MODEL_WIDTH), 0.25, 4.0, ((0, 4), (1, 4))),
        "ffn_gain": jnp.clip(1.0 + 0.1 * jax.random.normal(arg_keys[7], (MODEL_WIDTH,), jnp.float32), 0.5, 1.5),
        "gate_weight": noise(arg_keys[8], (MODEL_WIDTH, FF), MODEL_WIDTH ** -0.5, 0.125, ((0, 4), (1, 4))),
        "up_weight": noise(arg_keys[9], (MODEL_WIDTH, FF), MODEL_WIDTH ** -0.5, 0.125, ((0, 4), (1, 4))),
        "down_weight": noise(arg_keys[10], (FF, MODEL_WIDTH), 0.09, 1.25, ((0, 4), (1, 4))),
        "cotangent": noise(arg_keys[11], (TOKENS, MODEL_WIDTH), 1.0, 6.0, ((0, 8), (1, 4))),
    }


NORM_EPS = 1e-05
ROPE_BASE = 10000000.0
RES_SCALE = 0.22
SCORE_SCALE = 0.015625

@jax.custom_vjp
def lowered_input(v):
    return lax.optimization_barrier(v.astype(jnp.bfloat16)).astype(jnp.float32)

@jax.custom_vjp
def lowered_gradient(v):
    return v

def low_keep(v):
    return (lowered_input(v), None)

def low_pass(kept, grad):
    return (grad,)

def back_keep(v):
    return (v, None)

def back_low(kept, grad):
    return (lowered_input(grad),)
lowered_input.defvjp(low_keep, low_pass)
lowered_gradient.defvjp(back_keep, back_low)

def matrix_product(left, right):
    return jnp.dot(left, right, precision=lax.Precision.HIGHEST)

def rms_norm(operand, gain_vec):
    norm_scale = lax.rsqrt(lax.optimization_barrier(jnp.mean(operand * operand, axis=-1, keepdims=True)) + NORM_EPS)
    return operand * norm_scale * gain_vec

def rope_tables(segments):
    length_total = segments.shape[1]
    places = jnp.arange(length_total, dtype=jnp.int32)
    starts = jnp.concatenate([jnp.ones((segments.shape[0], 1), jnp.bool_), segments[:, 1:] != segments[:, :-1]], axis=1)
    first_place = lax.cummax(jnp.where(starts, places[None, :], 0), axis=1)
    offset = (places[None, :] - first_place).reshape(-1).astype(jnp.float32)
    half_width = HEAD_SIZE // 2
    inverse = ROPE_BASE ** (-(2.0 * jnp.arange(half_width, dtype=jnp.float32)) / HEAD_SIZE)
    angles = offset[:, None] * inverse[None, :]
    return (jnp.cos(angles)[:, None, :], jnp.sin(angles)[:, None, :])

def rotate(operand, cosine, sine_table):
    half_width = operand.shape[-1] // 2
    first_half = operand[..., :half_width]
    second = operand[..., half_width:]
    return jnp.concatenate([first_half * cosine - second * sine_table, second * cosine + first_half * sine_table], axis=-1)

def kv_group(query_rows, key_rows, value_rows, live_mask):
    scores = jnp.einsum('qrd,kd->rqk', query_rows, key_rows, precision=lax.Precision.HIGHEST) * SCORE_SCALE
    scores = jnp.where(live_mask[None], lowered_gradient(scores), -1e+30)
    row_max = lax.optimization_barrier(jnp.max(scores, axis=2, keepdims=True))
    numerator = jnp.exp(scores - row_max)
    weights = numerator / lax.optimization_barrier(jnp.sum(numerator, axis=2, keepdims=True))
    return jnp.einsum('rqk,kd->qrd', lowered_input(weights), value_rows, precision=lax.Precision.HIGHEST)

def one_sequence(query_rows, key_rows, value_rows, seg_row):
    length_total = seg_row.shape[0]
    places = jnp.arange(length_total, dtype=jnp.int32)
    live_mask = (places[None, :] <= places[:, None]) & (seg_row[None, :] == seg_row[:, None])
    grouped_heads = query_rows.reshape(length_total, KEY_VALUE_HEADS, QUERY_HEADS // KEY_VALUE_HEADS, HEAD_SIZE).transpose(1, 0, 2, 3)

    def per_group(members):
        return kv_group(members[0], members[1], members[2], live_mask)
    result = lax.map(jax.checkpoint(per_group), (grouped_heads, key_rows.transpose(1, 0, 2), value_rows.transpose(1, 0, 2)))
    return result.transpose(1, 0, 2, 3).reshape(length_total, QUERY_HEADS, HEAD_SIZE)

def forward(residual, attn_gain, query_weight, key_matrix, value_matrix, out_weight, ffn_gain, gate_weight, up_weight, down_weight, segments):
    count_tokens = residual.shape[0]
    sequence_list = segments.shape[0]
    cosine, sine_table = rope_tables(segments)
    normalized_input = lowered_input(rms_norm(residual, attn_gain))
    query_pre = lowered_gradient(matrix_product(normalized_input, query_weight)).reshape(count_tokens, QUERY_HEADS, HEAD_SIZE)
    key_unrotated = lowered_gradient(matrix_product(normalized_input, key_matrix)).reshape(count_tokens, KEY_VALUE_HEADS, HEAD_SIZE)
    value_rows = lowered_input(lowered_gradient(matrix_product(normalized_input, value_matrix))).reshape(count_tokens, KEY_VALUE_HEADS, HEAD_SIZE)
    query_rotated = lowered_input(rotate(query_pre, cosine, sine_table))
    key_rotated = lowered_input(rotate(key_unrotated, cosine, sine_table))

    def sequence_wise(members):
        return one_sequence(members[0], members[1], members[2], members[3])
    attention_output = lax.map(jax.checkpoint(sequence_wise), (query_rotated.reshape(sequence_list, SEQUENCE_LENGTH, QUERY_HEADS, HEAD_SIZE), key_rotated.reshape(sequence_list, SEQUENCE_LENGTH, KEY_VALUE_HEADS, HEAD_SIZE), value_rows.reshape(sequence_list, SEQUENCE_LENGTH, KEY_VALUE_HEADS, HEAD_SIZE), segments))
    heads_out = lowered_input(lowered_gradient(attention_output.reshape(count_tokens, QUERY_HEADS * HEAD_SIZE)))
    resid_mid = residual + RES_SCALE * lowered_gradient(matrix_product(heads_out, out_weight))
    normed_two = lowered_input(rms_norm(resid_mid, ffn_gain))
    gate_pre = lowered_gradient(matrix_product(normed_two, gate_weight))
    up_pre = lowered_gradient(matrix_product(normed_two, up_weight))
    hidden_act = lowered_input(jax.nn.silu(gate_pre) * up_pre)
    return resid_mid + RES_SCALE * lowered_gradient(matrix_product(hidden_act, down_weight))

def reference(hidden_in, segments, attn_gain, query_weight, key_matrix, value_matrix, out_weight, ffn_gain, gate_weight, up_weight, down_weight, cotangent):
    params = tuple((operand.astype(jnp.float32) for operand in (hidden_in, attn_gain, query_weight, key_matrix, value_matrix, out_weight, ffn_gain, gate_weight, up_weight, down_weight)))

    def wrapped(residual, gain_one, weight_q, weight_k, weight_v, weight_o, gain_two, weight_g, weight_u, weight_d):
        return forward(residual, gain_one, weight_q, weight_k, weight_v, weight_o, gain_two, weight_g, weight_u, weight_d, segments)
    layer_out, pullback = jax.vjp(wrapped, params[0], params[1], params[2], params[3], params[4], params[5], params[6], params[7], params[8], params[9])
    grads = pullback(cotangent.astype(jnp.float32))
    return (layer_out.astype(jnp.bfloat16), grads[0], grads[1], grads[2], grads[3], grads[4], grads[5], grads[6], grads[7], grads[8], grads[9])
```

```python
import functools

import jax
import jax.numpy as jnp
from jax import lax
from jax.experimental import pallas as pl
from jax.experimental.pallas import tpu as pltpu
from jax.sharding import PartitionSpec as P

F32, BF16 = jnp.float32, jnp.bfloat16
MESH = pl.DeviceIdType.MESH
DMA = pltpu.SemaphoreType.DMA

MODEL_WIDTH = 2048
HEAD_SIZE = 64
NORM_EPS = 1e-05
ROPE_BASE = 10000000.0
RES_SCALE = 0.22
SCORE_SCALE = 0.015625

NR = 4
BQ = 256
NEG = -1e30


def dot(a, b, dims):
    return lax.dot_general(a, b, (dims, ((), ())), preferred_element_type=F32)


def place():
    group, row, col = lax.axis_index("group"), lax.axis_index("row"), lax.axis_index("col")
    other_core = row + 1 - 2 * lax.rem(row, 2)
    other_x = lax.rem(row + 2, NR)
    both = other_x + 1 - 2 * lax.rem(row, 2)
    return group, row, col, other_core, other_x, both


def greet(devices):
    barrier = pltpu.get_barrier_semaphore()
    for device in devices:
        pl.semaphore_signal(barrier, inc=1, device_id=device, device_id_type=MESH)
    return barrier


def block_at(ref, row, col, shape):
    b0, b1 = shape
    return ref.at[pl.ds(pl.multiple_of(row * b0, b0), b0), pl.ds(pl.multiple_of(col * b1, b1), b1)]


def gather_kernel(n, nz, *refs):
    ins, outs = refs[:n], refs[n : 2 * n]
    local_sem, send_sem, recv_sem = refs[2 * n :]
    g, r, z, rc, rx, rxc = place()
    has_left, has_right = z > 0, z < nz - 1
    barrier = greet([(g, rc, z), (g, rx, z)])

    @pl.when(has_left)
    def _():
        pl.semaphore_signal(barrier, inc=1, device_id=(g, r, z - 1), device_id_type=MESH)

    @pl.when(has_right)
    def _():
        pl.semaphore_signal(barrier, inc=1, device_id=(g, r, z + 1), device_id_type=MESH)

    pl.semaphore_wait(barrier, 2 + has_left.astype(jnp.int32) + has_right.astype(jnp.int32))

    right, left, over_x, to_core = 0, nz - 1, 2 * (nz - 1), 3 * nz - 2

    def slot(i, row, col):
        return block_at(outs[i], row, col, ins[i].shape)

    def copy(i, src, row, col, where, device):
        return pltpu.make_async_remote_copy(
            src_ref=src,
            dst_ref=slot(i, row, col),
            send_sem=send_sem.at[i, where],
            recv_sem=recv_sem.at[i, row, col],
            device_id=device,
            device_id_type=MESH,
        )

    def own(i, where, device):
        return copy(i, ins[i], r, z, where, device)

    def forward(i, row, col, where, device):
        return copy(i, slot(i, row, col), row, col, where, device)

    def rank(col):
        return col - (col > z).astype(jnp.int32)

    def local(i):
        return pltpu.make_async_copy(ins[i], slot(i, r, z), local_sem.at[i])

    for i in range(n):
        local(i).start()

        @pl.when(has_right)
        def _():
            own(i, right, (g, r, z + 1)).start()

        @pl.when(has_left)
        def _():
            own(i, left, (g, r, z - 1)).start()

        own(i, over_x, (g, rx, z)).start()
        own(i, to_core, (g, rc, z)).start()

    def from_x(i, col, where):
        forward(i, rx, col, where, (g, rx, z)).wait_recv()
        forward(i, rx, col, where, (g, rc, z)).start()

    for i in range(n):
        from_x(i, z, to_core + 1)
    for k in range(1, nz):
        for i in range(n):

            @pl.when(z - k >= 0)
            def _():
                col = z - k
                forward(i, r, col, right, (g, rc, z)).wait_recv()
                if k < nz - 1:

                    @pl.when(has_right)
                    def _():
                        forward(i, r, col, right + k, (g, r, z + 1)).start()

                forward(i, r, col, over_x + 1 + rank(col), (g, rx, z)).start()
                forward(i, r, col, to_core + 2 + rank(col), (g, rc, z)).start()

            @pl.when(z + k < nz)
            def _():
                col = z + k
                forward(i, r, col, left, (g, rc, z)).wait_recv()
                if k < nz - 1:

                    @pl.when(has_left)
                    def _():
                        forward(i, r, col, left + k, (g, r, z - 1)).start()

                forward(i, r, col, over_x + 1 + rank(col), (g, rx, z)).start()
                forward(i, r, col, to_core + 2 + rank(col), (g, rc, z)).start()

        for i in range(n):

            @pl.when(z - k >= 0)
            def _():
                from_x(i, z - k, to_core + nz + 1 + z - k)

            @pl.when(z + k < nz)
            def _():
                from_x(i, z + k, to_core + nz + z + k)

    for i in range(n):
        for col in range(nz):
            forward(i, rc, col, to_core, (g, rc, z)).wait_recv()
            forward(i, rxc, col, to_core, (g, rc, z)).wait_recv()
        local(i).wait()
        for where in range(to_core + 2 * nz):

            def sent(where=where):
                own(i, where, (g, rc, z)).wait_send()

            if where < left:
                pl.when(has_right & (z - where >= 0))(sent)
            elif where < over_x:
                pl.when(has_left & (z + (where - left) < nz))(sent)
            else:
                sent()


def gather(arrays, collective_id):
    n, nz = len(arrays), lax.axis_size("col")
    anywhere = pl.BlockSpec(memory_space=pl.ANY)
    return pl.pallas_call(
        functools.partial(gather_kernel, n, nz),
        out_shape=[
            jax.ShapeDtypeStruct((a.shape[0] * NR, a.shape[1] * nz), a.dtype) for a in arrays
        ],
        in_specs=[anywhere] * n,
        out_specs=[anywhere] * n,
        scratch_shapes=[DMA((n,)), DMA((n, 5 * nz - 2)), DMA((n, NR, nz))],
        compiler_params=pltpu.CompilerParams(collective_id=collective_id, has_side_effects=True),
        cost_estimate=pl.CostEstimate(flops=0, bytes_accessed=60 * 2**20, transcendentals=0),
        name="gather",
    )(*arrays)


def in_rows(total, step, body):
    step = min(step, total)
    if total == step:
        body(pl.ds(0, step))
    else:

        def one(i, carry):
            body(pl.ds(pl.multiple_of(i * step, step), step))
            return carry

        lax.fori_loop(0, total // step, one, 0)


def scatter_kernel(n, nz, *refs):
    ins, outs = refs[:n], refs[n : 2 * n]
    bufs = [refs[2 * n + 6 * i : 2 * n + 6 * (i + 1)] for i in range(n)]
    load_sem, core_send, core_recv, x_send, x_recv, z_send, z_recv = refs[8 * n :]
    g, r, z, rc, rx, rxc = place()
    barrier = greet(
        [(g, rc, z), (g, rx, z)] + [(g, r, lax.rem(z + k, nz)) for k in range(1, nz)]
    )
    pl.semaphore_wait(barrier, nz + 1)
    order = [(nz // 2 + k) % nz for k in range(nz // 2)] + list(range(nz // 2 - 1, 0, -1)) + [0]

    def block(i, row, step):
        b0, b1 = ins[i].shape[0] // NR, ins[i].shape[1] // nz
        return block_at(ins[i], row, lax.rem(z + order[step], nz), (b0, b1))

    def load(i, way, step):
        return pltpu.make_async_copy(
            block(i, (rx, r)[way], step), bufs[i][0].at[way, step], load_sem.at[i, way, step]
        )

    def remote(src, dst, send, recv, device):
        return pltpu.make_async_remote_copy(
            src_ref=src,
            dst_ref=dst,
            send_sem=send,
            recv_sem=recv,
            device_id=device,
            device_id_type=MESH,
        )

    def core(i, way, step):
        return remote(
            block(i, (rxc, rc)[way], step),
            bufs[i][1].at[way, step],
            core_send.at[i, way, step],
            core_recv.at[i, way, step],
            (g, rc, z),
        )

    def over_x(i, step):
        return remote(
            bufs[i][2].at[step], bufs[i][3].at[step], x_send.at[i, step], x_recv.at[i, step], (g, rx, z)
        )

    def along_z(i, step):
        return remote(
            bufs[i][4].at[step],
            bufs[i][5].at[step],
            z_send.at[i, step],
            z_recv.at[i, step],
            (g, r, lax.rem(z + order[step], nz)),
        )

    for i in range(n):
        for way in range(2):
            for step in range(nz):
                core(i, way, step).start()
                load(i, way, step).start()
    for i in range(n):
        own, from_core, half, from_x, mine, from_z = bufs[i]
        for step in range(nz):
            load(i, 0, step).wait()
            core(i, 0, step).wait_recv()

            def add(rows):
                half[step, rows, :] = (
                    own[0, step, rows, :].astype(F32) + from_core[0, step, rows, :].astype(F32)
                ).astype(half.dtype)

            in_rows(own.shape[2], 64, add)
            over_x(i, step).start()
    for i in range(n):
        own, from_core, half, from_x, mine, from_z = bufs[i]

        def total(step, rows):
            return (
                own[1, step, rows, :].astype(F32)
                + from_core[1, step, rows, :].astype(F32)
                + from_x[step, rows, :].astype(F32)
            )

        for step in range(nz):
            load(i, 1, step).wait()
            core(i, 1, step).wait_recv()
            over_x(i, step).wait_recv()
            if step < nz - 1:

                def add(rows):
                    mine[step, rows, :] = total(step, rows).astype(mine.dtype)

                in_rows(own.shape[2], 64, add)
                along_z(i, step).start()
    for i in range(n):
        own, from_core, half, from_x, mine, from_z = bufs[i]
        for step in range(nz - 1):
            along_z(i, step).wait_recv()

        def finish(rows):
            result = (
                own[1, nz - 1, rows, :].astype(F32)
                + from_core[1, nz - 1, rows, :].astype(F32)
                + from_x[nz - 1, rows, :].astype(F32)
            )
            for step in range(nz - 1):
                result = result + from_z[step, rows, :].astype(F32)
            outs[i][rows, :] = result

        in_rows(own.shape[2], 64, finish)
    for i in range(n):
        for step in range(nz):
            core(i, 0, step).wait_send()
            core(i, 1, step).wait_send()
            over_x(i, step).wait_send()
            if step < nz - 1:
                along_z(i, step).wait_send()


def reduce_scatter(arrays, collective_id):
    n, nz = len(arrays), lax.axis_size("col")
    scratch = []
    for a in arrays:
        shape = (a.shape[0] // NR, a.shape[1] // nz)
        for lead in ((2, nz), (2, nz), (nz,), (nz,), (nz - 1,), (nz - 1,)):
            scratch.append(pltpu.VMEM(lead + shape, a.dtype))
    scratch += [DMA((n, 2, nz))] * 3 + [DMA((n, nz))] * 4
    return pl.pallas_call(
        functools.partial(scatter_kernel, n, nz),
        out_shape=[
            jax.ShapeDtypeStruct((a.shape[0] // NR, a.shape[1] // nz), F32) for a in arrays
        ],
        in_specs=[pl.BlockSpec(memory_space=pl.ANY)] * n,
        out_specs=[pl.BlockSpec(memory_space=pltpu.VMEM)] * n,
        scratch_shapes=scratch,
        compiler_params=pltpu.CompilerParams(
            collective_id=collective_id, has_side_effects=True, vmem_limit_bytes=48 * 2**20
        ),
        cost_estimate=pl.CostEstimate(flops=0, bytes_accessed=60 * 2**20, transcendentals=0),
        name="reduce_scatter",
    )(*arrays)


def swap64(v):
    parts = []
    for i in range(0, v.shape[1], 128):
        parts += [v[:, i + 64 : i + 128], v[:, i : i + 64]]
    return jnp.concatenate(parts, axis=1)


def lane_in(shape, low, high):
    lane = lax.rem(lax.broadcasted_iota(jnp.int32, shape, 1), 128)
    return (lane >= low) & (lane < high)


def stack_heads(v, half):
    zero = jnp.zeros_like(v)
    return jnp.concatenate(
        [
            jnp.where(lane_in(v.shape, 0, half), v, zero),
            jnp.where(lane_in(v.shape, half, 2 * half), v, zero),
        ],
        axis=0,
    )


def live(first, i, j):
    shape = (BQ, 2 * BQ)
    key = lax.broadcasted_iota(jnp.int32, shape, 0) + j * BQ
    query = lax.rem(lax.broadcasted_iota(jnp.int32, shape, 1), BQ) + i * BQ
    return (key <= query) & (key >= first)


def attend_forward_kernel(low_ref, rot_ref, val_ref, first_ref, out_ref, log_ref, keys_ref):
    i = pl.program_id(0)

    @pl.when(i == 0)
    def _():
        keys_ref[...] = swap64(rot_ref[...])

    query = stack_heads(rot_ref[pl.ds(pl.multiple_of(i * BQ, BQ), BQ), :], 32)
    first = jnp.concatenate([first_ref[0], first_ref[0]], axis=1)

    def step(j, state):
        top, total, acc = state
        rows = pl.ds(pl.multiple_of(j * BQ, BQ), BQ)
        scores = dot(keys_ref[rows, :], query, ((1,), (1,))) * SCORE_SCALE
        scores = jnp.where(live(first, i, j), scores, NEG)
        new_top = jnp.maximum(top, jnp.max(scores, axis=0, keepdims=True))
        weights = jnp.exp(scores - new_top)
        fade = jnp.exp(top - new_top)
        total = total * fade + jnp.sum(weights, axis=0, keepdims=True)
        acc = acc * fade + dot(val_ref[rows, :], weights.astype(BF16), ((0,), (0,)))
        return new_top, total, acc

    state = (
        jnp.full((1, 2 * BQ), NEG, F32),
        jnp.zeros((1, 2 * BQ), F32),
        jnp.zeros((128, 2 * BQ), F32),
    )
    top, total, acc = lax.fori_loop(low_ref[i], i, step, step(i, state))
    acc = (acc / total).T
    out_ref[...] = jnp.where(lane_in((BQ, 128), 0, 64), acc[:BQ], acc[BQ:]).astype(BF16)
    log_ref[0] = top + jnp.log(total)


def attend_backward_kernel(
    low_ref,
    rot_ref,
    val_ref,
    first_ref,
    log_ref,
    out_ref,
    grad_ref,
    grot_ref,
    gval_ref,
    keys_ref,
    gkey_ref,
):
    i, n = pl.program_id(0), pl.num_programs(0)

    @pl.when(i == 0)
    def _():
        keys_ref[...] = swap64(rot_ref[...])
        gkey_ref[...] = jnp.zeros_like(gkey_ref)
        gval_ref[...] = jnp.zeros_like(gval_ref)

    here = pl.ds(pl.multiple_of(i * BQ, BQ), BQ)
    query = stack_heads(rot_ref[here, :], 32)
    grad = grad_ref[...]
    grads = stack_heads(grad, 64)
    first = jnp.concatenate([first_ref[0], first_ref[0]], axis=1)
    log_row = log_ref[0]
    product = (grad.astype(F32) * out_ref[...].astype(F32)).T
    center = jnp.concatenate(
        [
            jnp.sum(product[:64], axis=0, keepdims=True),
            jnp.sum(product[64:], axis=0, keepdims=True),
        ],
        axis=1,
    )

    def step(j, acc):
        rows = pl.ds(pl.multiple_of(j * BQ, BQ), BQ)
        key = keys_ref[rows, :]
        scores = dot(key, query, ((1,), (1,))) * SCORE_SCALE
        weights = jnp.where(live(first, i, j), jnp.exp(scores - log_row), 0.0)
        grad_weights = dot(val_ref[rows, :], grads, ((1,), (1,)))
        grad_scores = (weights * (grad_weights - center)).astype(BF16)
        gval_ref[rows, :] += dot(weights.astype(BF16), grads, ((1,), (0,)))
        gkey_ref[rows, :] += dot(grad_scores, query, ((1,), (0,)))
        return acc + dot(grad_scores, key, ((0,), (0,)))

    acc = lax.fori_loop(low_ref[i], i + 1, step, jnp.zeros((2 * BQ, 256), F32))
    grot_ref[here, :] = jnp.where(lane_in((BQ, 256), 0, 32), acc[:BQ], acc[BQ:]) * SCORE_SCALE

    @pl.when(i == n - 1)
    def _():
        def put(rows):
            moved = swap64(gkey_ref[rows, :] * SCORE_SCALE)
            grot_ref[rows, :] = jnp.where(lane_in((BQ, 256), 0, 64), grot_ref[rows, :], moved)

        in_rows(grot_ref.shape[0], BQ, put)


def attend_forward(low, rot, val, first):
    t = rot.shape[0]
    n = t // BQ
    whole = lambda i, low: (0, 0)
    row = lambda i, low: (i, 0, 0)
    return pl.pallas_call(
        attend_forward_kernel,
        grid_spec=pltpu.PrefetchScalarGridSpec(
            num_scalar_prefetch=1,
            grid=(n,),
            in_specs=[
                pl.BlockSpec((t, 256), whole),
                pl.BlockSpec((t, 128), whole),
                pl.BlockSpec((1, 1, BQ), row),
            ],
            out_specs=[
                pl.BlockSpec((BQ, 128), lambda i, low: (i, 0)),
                pl.BlockSpec((1, 1, 2 * BQ), row),
            ],
            scratch_shapes=[pltpu.VMEM((t, 256), BF16)],
        ),
        out_shape=[
            jax.ShapeDtypeStruct((t, 128), BF16),
            jax.ShapeDtypeStruct((n, 1, 2 * BQ), F32),
        ],
        compiler_params=pltpu.CompilerParams(vmem_limit_bytes=40 * 2**20),
        cost_estimate=pl.CostEstimate(
            flops=12 * 10**9, bytes_accessed=4 * 2**20, transcendentals=4 * 10**6
        ),
        name="attend_forward",
    )(low, rot, val, first)


def attend_backward(low, rot, val, first, log_all, out, grad):
    t = rot.shape[0]
    n = t // BQ
    whole = lambda i, low: (0, 0)
    row = lambda i, low: (i, 0, 0)
    some = lambda i, low: (i, 0)
    return pl.pallas_call(
        attend_backward_kernel,
        grid_spec=pltpu.PrefetchScalarGridSpec(
            num_scalar_prefetch=1,
            grid=(n,),
            in_specs=[
                pl.BlockSpec((t, 256), whole),
                pl.BlockSpec((t, 128), whole),
                pl.BlockSpec((1, 1, BQ), row),
                pl.BlockSpec((1, 1, 2 * BQ), row),
                pl.BlockSpec((BQ, 128), some),
                pl.BlockSpec((BQ, 128), some),
            ],
            out_specs=[pl.BlockSpec((t, 256), whole), pl.BlockSpec((t, 128), whole)],
            scratch_shapes=[pltpu.VMEM((t, 256), BF16), pltpu.VMEM((t, 256), F32)],
        ),
        out_shape=[jax.ShapeDtypeStruct((t, 256), F32), jax.ShapeDtypeStruct((t, 128), F32)],
        compiler_params=pltpu.CompilerParams(vmem_limit_bytes=40 * 2**20),
        cost_estimate=pl.CostEstimate(
            flops=20 * 10**9, bytes_accessed=8 * 2**20, transcendentals=4 * 10**6
        ),
        name="attend_backward",
    )(low, rot, val, first, log_all, out, grad)


def pack_tokens(values):
    rows = values.reshape(-1, 128)
    return jnp.pad(rows, ((0, 8 - rows.shape[0]), (0, 0)))


def pack_all_tokens(values, nz):
    rows = values.reshape(NR, -1, 128)
    rows = jnp.pad(rows, ((0, 0), (0, 8 - rows.shape[1]), (0, 0)))
    return jnp.tile(rows.reshape(NR * 8, 128), (1, nz))


def group_share(operand, axis, parts):
    shape = operand.shape
    groups = lax.axis_size("group")
    width = shape[axis] // parts // groups
    split = operand.reshape(shape[:axis] + (parts, groups, width) + shape[axis + 1 :])
    return lax.dynamic_index_in_dim(split, lax.axis_index("group"), axis + 1, keepdims=False)


def sum_over_group(operand):
    if lax.axis_size("group") == 2:
        other = lax.ppermute(operand, "group", [(0, 1), (1, 0)])
        return operand.astype(F32) + other.astype(F32)
    return lax.psum(operand, "group").astype(F32)


def on_device(
    hidden_in,
    segments,
    attn_gain,
    query_weight,
    key_matrix,
    value_matrix,
    out_weight,
    ffn_gain,
    gate_weight,
    up_weight,
    down_weight,
    cotangent,
):
    row, col = lax.axis_index("row"), lax.axis_index("col")
    nz, groups = lax.axis_size("col"), lax.axis_size("group")
    rows_dev, cols_dev = hidden_in.shape
    tokens = rows_dev * NR
    width = cols_dev * nz
    ffn = gate_weight.shape[1] // nz
    part = ffn // groups

    seg = segments.reshape(-1)
    places = jnp.arange(tokens, dtype=jnp.int32)
    first = jnp.sum((seg[None, :] < seg[:, None]).astype(jnp.int32), axis=1)
    low = first[::BQ] // BQ
    first_rows = first.reshape(-1, 1, BQ)
    offset = (places - first).astype(F32)
    half_width = HEAD_SIZE // 2
    inverse = ROPE_BASE ** (-(2.0 * jnp.arange(half_width, dtype=F32)) / HEAD_SIZE)
    angles = offset[:, None] * inverse[None, :]
    cosine = jnp.tile(jnp.cos(angles), (1, 4))
    sine = jnp.tile(jnp.sin(angles), (1, 4))

    q = query_weight.reshape(cols_dev, nz, 2, 2, half_width)
    kv_of = lambda m: jnp.repeat(m.reshape(cols_dev, 2, HEAD_SIZE), nz // 2, axis=1)
    k = kv_of(key_matrix).reshape(cols_dev, nz, 2, half_width)
    v = kv_of(value_matrix)
    qkv_send = jnp.concatenate(
        [q[:, :, 0, 0], q[:, :, 1, 0], k[:, :, 0], q[:, :, 0, 1], q[:, :, 1, 1], k[:, :, 1], v],
        axis=2,
    ).reshape(cols_dev, nz * 256)
    qkv = lax.all_to_all(qkv_send, "col", 1, 0, tiled=True)
    joint = jnp.concatenate(
        [
            qkv[:, :96],
            qkv[:, 64:96],
            qkv[:, 96:192],
            qkv[:, 160:192],
            qkv[:, 192:],
            qkv[:, 192:],
        ],
        axis=1,
    )
    out_rows = lax.all_to_all(out_weight, "col", 0, 1, tiled=True)
    gate_up_send = jnp.concatenate(
        [group_share(gate_weight, 1, nz), group_share(up_weight, 1, nz)], axis=2
    ).reshape(cols_dev, nz * 2 * part)
    gate_up_part = lax.all_to_all(gate_up_send, "col", 1, 0, tiled=True)
    gate_up = lax.all_gather(gate_up_part, "group", axis=1, tiled=True)
    down_send = group_share(down_weight, 0, nz).reshape(nz * part, cols_dev)
    down_part = lax.all_to_all(down_send, "col", 0, 1, tiled=True)
    down = lax.all_gather(down_part, "group", axis=0, tiled=True)

    def gates(a):
        return a.reshape(-1, groups, 2, part)[:, :, 0].reshape(-1, ffn)

    def ups(a):
        return a.reshape(-1, groups, 2, part)[:, :, 1].reshape(-1, ffn)

    residual = hidden_in.astype(F32)
    grad_top = cotangent.astype(F32)
    grad_ffn = (RES_SCALE * grad_top).astype(BF16)
    x_all, gain_all, grad_ffn_all = gather(
        [hidden_in, jnp.broadcast_to(attn_gain[None, :], (8, cols_dev)), grad_ffn], 0
    )
    wide = x_all.astype(F32)
    scale_one = lax.rsqrt(jnp.mean(wide * wide, axis=1) + NORM_EPS)
    normed_one = (wide * scale_one[:, None] * gain_all[:1]).astype(BF16)

    pre = dot(normed_one, joint, ((1,), (0,)))
    pre_one, pre_two = pre[:, :128], pre[:, 128:256]
    rot = jnp.concatenate(
        [pre_one * cosine - pre_two * sine, pre_two * cosine + pre_one * sine], axis=1
    ).astype(BF16)
    val = pre[:, 256:].astype(BF16)
    heads_out, log_all = attend_forward(low, rot, val, first_rows)
    attn_part = dot(heads_out, out_rows, ((1,), (0,))).astype(BF16)
    (attn_sum,) = reduce_scatter([attn_part], 1)
    resid_mid = residual + RES_SCALE * attn_sum

    squares = jnp.sum(resid_mid * resid_mid, axis=1)
    raw_two, square_all = gather(
        [(resid_mid * ffn_gain[None, :]).astype(BF16), pack_tokens(squares)], 2
    )
    square_sum = jnp.sum(square_all.reshape(NR, 8, nz, 128), axis=2)[:, : rows_dev // 128]
    scale_two = lax.rsqrt(square_sum.reshape(tokens) / width + NORM_EPS)

    both = dot(raw_two, gate_up, ((1,), (0,))) * scale_two[:, None]
    gate_pre, up_pre = gates(both), ups(both)
    gate_sig = jax.nn.sigmoid(gate_pre)
    gate_act = gate_pre * gate_sig
    hidden_act = (gate_act * up_pre).astype(BF16)
    down_part_sum = dot(hidden_act, down, ((1,), (0,))).astype(BF16)
    grad_hidden = dot(grad_ffn_all, down, ((1,), (1,)))
    grad_gate = grad_hidden * up_pre * gate_sig * (1.0 + gate_pre * (1.0 - gate_sig))
    grad_up = grad_hidden * gate_act
    inner_two = jnp.sum(grad_gate * gate_pre + grad_up * up_pre, axis=1)

    def pair(a, b):
        return jnp.stack([a.reshape(tokens, groups, part), b.reshape(tokens, groups, part)], axis=2).reshape(
            tokens, 2 * ffn
        )

    grad_pair = pair(grad_gate.astype(BF16), grad_up.astype(BF16))
    grad_pair_scaled = pair(
        (grad_gate * scale_two[:, None]).astype(BF16), (grad_up * scale_two[:, None]).astype(BF16)
    )
    grad_two_part = dot(grad_pair, gate_up, ((1,), (1,))).astype(BF16)
    down_sum, grad_two, inner_two_sum = reduce_scatter(
        [down_part_sum, grad_two_part, pack_all_tokens(inner_two, nz)], 3
    )
    layer_out = (resid_mid + RES_SCALE * down_sum).astype(BF16)
    scale_two_own = lax.dynamic_slice_in_dim(scale_two, row * rows_dev, rows_dev)[:, None]
    inner_two_own = inner_two_sum[: rows_dev // 128].reshape(rows_dev, 1)
    grad_mid = (
        grad_top
        + scale_two_own * ffn_gain[None, :] * grad_two
        - resid_mid * (scale_two_own * scale_two_own * inner_two_own / width)
    )
    ffn_gain_part = jnp.sum(grad_two * resid_mid * scale_two_own, axis=0)
    grad_attn = (RES_SCALE * grad_mid).astype(BF16)
    (grad_attn_all,) = gather([grad_attn], 4)

    down_grad_part = dot(hidden_act, grad_ffn_all, ((0,), (0,))).astype(BF16)
    down_grad_part = lax.psum_scatter(down_grad_part, "group", scatter_dimension=0, tiled=True)
    down_grad_part = lax.all_to_all(
        down_grad_part.reshape(part, nz, cols_dev), "col", 1, 0, tiled=True
    ).reshape(nz, part, cols_dev)
    down_grad = (
        lax.all_gather(down_grad_part, "group", axis=1, tiled=True)
        .reshape(nz * ffn, cols_dev)
        .astype(F32)
    )
    pair_grad_part = dot(raw_two, grad_pair_scaled, ((0,), (0,))).astype(BF16)
    pair_grad_part = lax.psum_scatter(pair_grad_part, "group", scatter_dimension=1, tiled=True)
    pair_grad_part = lax.all_to_all(pair_grad_part, "col", 0, 1, tiled=True).reshape(
        cols_dev, nz, 2 * part
    )
    pair_grad = lax.all_gather(pair_grad_part, "group", axis=2, tiled=True).reshape(
        cols_dev, nz, groups, 2, part
    )
    gate_grad = pair_grad[:, :, :, 0].reshape(cols_dev, nz * ffn).astype(F32)
    up_grad = pair_grad[:, :, :, 1].reshape(cols_dev, nz * ffn).astype(F32)

    grad_heads = dot(grad_attn_all, out_rows, ((1,), (1,))).astype(BF16)
    out_grad_part = dot(heads_out, grad_attn_all, ((0,), (0,))).astype(BF16)
    out_grad = sum_over_group(
        lax.all_to_all(out_grad_part, "col", 1, 0, tiled=True)
    )
    grad_rot, grad_val = attend_backward(
        low, rot, val, first_rows, log_all, heads_out, grad_heads
    )
    inner_one = jnp.sum(grad_rot * rot.astype(F32), axis=1) + jnp.sum(
        grad_val * val.astype(F32), axis=1
    )
    grot_one, grot_two = grad_rot[:, :128], grad_rot[:, 128:]
    grad_pre = jnp.concatenate(
        [grot_one * cosine + grot_two * sine, grot_two * cosine - grot_one * sine, grad_val], axis=1
    ).astype(BF16)
    grad_one_part = dot(grad_pre, joint, ((1,), (1,))).astype(BF16)
    grad_one, inner_one_sum = reduce_scatter([grad_one_part, pack_all_tokens(inner_one, nz)], 5)
    scale_one_own = lax.dynamic_slice_in_dim(scale_one, row * rows_dev, rows_dev)[:, None]
    inner_one_own = inner_one_sum[: rows_dev // 128].reshape(rows_dev, 1)
    input_grad = (
        grad_mid
        + scale_one_own * attn_gain[None, :] * grad_one
        - residual * (scale_one_own * scale_one_own * inner_one_own / width)
    )
    attn_gain_part = jnp.sum(grad_one * residual * scale_one_own, axis=0)
    attn_gain_grad, ffn_gain_grad = lax.psum((attn_gain_part, ffn_gain_part), ("group", "row"))

    joint_grad = dot(normed_one, grad_pre, ((0,), (0,)))
    qkv_grad = jnp.concatenate(
        [
            joint_grad[:, :64],
            joint_grad[:, 64:96] + joint_grad[:, 96:128],
            joint_grad[:, 128:192],
            joint_grad[:, 192:224] + joint_grad[:, 224:256],
            joint_grad[:, 256:320] + joint_grad[:, 320:],
        ],
        axis=1,
    ).astype(BF16)
    qkv_grad = sum_over_group(
        lax.all_to_all(qkv_grad, "col", 0, 1, tiled=True).reshape(cols_dev, nz * 256)
    ).reshape(cols_dev, nz, 256)
    query_grad = jnp.stack(
        [
            jnp.concatenate([qkv_grad[:, :, :32], qkv_grad[:, :, 96:128]], axis=2),
            jnp.concatenate([qkv_grad[:, :, 32:64], qkv_grad[:, :, 128:160]], axis=2),
        ],
        axis=2,
    ).reshape(cols_dev, nz * 128)

    def kv_grad(a):
        return jnp.sum(a.reshape(cols_dev, 2, nz // 2, HEAD_SIZE), axis=2).reshape(cols_dev, 2 * HEAD_SIZE)

    key_grad = kv_grad(jnp.concatenate([qkv_grad[:, :, 64:96], qkv_grad[:, :, 160:192]], axis=2))
    value_grad = kv_grad(qkv_grad[:, :, 192:])
    return (
        layer_out,
        input_grad,
        attn_gain_grad,
        query_grad,
        key_grad,
        value_grad,
        out_grad,
        ffn_gain_grad,
        gate_grad,
        up_grad,
        down_grad,
    )


def solution(mesh):
    return jax.shard_map(
        on_device,
        mesh=mesh,
        in_specs=(
            P(("group", "row"), "col"),
            P("group", None),
            P("col"),
            P("col", "row"),
            P("col", "row"),
            P("col", "row"),
            P("row", "col"),
            P("col"),
            P("col", "row"),
            P("col", "row"),
            P("row", "col"),
            P(("group", "row"), "col"),
        ),
        out_specs=(
            P(("group", "row"), "col"),
            P(("group", "row"), "col"),
            P("col"),
            P("col", "row"),
            P("col", "row"),
            P("col", "row"),
            P("row", "col"),
            P("col"),
            P("col", "row"),
            P("col", "row"),
            P("row", "col"),
        ),
        check_vma=False,
    )
```

```python
import functools

import jax
import jax.numpy as jnp
from jax import lax
from jax.experimental import pallas as pl
from jax.experimental.pallas import tpu as pltpu
from jax.sharding import PartitionSpec as P

F32, BF16 = jnp.float32, jnp.bfloat16
MESH = pl.DeviceIdType.MESH
DMA = pltpu.SemaphoreType.DMA

MODEL_WIDTH = 2048
HEAD_SIZE = 64
NORM_EPS = 1e-05
ROPE_BASE = 10000000.0
RES_SCALE = 0.22
SCORE_SCALE = 0.015625

NR = 4
BQ = 256
NEG = -1e30


def dot(a, b, dims):
    return lax.dot_general(a, b, (dims, ((), ())), preferred_element_type=F32)


def place():
    group, row, col = lax.axis_index("group"), lax.axis_index("row"), lax.axis_index("col")
    other_core = row + 1 - 2 * lax.rem(row, 2)
    other_x = lax.rem(row + 2, NR)
    both = other_x + 1 - 2 * lax.rem(row, 2)
    return group, row, col, other_core, other_x, both


def greet(devices):
    barrier = pltpu.get_barrier_semaphore()
    for device in devices:
        pl.semaphore_signal(barrier, inc=1, device_id=device, device_id_type=MESH)
    return barrier


def block_at(ref, row, col, shape):
    b0, b1 = shape
    return ref.at[pl.ds(pl.multiple_of(row * b0, b0), b0), pl.ds(pl.multiple_of(col * b1, b1), b1)]


class Spread:
    def __init__(self, arrays, pieces, outs, mode):
        self.arrays, self.pieces, self.mode = list(arrays), pieces, mode
        self.base = [jax.ShapeDtypeStruct(o, arrays[0].dtype) for o in outs]
        self.outs = self.base + (self.base if mode == "twin" else [])
        n, nz = len(pieces), lax.axis_size("col")
        self.scratch = [DMA((n, 2))] + [DMA((n, nz))] * (2 if mode == "plain" else 4)

    def bind(self, ins, outs, sems):
        self.i, self.o, self.sems = ins, outs, sems
        self.g, self.r, self.z = place()[:3]

    def src(self, n, col, half):
        which, src, _, _ = self.pieces[n]
        return self.i[which].at[src(col, half)]

    def dst(self, n, col, half, twin=False):
        _, _, which, dst = self.pieces[n]
        return self.o[which + (len(self.base) if twin else 0)].at[dst(col, half)]

    def half(self):
        return self.g if self.mode in ("share", "sum") else 0

    def send(self, n, col):
        return pltpu.make_async_remote_copy(
            src_ref=self.src(n, col, self.half()),
            dst_ref=self.dst(n, self.z, self.half()),
            send_sem=self.sems[1].at[n, col],
            recv_sem=self.sems[2].at[n, self.z],
            device_id=(self.g, self.r, col),
            device_id_type=MESH,
        )

    def arrived(self, n, col):
        return pltpu.make_async_remote_copy(
            src_ref=self.src(n, col, self.half()),
            dst_ref=self.dst(n, col, self.half()),
            send_sem=self.sems[1].at[n, col],
            recv_sem=self.sems[2].at[n, col],
            device_id=(self.g, self.r, col),
            device_id_type=MESH,
        )

    def cross(self, n, col, own=False):
        src = self.src(n, self.z, self.half()) if own else self.dst(n, col, self.half())
        return pltpu.make_async_remote_copy(
            src_ref=src,
            dst_ref=self.dst(n, col, self.half(), self.mode == "twin"),
            send_sem=self.sems[3].at[n, col],
            recv_sem=self.sems[4].at[n, col],
            device_id=(1 - self.g, self.r, self.z),
            device_id_type=MESH,
        )

    def crossed(self, n, col):
        half = 1 - self.g if self.mode in ("share", "sum") else 0
        place_there = self.dst(n, col, half, self.mode == "twin")
        return pltpu.make_async_remote_copy(
            src_ref=place_there,
            dst_ref=place_there,
            send_sem=self.sems[3].at[n, col],
            recv_sem=self.sems[4].at[n, col],
            device_id=(1 - self.g, self.r, self.z),
            device_id_type=MESH,
        )

    def local(self, n):
        halves = (0, 1) if self.mode == "share" else (self.half(),)
        return [
            pltpu.make_async_copy(
                self.src(n, self.z, h), self.dst(n, self.z, h), self.sems[0].at[n, m]
            )
            for m, h in enumerate(halves)
        ]

    def start(self, nz):
        for k in range(1, nz):
            for n in range(len(self.pieces)):
                self.send(n, lax.rem(self.z + k, nz)).start()
        for n in range(len(self.pieces)):
            for copy in self.local(n):
                copy.start()
            if self.mode in ("sum", "twin"):
                self.cross(n, self.z, own=True).start()

    def step(self, k, nz):
        for n in range(len(self.pieces)):
            for near, col in ((self.z - k >= 0, self.z - k), (self.z + k < nz, self.z + k)):

                @pl.when(near)
                def _():
                    self.arrived(n, col).wait_recv()
                    if self.mode != "plain":
                        self.cross(n, col).start()

    def finish(self, nz):
        for n in range(len(self.pieces)):
            for copy in self.local(n):
                copy.wait()
            for k in range(1, nz):
                col = lax.rem(self.z + k, nz)
                self.send(n, col).wait_send()
                if self.mode != "plain":
                    self.crossed(n, col).wait_recv()
                    self.crossed(n, col).wait_send()
            if self.mode in ("sum", "twin"):
                self.crossed(n, self.z).wait_recv()
                self.cross(n, self.z, own=True).wait_send()


class Swap:
    def __init__(self, array, pieces, out):
        self.arrays, self.pieces = [array], pieces
        self.outs = [jax.ShapeDtypeStruct(out, array.dtype)]
        self.scratch = [DMA((len(pieces),))] * 2

    def bind(self, ins, outs, sems):
        self.i, self.o, self.sems = ins[0], outs[0], sems
        self.g, self.r, self.z = place()[:3]

    def copy(self, n):
        src, dst = self.pieces[n]
        return pltpu.make_async_remote_copy(
            src_ref=self.i.at[src(1 - self.g)],
            dst_ref=self.o.at[dst],
            send_sem=self.sems[0].at[n],
            recv_sem=self.sems[1].at[n],
            device_id=(1 - self.g, self.r, self.z),
            device_id_type=MESH,
        )

    def start(self, nz):
        for n in range(len(self.pieces)):
            self.copy(n).start()

    def step(self, k, nz):
        pass

    def finish(self, nz):
        for n in range(len(self.pieces)):
            self.copy(n).wait()


def bind_extras(extras, ins, outs, sems):
    for extra in extras:
        n, m, k = len(extra.arrays), len(extra.outs), len(extra.scratch)
        extra.bind(ins[:n], outs[:m], sems[:k])
        ins, outs, sems = ins[n:], outs[m:], sems[k:]


def greetings(extras, nz, devices):
    g, r, z = place()[:3]
    if any(isinstance(extra, Spread) for extra in extras):
        devices = devices[:2] + [(g, r, lax.rem(z + k, nz)) for k in range(1, nz)]
    if any(isinstance(extra, Swap) or extra.mode != "plain" for extra in extras):
        devices = devices + [(1 - g, r, z)]
    return devices


def gather_kernel(n, nz, units, extras, *refs):
    n_in, n_out = n + sum(len(e.arrays) for e in extras), n + sum(len(e.outs) for e in extras)
    ins, outs, sems = refs[:n], refs[n_in : n_in + n], refs[n_in + n_out :]
    local_sem, send_sem, recv_sem = sems[:3]
    bind_extras(extras, refs[n:n_in], refs[n_in + n : n_in + n_out], sems[3:])
    g, r, z, rc, rx, rxc = place()
    has_left, has_right = z > 0, z < nz - 1
    if any(isinstance(extra, Spread) for extra in extras):
        devices = greetings(extras, nz, [(g, rc, z), (g, rx, z)])
        barrier = greet(devices)
        pl.semaphore_wait(barrier, len(devices))
    else:
        devices = greetings(extras, nz, [(g, rc, z), (g, rx, z)])
        barrier = greet(devices)

        @pl.when(has_left)
        def _():
            pl.semaphore_signal(barrier, inc=1, device_id=(g, r, z - 1), device_id_type=MESH)

        @pl.when(has_right)
        def _():
            pl.semaphore_signal(barrier, inc=1, device_id=(g, r, z + 1), device_id_type=MESH)

        count = has_left.astype(jnp.int32) + has_right.astype(jnp.int32)
        pl.semaphore_wait(barrier, len(devices) + count)

    right, left, over_x, to_core = 0, nz - 1, 2 * (nz - 1), 3 * nz - 2

    def own_part(u):
        i, start, size = units[u]
        return ins[i].at[pl.ds(start, size), :]

    def slot(u, row, col):
        i, start, size = units[u]
        b0, b1 = ins[i].shape
        return outs[i].at[
            pl.ds(pl.multiple_of(row * b0 + start, size), size),
            pl.ds(pl.multiple_of(col * b1, b1), b1),
        ]

    def copy(u, src, row, col, where, device):
        return pltpu.make_async_remote_copy(
            src_ref=src,
            dst_ref=slot(u, row, col),
            send_sem=send_sem.at[u, where],
            recv_sem=recv_sem.at[u, row, col],
            device_id=device,
            device_id_type=MESH,
        )

    def own(u, where, device):
        return copy(u, own_part(u), r, z, where, device)

    def forward(u, row, col, where, device):
        return copy(u, slot(u, row, col), row, col, where, device)

    def rank(col):
        return col - (col > z).astype(jnp.int32)

    def local(u):
        return pltpu.make_async_copy(own_part(u), slot(u, r, z), local_sem.at[u])

    every = range(len(units))
    for u in every:

        @pl.when(has_right)
        def _():
            own(u, right, (g, r, z + 1)).start()

        @pl.when(has_left)
        def _():
            own(u, left, (g, r, z - 1)).start()

        own(u, over_x, (g, rx, z)).start()
    for u in every:
        own(u, to_core, (g, rc, z)).start()
        local(u).start()
    for extra in extras:
        extra.start(nz)

    def from_x(u, k):
        for near, col, where in (
            (z - k >= 0, z - k, to_core + 1 if k == 0 else to_core + nz + 1 + z - k),
            (z + k < nz, z + k, to_core + nz + z + k),
        )[: 1 if k == 0 else 2]:

            @pl.when(near)
            def _():
                forward(u, rx, col, where, (g, rx, z)).wait_recv()
                forward(u, rx, col, where, (g, rc, z)).start()

    def from_z(u, k):
        for near, more, col, device, flow in (
            (z - k >= 0, has_right, z - k, (g, r, z + 1), right),
            (z + k < nz, has_left, z + k, (g, r, z - 1), left),
        ):

            @pl.when(near)
            def _():
                forward(u, r, col, flow, (g, rc, z)).wait_recv()
                if k < nz - 1:

                    @pl.when(more)
                    def _():
                        forward(u, r, col, flow + k, device).start()

                forward(u, r, col, over_x + 1 + rank(col), (g, rx, z)).start()
                forward(u, r, col, to_core + 2 + rank(col), (g, rc, z)).start()

    for k in range(1, nz):
        for u in every:
            from_z(u, k)
            from_x(u, k - 1)
        if k > 1:
            for extra in extras:
                extra.step(k - 1, nz)
    for u in every:
        from_x(u, nz - 1)
    for extra in extras:
        extra.step(nz - 1, nz)

    for u in every:
        for col in range(nz):
            forward(u, rc, col, to_core, (g, rc, z)).wait_recv()
            forward(u, rxc, col, to_core, (g, rc, z)).wait_recv()
        local(u).wait()
        for where in range(to_core + 2 * nz):

            def sent(where=where):
                own(u, where, (g, rc, z)).wait_send()

            if where < left:
                pl.when(has_right & (z - where >= 0))(sent)
            elif where < over_x:
                pl.when(has_left & (z + (where - left) < nz))(sent)
            else:
                sent()
    for extra in extras:
        extra.finish(nz)


def flat(lists):
    return [item for some in lists for item in some]


def gather(arrays, collective_id, extras=()):
    n, nz = len(arrays), lax.axis_size("col")
    units = []
    for i, a in enumerate(arrays):
        parts = 2 if a.shape[0] % 256 == 0 else 1
        units += [(i, m * (a.shape[0] // parts), a.shape[0] // parts) for m in range(parts)]
    anywhere = pl.BlockSpec(memory_space=pl.ANY)
    extra_in, extra_out = flat(e.arrays for e in extras), flat(e.outs for e in extras)
    outs = pl.pallas_call(
        functools.partial(gather_kernel, n, nz, units, extras),
        out_shape=[
            jax.ShapeDtypeStruct((a.shape[0] * NR, a.shape[1] * nz), a.dtype) for a in arrays
        ]
        + extra_out,
        in_specs=[anywhere] * (n + len(extra_in)),
        out_specs=[anywhere] * (n + len(extra_out)),
        scratch_shapes=[DMA((len(units),)), DMA((len(units), 5 * nz - 2)), DMA((len(units), NR, nz))]
        + flat(e.scratch for e in extras),
        compiler_params=pltpu.CompilerParams(collective_id=collective_id, has_side_effects=True),
        cost_estimate=pl.CostEstimate(flops=0, bytes_accessed=60 * 2**20, transcendentals=0),
        name="gather",
    )(*arrays, *extra_in)
    return outs[:n], outs[n:]


def in_rows(total, step, body):
    step = min(step, total)
    if total == step:
        body(pl.ds(0, step))
    else:

        def one(i, carry):
            body(pl.ds(pl.multiple_of(i * step, step), step))
            return carry

        lax.fori_loop(0, total // step, one, 0)


def scatter_kernel(n, nz, extras, *refs):
    n_in, n_out = n + sum(len(e.arrays) for e in extras), n + sum(len(e.outs) for e in extras)
    ins, outs, rest = refs[:n], refs[n_in : n_in + n], refs[n_in + n_out :]
    bufs = [rest[6 * i : 6 * (i + 1)] for i in range(n)]
    load_sem, core_send, core_recv, x_send, x_recv, z_send, z_recv = rest[6 * n : 6 * n + 7]
    bind_extras(extras, refs[n:n_in], refs[n_in + n : n_in + n_out], rest[6 * n + 7 :])
    g, r, z, rc, rx, rxc = place()
    pair = z + 1 - 2 * lax.rem(z, 2)
    far, far_pair = lax.rem(z + 2, nz), lax.rem(pair + 2, nz)
    devices = greetings(extras, nz, [(g, rc, z), (g, rx, z), (g, r, pair), (g, r, far)])
    barrier = greet(devices)
    pl.semaphore_wait(barrier, len(devices))
    order = (far_pair, pair, far, z)
    steps = range(len(order))

    def block(i, row, step):
        b0, b1 = ins[i].shape[0] // NR, ins[i].shape[1] // nz
        return block_at(ins[i], row, order[step], (b0, b1))

    def load(i, way, step):
        return pltpu.make_async_copy(
            block(i, (rx, r)[way], step), bufs[i][0].at[way, step], load_sem.at[i, way, step]
        )

    def remote(src, dst, send, recv, device):
        return pltpu.make_async_remote_copy(
            src_ref=src,
            dst_ref=dst,
            send_sem=send,
            recv_sem=recv,
            device_id=device,
            device_id_type=MESH,
        )

    def core(i, way, step):
        return remote(
            block(i, (rxc, rc)[way], step),
            bufs[i][1].at[way, step],
            core_send.at[i, way, step],
            core_recv.at[i, way, step],
            (g, rc, z),
        )

    def over_x(i, step):
        return remote(
            bufs[i][2].at[step], bufs[i][3].at[step], x_send.at[i, step], x_recv.at[i, step], (g, rx, z)
        )

    def along_z(i, step):
        return remote(
            bufs[i][4].at[step],
            bufs[i][5].at[step],
            z_send.at[i, step],
            z_recv.at[i, step],
            (g, r, far if step == 2 else pair),
        )

    for i in range(n):
        for way in range(2):
            for step in steps:
                core(i, way, step).start()
                load(i, way, step).start()
    for i in range(n):
        own, from_core, half, from_x, mine, from_z = bufs[i]
        for step in steps:
            load(i, 0, step).wait()
            core(i, 0, step).wait_recv()

            def add(rows):
                half[step, rows, :] = (
                    own[0, step, rows, :].astype(F32) + from_core[0, step, rows, :].astype(F32)
                ).astype(half.dtype)

            in_rows(own.shape[2], 64, add)
            over_x(i, step).start()
        if i == 0:
            for extra in extras:
                extra.start(nz)
    for i in range(n):
        own, from_core, half, from_x, mine, from_z = bufs[i]

        def total(step, rows):
            result = (
                own[1, step, rows, :].astype(F32)
                + from_core[1, step, rows, :].astype(F32)
                + from_x[step, rows, :].astype(F32)
            )
            if step == 2:
                result = result + from_z[0, rows, :].astype(F32)
            if step == 3:
                result = result + from_z[1, rows, :].astype(F32) + from_z[2, rows, :].astype(F32)
            return result

        for step in steps:
            load(i, 1, step).wait()
            core(i, 1, step).wait_recv()
            over_x(i, step).wait_recv()
            if step == 2:
                along_z(i, 0).wait_recv()
            if step == 3:
                along_z(i, 1).wait_recv()
                along_z(i, 2).wait_recv()

            def add(rows):
                if step == 3:
                    outs[i][rows, :] = total(step, rows)
                else:
                    mine[step, rows, :] = total(step, rows).astype(mine.dtype)

            in_rows(own.shape[2], 64, add)
            if step < 3:
                along_z(i, step).start()
            if i == 0 and 1 <= step:
                for extra in extras:
                    extra.step(step, nz)
    for i in range(n):
        for step in steps:
            core(i, 0, step).wait_send()
            core(i, 1, step).wait_send()
            over_x(i, step).wait_send()
            if step < 3:
                along_z(i, step).wait_send()
    for extra in extras:
        extra.finish(nz)


def reduce_scatter(arrays, collective_id, extras=()):
    n, nz = len(arrays), lax.axis_size("col")
    scratch = []
    for a in arrays:
        shape = (a.shape[0] // NR, a.shape[1] // nz)
        for lead in ((2, nz), (2, nz), (nz,), (nz,), (nz - 1,), (nz - 1,)):
            scratch.append(pltpu.VMEM(lead + shape, a.dtype))
    scratch += [DMA((n, 2, nz))] * 3 + [DMA((n, nz))] * 4
    anywhere = pl.BlockSpec(memory_space=pl.ANY)
    extra_in, extra_out = flat(e.arrays for e in extras), flat(e.outs for e in extras)
    outs = pl.pallas_call(
        functools.partial(scatter_kernel, n, nz, extras),
        out_shape=[
            jax.ShapeDtypeStruct((a.shape[0] // NR, a.shape[1] // nz), F32) for a in arrays
        ]
        + extra_out,
        in_specs=[anywhere] * (n + len(extra_in)),
        out_specs=[pl.BlockSpec(memory_space=pltpu.VMEM)] * n + [anywhere] * len(extra_out),
        scratch_shapes=scratch + flat(e.scratch for e in extras),
        compiler_params=pltpu.CompilerParams(
            collective_id=collective_id, has_side_effects=True, vmem_limit_bytes=48 * 2**20
        ),
        cost_estimate=pl.CostEstimate(flops=0, bytes_accessed=60 * 2**20, transcendentals=0),
        name="reduce_scatter",
    )(*arrays, *extra_in)
    return outs[:n], outs[n:]


def swap64(v):
    parts = []
    for i in range(0, v.shape[1], 128):
        parts += [v[:, i + 64 : i + 128], v[:, i : i + 64]]
    return jnp.concatenate(parts, axis=1)


def lane_in(shape, low, high):
    lane = lax.rem(lax.broadcasted_iota(jnp.int32, shape, 1), 128)
    return (lane >= low) & (lane < high)


def stack_heads(v, half):
    zero = jnp.zeros_like(v)
    return jnp.concatenate(
        [
            jnp.where(lane_in(v.shape, 0, half), v, zero),
            jnp.where(lane_in(v.shape, half, 2 * half), v, zero),
        ],
        axis=0,
    )


def live(first, i, j):
    shape = (BQ, 2 * BQ)
    key = lax.broadcasted_iota(jnp.int32, shape, 0) + j * BQ
    query = lax.rem(lax.broadcasted_iota(jnp.int32, shape, 1), BQ) + i * BQ
    return (key <= query) & (key >= first)


def attend_forward_kernel(low_ref, rot_ref, val_ref, first_ref, out_ref, log_ref, keys_ref):
    i = pl.program_id(0)

    @pl.when(i == 0)
    def _():
        keys_ref[...] = swap64(rot_ref[...])

    query = stack_heads(rot_ref[pl.ds(pl.multiple_of(i * BQ, BQ), BQ), :], 32)
    first = jnp.concatenate([first_ref[0], first_ref[0]], axis=1)

    def step(j, state):
        top, total, acc = state
        rows = pl.ds(pl.multiple_of(j * BQ, BQ), BQ)
        scores = dot(keys_ref[rows, :], query, ((1,), (1,))) * SCORE_SCALE
        scores = jnp.where(live(first, i, j), scores, NEG)
        new_top = jnp.maximum(top, jnp.max(scores, axis=0, keepdims=True))
        weights = jnp.exp(scores - new_top)
        fade = jnp.exp(top - new_top)
        total = total * fade + jnp.sum(weights, axis=0, keepdims=True)
        acc = acc * fade + dot(val_ref[rows, :], weights.astype(BF16), ((0,), (0,)))
        return new_top, total, acc

    state = (
        jnp.full((1, 2 * BQ), NEG, F32),
        jnp.zeros((1, 2 * BQ), F32),
        jnp.zeros((128, 2 * BQ), F32),
    )
    top, total, acc = lax.fori_loop(low_ref[i], i, step, step(i, state))
    acc = (acc / total).T
    out_ref[...] = jnp.where(lane_in((BQ, 128), 0, 64), acc[:BQ], acc[BQ:]).astype(BF16)
    log_ref[0] = top + jnp.log(total)


def attend_backward_kernel(
    low_ref,
    rot_ref,
    val_ref,
    first_ref,
    log_ref,
    out_ref,
    grad_ref,
    grot_ref,
    gval_ref,
    keys_ref,
    gkey_ref,
):
    i, n = pl.program_id(0), pl.num_programs(0)

    @pl.when(i == 0)
    def _():
        keys_ref[...] = swap64(rot_ref[...])
        gkey_ref[...] = jnp.zeros_like(gkey_ref)
        gval_ref[...] = jnp.zeros_like(gval_ref)

    here = pl.ds(pl.multiple_of(i * BQ, BQ), BQ)
    query = stack_heads(rot_ref[here, :], 32)
    grad = grad_ref[...]
    grads = stack_heads(grad, 64)
    first = jnp.concatenate([first_ref[0], first_ref[0]], axis=1)
    log_row = log_ref[0]
    product = (grad.astype(F32) * out_ref[...].astype(F32)).T
    center = jnp.concatenate(
        [
            jnp.sum(product[:64], axis=0, keepdims=True),
            jnp.sum(product[64:], axis=0, keepdims=True),
        ],
        axis=1,
    )

    def step(j, acc):
        rows = pl.ds(pl.multiple_of(j * BQ, BQ), BQ)
        key = keys_ref[rows, :]
        scores = dot(key, query, ((1,), (1,))) * SCORE_SCALE
        weights = jnp.where(live(first, i, j), jnp.exp(scores - log_row), 0.0)
        grad_weights = dot(val_ref[rows, :], grads, ((1,), (1,)))
        grad_scores = (weights * (grad_weights - center)).astype(BF16)
        gval_ref[rows, :] += dot(weights.astype(BF16), grads, ((1,), (0,)))
        gkey_ref[rows, :] += dot(grad_scores, query, ((1,), (0,)))
        return acc + dot(grad_scores, key, ((0,), (0,)))

    acc = lax.fori_loop(low_ref[i], i + 1, step, jnp.zeros((2 * BQ, 256), F32))
    grot_ref[here, :] = jnp.where(lane_in((BQ, 256), 0, 32), acc[:BQ], acc[BQ:]) * SCORE_SCALE

    @pl.when(i == n - 1)
    def _():
        def put(rows):
            moved = swap64(gkey_ref[rows, :] * SCORE_SCALE)
            grot_ref[rows, :] = jnp.where(lane_in((BQ, 256), 0, 64), grot_ref[rows, :], moved)

        in_rows(grot_ref.shape[0], BQ, put)


def attend_forward(low, rot, val, first):
    t = rot.shape[0]
    n = t // BQ
    whole = lambda i, low: (0, 0)
    row = lambda i, low: (i, 0, 0)
    return pl.pallas_call(
        attend_forward_kernel,
        grid_spec=pltpu.PrefetchScalarGridSpec(
            num_scalar_prefetch=1,
            grid=(n,),
            in_specs=[
                pl.BlockSpec((t, 256), whole),
                pl.BlockSpec((t, 128), whole),
                pl.BlockSpec((1, 1, BQ), row),
            ],
            out_specs=[
                pl.BlockSpec((BQ, 128), lambda i, low: (i, 0)),
                pl.BlockSpec((1, 1, 2 * BQ), row),
            ],
            scratch_shapes=[pltpu.VMEM((t, 256), BF16)],
        ),
        out_shape=[
            jax.ShapeDtypeStruct((t, 128), BF16),
            jax.ShapeDtypeStruct((n, 1, 2 * BQ), F32),
        ],
        compiler_params=pltpu.CompilerParams(vmem_limit_bytes=40 * 2**20),
        cost_estimate=pl.CostEstimate(
            flops=12 * 10**9, bytes_accessed=4 * 2**20, transcendentals=4 * 10**6
        ),
        name="attend_forward",
    )(low, rot, val, first)


def attend_backward(low, rot, val, first, log_all, out, grad):
    t = rot.shape[0]
    n = t // BQ
    whole = lambda i, low: (0, 0)
    row = lambda i, low: (i, 0, 0)
    some = lambda i, low: (i, 0)
    return pl.pallas_call(
        attend_backward_kernel,
        grid_spec=pltpu.PrefetchScalarGridSpec(
            num_scalar_prefetch=1,
            grid=(n,),
            in_specs=[
                pl.BlockSpec((t, 256), whole),
                pl.BlockSpec((t, 128), whole),
                pl.BlockSpec((1, 1, BQ), row),
                pl.BlockSpec((1, 1, 2 * BQ), row),
                pl.BlockSpec((BQ, 128), some),
                pl.BlockSpec((BQ, 128), some),
            ],
            out_specs=[pl.BlockSpec((t, 256), whole), pl.BlockSpec((t, 128), whole)],
            scratch_shapes=[pltpu.VMEM((t, 256), BF16), pltpu.VMEM((t, 256), F32)],
        ),
        out_shape=[jax.ShapeDtypeStruct((t, 256), F32), jax.ShapeDtypeStruct((t, 128), F32)],
        compiler_params=pltpu.CompilerParams(vmem_limit_bytes=40 * 2**20),
        cost_estimate=pl.CostEstimate(
            flops=20 * 10**9, bytes_accessed=8 * 2**20, transcendentals=4 * 10**6
        ),
        name="attend_backward",
    )(low, rot, val, first, log_all, out, grad)


def pack(values, rows=8):
    lines = values.reshape(-1, 128)
    return jnp.pad(lines, ((0, rows - lines.shape[0]), (0, 0)))


def by_row(values):
    return values.reshape(NR, -1, 128)


def by_col(values, nz):
    return values.reshape(nz, -1, 128)


def sum_over_group(operand):
    if lax.axis_size("group") == 2:
        other = lax.ppermute(operand, "group", [(0, 1), (1, 0)])
        return operand.astype(F32) + other.astype(F32)
    return lax.psum(operand, "group").astype(F32)


def at(start, size):
    return pl.ds(pl.multiple_of(start, size), size)


def on_device(
    hidden_in,
    segments,
    attn_gain,
    query_weight,
    key_matrix,
    value_matrix,
    out_weight,
    ffn_gain,
    gate_weight,
    up_weight,
    down_weight,
    cotangent,
):
    row, col = lax.axis_index("row"), lax.axis_index("col")
    nz, groups = lax.axis_size("col"), lax.axis_size("group")
    two = groups == 2
    share = "share" if two else "plain"
    parts = 2 if two else 1
    rows_dev, cols_dev = hidden_in.shape
    tokens = rows_dev * NR
    width = cols_dev * nz
    ffn = gate_weight.shape[1] // nz
    ffn_part = ffn // parts
    depth = cols_dev // parts
    heads = query_weight.shape[1] // nz
    head_part = heads // parts
    every = slice(None)

    seg = segments.reshape(-1)
    numbers = jnp.arange(8, dtype=jnp.int32)
    sizes = jnp.sum((seg[None, :] == numbers[:, None]).astype(jnp.int32), axis=1)
    first = jnp.sum(jnp.where(numbers[:, None] < seg[None, :], sizes[:, None], 0), axis=0)
    places = jnp.arange(tokens, dtype=jnp.int32)
    low = first[::BQ] // BQ
    first_rows = first.reshape(-1, 1, BQ)
    offset = (places - first).astype(F32)
    half_width = HEAD_SIZE // 2
    inverse = ROPE_BASE ** (-(2.0 * jnp.arange(half_width, dtype=F32)) / HEAD_SIZE)
    angles = offset[:, None] * inverse[None, :]
    cosine = jnp.tile(jnp.cos(angles), (1, 4))
    sine = jnp.tile(jnp.sin(angles), (1, 4))

    names = jnp.arange(4 * HEAD_SIZE).reshape(4, 2, half_width)
    order = jnp.concatenate(
        [names[(0, 1, 2, 2), 0].reshape(-1), names[(0, 1, 2, 2), 1].reshape(-1)]
        + [names[3].reshape(-1)] * 2
    )
    permutation = (jnp.arange(4 * HEAD_SIZE)[:, None] == order[None, :]).astype(BF16)

    residual = hidden_in.astype(F32)
    grad_top = cotangent.astype(F32)
    grad_ffn = (RES_SCALE * grad_top).astype(BF16)
    joint_kv = jnp.concatenate(
        [
            key_matrix[:, :HEAD_SIZE],
            value_matrix[:, :HEAD_SIZE],
            key_matrix[:, HEAD_SIZE:],
            value_matrix[:, HEAD_SIZE:],
        ],
        axis=1,
    )
    kv = 2 * HEAD_SIZE
    spread_heads = Spread(
        [query_weight, joint_kv],
        [
            (
                0,
                lambda c, h: (at(h * depth, depth), at(c * heads, heads)),
                0,
                lambda c, h: (at(c * cols_dev + h * depth, depth), pl.ds(0, heads)),
            ),
            (
                1,
                lambda c, h: (at(h * depth, depth), at(c * 2 // nz * kv, kv)),
                0,
                lambda c, h: (at(c * cols_dev + h * depth, depth), pl.ds(heads, kv)),
            ),
        ],
        [(width, heads + kv)],
        share,
    )
    spread_out = Spread(
        [out_weight],
        [
            (
                0,
                lambda c, h: (at(c * heads + h * head_part, head_part), every),
                0,
                lambda c, h: (at(h * head_part, head_part), at(c * cols_dev, cols_dev)),
            )
        ],
        [(heads, width)],
        share,
    )
    (x_all, gain_all, grad_ffn_all), (natural, out_rows) = gather(
        [hidden_in, jnp.broadcast_to(attn_gain[None, :], (8, cols_dev)), grad_ffn],
        0,
        [spread_heads, spread_out],
    )
    joint = dot(natural, permutation, ((1,), (0,))).astype(BF16)

    wide = x_all.astype(F32)
    scale_one = lax.rsqrt(jnp.mean(wide * wide, axis=1) + NORM_EPS)
    normed_one = (wide * scale_one[:, None] * gain_all[:1]).astype(BF16)

    pre = dot(normed_one, joint, ((1,), (0,)))
    pre_one, pre_two = pre[:, :128], pre[:, 128:256]
    rot = jnp.concatenate(
        [pre_one * cosine - pre_two * sine, pre_two * cosine + pre_one * sine], axis=1
    ).astype(BF16)
    val = pre[:, 256:].astype(BF16)
    heads_out, log_all = attend_forward(low, rot, val, first_rows)
    attn_part = dot(heads_out, out_rows, ((1,), (0,))).astype(BF16)

    def units_piece(which):
        return (
            which,
            lambda c, h: (at(h * depth, depth), at(c * ffn, ffn)),
            0,
            lambda c, h: (at(c * cols_dev + h * depth, depth), pl.ds(which * ffn, ffn)),
        )

    spread_gate_up = Spread(
        [gate_weight, up_weight], [units_piece(0), units_piece(1)], [(width, 2 * ffn)], share
    )
    (attn_sum,), (gate_up,) = reduce_scatter([attn_part], 1, [spread_gate_up])
    resid_mid = residual + RES_SCALE * attn_sum

    squares = jnp.sum(resid_mid * resid_mid, axis=1)
    spread_down = Spread(
        [down_weight],
        [
            (
                0,
                lambda c, h: (at(c * ffn + h * ffn_part, ffn_part), every),
                0,
                lambda c, h: (at(h * ffn_part, ffn_part), at(c * cols_dev, cols_dev)),
            )
        ],
        [(ffn, width)],
        share,
    )
    (raw_two, square_all), (down,) = gather(
        [(resid_mid * ffn_gain[None, :]).astype(BF16), pack(squares)], 2, [spread_down]
    )
    square_sum = jnp.sum(square_all.reshape(NR, 8, nz, 128), axis=2)[:, : rows_dev // 128]
    scale_two = lax.rsqrt(square_sum.reshape(tokens) / width + NORM_EPS)

    both = dot(raw_two, gate_up, ((1,), (0,))) * scale_two[:, None]
    gate_pre, up_pre = both[:, :ffn], both[:, ffn:]
    gate_sig = jax.nn.sigmoid(gate_pre)
    gate_act = gate_pre * gate_sig
    hidden_act = (gate_act * up_pre).astype(BF16)
    down_part_sum = dot(hidden_act, down, ((1,), (0,))).astype(BF16)
    down_grad_part = dot(hidden_act, grad_ffn_all, ((0,), (0,))).astype(BF16)
    swaps = []
    if two:
        swaps = [
            Swap(
                down_grad_part,
                [(lambda h: (at(h * ffn_part, ffn_part), every), (every, every))],
                (ffn_part, width),
            )
        ]
    (down_sum,), others = reduce_scatter([down_part_sum], 3, swaps)
    layer_out = (resid_mid + RES_SCALE * down_sum).astype(BF16)

    def half_of(a, axis):
        size = a.shape[axis] // parts
        return lax.dynamic_slice_in_dim(a, lax.axis_index("group") * size, size, axis)

    def plus(a, b):
        return (a.astype(F32) + b.astype(F32)).astype(BF16)

    if two:
        down_grad_part = plus(half_of(down_grad_part, 0), others[0])
    spread_down_grad = Spread(
        [down_grad_part],
        [
            (
                0,
                lambda c, h: (every, at(c * cols_dev, cols_dev)),
                0,
                lambda c, h: (at(c * ffn + h * ffn_part, ffn_part), every),
            )
        ],
        [(ffn * nz, cols_dev)],
        "sum" if two else "plain",
    )

    grad_hidden = dot(grad_ffn_all, down, ((1,), (1,)))
    grad_gate = grad_hidden * up_pre * gate_sig * (1.0 + gate_pre * (1.0 - gate_sig))
    grad_up = grad_hidden * gate_act
    inner_two = jnp.sum(grad_gate * gate_pre + grad_up * up_pre, axis=1)
    grad_pair = jnp.concatenate([grad_gate, grad_up], axis=1)
    grad_pair_scaled = (grad_pair * scale_two[:, None]).astype(BF16)
    grad_two_part = dot(grad_pair.astype(BF16), gate_up, ((1,), (1,))).astype(BF16)
    pair_grad_part = dot(raw_two, grad_pair_scaled, ((0,), (0,))).astype(BF16)
    stats = jnp.tile(
        jnp.pad(by_row(inner_two), ((0, 0), (0, 4), (0, 0))).reshape(NR * 8, 128), (1, nz)
    )
    extras = [spread_down_grad]
    if two:
        extras.append(
            Swap(
                pair_grad_part,
                [
                    (
                        lambda h, m=m: (every, at((2 * m + h) * ffn_part, ffn_part)),
                        (every, pl.ds(m * ffn_part, ffn_part)),
                    )
                    for m in range(2)
                ],
                (width, 2 * ffn_part),
            )
        )
    (grad_two, inner_two_sum), others = reduce_scatter([grad_two_part, stats], 4, extras)
    down_grad = others[0]
    if two:
        pair_grad_part = plus(
            jnp.concatenate(
                [half_of(pair_grad_part[:, :ffn], 1), half_of(pair_grad_part[:, ffn:], 1)], axis=1
            ),
            others[1],
        )
    scale_two_own = lax.dynamic_slice_in_dim(scale_two, row * rows_dev, rows_dev)[:, None]
    inner_two_own = inner_two_sum[: rows_dev // 128].reshape(rows_dev, 1)
    grad_mid = (
        grad_top
        + scale_two_own * ffn_gain[None, :] * grad_two
        - resid_mid * (scale_two_own * scale_two_own * inner_two_own / width)
    )
    ffn_gain_part = jnp.sum(grad_two * resid_mid * scale_two_own, axis=0)
    grad_attn = (RES_SCALE * grad_mid).astype(BF16)

    def grad_piece(which):
        return (
            0,
            lambda c, h: (at(c * cols_dev, cols_dev), pl.ds(which * ffn_part, ffn_part)),
            which,
            lambda c, h: (every, at(c * ffn + h * ffn_part, ffn_part)),
        )

    spread_pair_grad = Spread(
        [pair_grad_part],
        [grad_piece(0), grad_piece(1)],
        [(cols_dev, ffn * nz)] * 2,
        "sum" if two else "plain",
    )
    (grad_attn_all,), (gate_grad, up_grad) = gather([grad_attn], 5, [spread_pair_grad])

    grad_heads = dot(grad_attn_all, out_rows, ((1,), (1,))).astype(BF16)
    out_grad_part = dot(heads_out, grad_attn_all, ((0,), (0,))).astype(BF16)
    grad_rot, grad_val = attend_backward(
        low, rot, val, first_rows, log_all, heads_out, grad_heads
    )
    inner_one = jnp.sum(grad_rot * rot.astype(F32), axis=1) + jnp.sum(
        grad_val * val.astype(F32), axis=1
    )
    grot_one, grot_two = grad_rot[:, :128], grad_rot[:, 128:]
    grad_pre = jnp.concatenate(
        [grot_one * cosine + grot_two * sine, grot_two * cosine - grot_one * sine, grad_val], axis=1
    ).astype(BF16)
    grad_natural = dot(grad_pre, permutation, ((1,), (1,))).astype(BF16)
    grad_one_part = dot(grad_natural, natural, ((1,), (1,))).astype(BF16)
    natural_grad = dot(normed_one, grad_natural, ((0,), (0,)))
    attn_gain_part = jnp.sum(natural_grad * natural.astype(F32), axis=1) / gain_all[0]
    natural_grad = natural_grad.astype(BF16)
    mine = (jnp.arange(nz) == col)[:, None, None]
    gain_lines = jnp.concatenate(
        [by_col(attn_gain_part, nz), jnp.where(mine, pack(ffn_gain_part, 4)[None], 0.0)], axis=1
    )
    lines = jnp.concatenate(
        [
            jnp.broadcast_to(by_row(inner_one)[:, None], (NR, nz, 4, 128)),
            jnp.broadcast_to(gain_lines[None], (NR, nz, 8, 128)),
            jnp.zeros((NR, nz, 4, 128), F32),
        ],
        axis=2,
    )
    stats = jnp.transpose(lines, (0, 2, 1, 3)).reshape(NR * 16, nz * 128)
    spread_small = Spread(
        [out_grad_part, natural_grad],
        [
            (
                0,
                lambda c, h: (every, at(c * cols_dev, cols_dev)),
                0,
                lambda c, h: (at(c * heads, heads), every),
            ),
            (
                1,
                lambda c, h: (at(c * cols_dev, cols_dev), pl.ds(0, heads)),
                1,
                lambda c, h: (every, at(c * heads, heads)),
            ),
            (
                1,
                lambda c, h: (at(c * cols_dev, cols_dev), pl.ds(heads, kv)),
                2,
                lambda c, h: (every, at(c * kv, kv)),
            ),
        ],
        [(heads * nz, cols_dev), (cols_dev, heads * nz), (cols_dev, kv * nz)],
        "twin" if two else "plain",
    )
    (grad_one, last), small = reduce_scatter([grad_one_part, stats], 6, [spread_small])
    scale_one_own = lax.dynamic_slice_in_dim(scale_one, row * rows_dev, rows_dev)[:, None]
    inner_one_own = last[:4].reshape(rows_dev, 1)
    input_grad = (
        grad_mid
        + scale_one_own * attn_gain[None, :] * grad_one
        - residual * (scale_one_own * scale_one_own * inner_one_own / width)
    )
    gain_grads = sum_over_group(last[4:12])
    if two:
        out_grad, query_grad, kv_grad = (
            small[m].astype(F32) + small[m + 3].astype(F32) for m in range(3)
        )
        down_grad, gate_grad, up_grad = (
            a.astype(F32) for a in (down_grad, gate_grad, up_grad)
        )
    else:
        out_grad, query_grad, kv_grad, down_grad, gate_grad, up_grad = (
            lax.psum(a, "group").astype(F32) for a in (*small, down_grad, gate_grad, up_grad)
        )
    kv_grad = jnp.sum(kv_grad.reshape(cols_dev, 2, nz // 2, 2, HEAD_SIZE), axis=2)
    key_grad = kv_grad[:, :, 0].reshape(cols_dev, 2 * HEAD_SIZE)
    value_grad = kv_grad[:, :, 1].reshape(cols_dev, 2 * HEAD_SIZE)
    return (
        layer_out,
        input_grad,
        gain_grads[:4].reshape(cols_dev),
        query_grad,
        key_grad,
        value_grad,
        out_grad,
        gain_grads[4:].reshape(cols_dev),
        gate_grad,
        up_grad,
        down_grad,
    )


def solution(mesh):
    return jax.shard_map(
        on_device,
        mesh=mesh,
        in_specs=(
            P(("group", "row"), "col"),
            P("group", None),
            P("col"),
            P("col", "row"),
            P("col", "row"),
            P("col", "row"),
            P("row", "col"),
            P("col"),
            P("col", "row"),
            P("col", "row"),
            P("row", "col"),
            P(("group", "row"), "col"),
        ),
        out_specs=(
            P(("group", "row"), "col"),
            P(("group", "row"), "col"),
            P("col"),
            P("col", "row"),
            P("col", "row"),
            P("col", "row"),
            P("row", "col"),
            P("col"),
            P("col", "row"),
            P("col", "row"),
            P("row", "col"),
        ),
        check_vma=False,
    )
```

```python
import functools

import jax
import jax.numpy as jnp
from jax import lax
from jax.experimental import pallas as pl
from jax.experimental.pallas import tpu as pltpu
from jax.sharding import PartitionSpec as P

F32, BF16 = jnp.float32, jnp.bfloat16
MESH = pl.DeviceIdType.MESH
DMA = pltpu.SemaphoreType.DMA

MODEL_WIDTH = 2048
HEAD_SIZE = 64
NORM_EPS = 1e-05
ROPE_BASE = 10000000.0
RES_SCALE = 0.22
SCORE_SCALE = 0.015625

NR = 4
BQ = 256
NEG = -1e30
SHORT = pl.CostEstimate(flops=0, bytes_accessed=2**20, transcendentals=0)


def dot(a, b, dims):
    return lax.dot_general(a, b, (dims, ((), ())), preferred_element_type=F32)


def place():
    group, row, col = lax.axis_index("group"), lax.axis_index("row"), lax.axis_index("col")
    other_core = row + 1 - 2 * lax.rem(row, 2)
    other_x = lax.rem(row + 2, NR)
    both = other_x + 1 - 2 * lax.rem(row, 2)
    return group, row, col, other_core, other_x, both


def greet(devices):
    barrier = pltpu.get_barrier_semaphore()
    for device in devices:
        pl.semaphore_signal(barrier, inc=1, device_id=device, device_id_type=MESH)
    return barrier


def block_at(ref, row, col, shape):
    b0, b1 = shape
    return ref.at[pl.ds(pl.multiple_of(row * b0, b0), b0), pl.ds(pl.multiple_of(col * b1, b1), b1)]


class Spread:
    def __init__(self, arrays, pieces, outs, mode):
        self.arrays, self.pieces, self.mode = list(arrays), pieces, mode
        self.base = [jax.ShapeDtypeStruct(o, arrays[0].dtype) for o in outs]
        self.outs = self.base + (self.base if mode == "twin" else [])
        n, nz = len(pieces), lax.axis_size("col")
        self.scratch = [DMA((n, 2))] + [DMA((n, nz))] * (2 if mode == "plain" else 4)

    def bind(self, ins, outs, sems):
        self.i, self.o, self.sems = ins, outs, sems
        self.g, self.r, self.z = place()[:3]

    def src(self, n, col, half):
        which, src, _, _ = self.pieces[n]
        return self.i[which].at[src(col, half)]

    def dst(self, n, col, half, twin=False):
        _, _, which, dst = self.pieces[n]
        return self.o[which + (len(self.base) if twin else 0)].at[dst(col, half)]

    def half(self):
        return self.g if self.mode in ("share", "sum") else 0

    def send(self, n, col):
        return pltpu.make_async_remote_copy(
            src_ref=self.src(n, col, self.half()),
            dst_ref=self.dst(n, self.z, self.half()),
            send_sem=self.sems[1].at[n, col],
            recv_sem=self.sems[2].at[n, self.z],
            device_id=(self.g, self.r, col),
            device_id_type=MESH,
        )

    def arrived(self, n, col):
        return pltpu.make_async_remote_copy(
            src_ref=self.src(n, col, self.half()),
            dst_ref=self.dst(n, col, self.half()),
            send_sem=self.sems[1].at[n, col],
            recv_sem=self.sems[2].at[n, col],
            device_id=(self.g, self.r, col),
            device_id_type=MESH,
        )

    def cross(self, n, col, own=False):
        src = self.src(n, self.z, self.half()) if own else self.dst(n, col, self.half())
        return pltpu.make_async_remote_copy(
            src_ref=src,
            dst_ref=self.dst(n, col, self.half(), self.mode == "twin"),
            send_sem=self.sems[3].at[n, col],
            recv_sem=self.sems[4].at[n, col],
            device_id=(1 - self.g, self.r, self.z),
            device_id_type=MESH,
        )

    def crossed(self, n, col):
        half = 1 - self.g if self.mode in ("share", "sum") else 0
        place_there = self.dst(n, col, half, self.mode == "twin")
        return pltpu.make_async_remote_copy(
            src_ref=place_there,
            dst_ref=place_there,
            send_sem=self.sems[3].at[n, col],
            recv_sem=self.sems[4].at[n, col],
            device_id=(1 - self.g, self.r, self.z),
            device_id_type=MESH,
        )

    def local(self, n):
        halves = (0, 1) if self.mode == "share" else (self.half(),)
        return [
            pltpu.make_async_copy(
                self.src(n, self.z, h), self.dst(n, self.z, h), self.sems[0].at[n, m]
            )
            for m, h in enumerate(halves)
        ]

    def start(self, nz):
        for k in range(1, nz):
            for n in range(len(self.pieces)):
                self.send(n, lax.rem(self.z + k, nz)).start()
        for n in range(len(self.pieces)):
            for copy in self.local(n):
                copy.start()
            if self.mode in ("sum", "twin"):
                self.cross(n, self.z, own=True).start()

    def step(self, k, nz):
        for n in range(len(self.pieces)):
            for near, col in ((self.z - k >= 0, self.z - k), (self.z + k < nz, self.z + k)):

                @pl.when(near)
                def _():
                    self.arrived(n, col).wait_recv()
                    if self.mode != "plain":
                        self.cross(n, col).start()

    def finish(self, nz):
        for n in range(len(self.pieces)):
            for copy in self.local(n):
                copy.wait()
            for k in range(1, nz):
                col = lax.rem(self.z + k, nz)
                self.send(n, col).wait_send()
                if self.mode != "plain":
                    self.crossed(n, col).wait_recv()
                    self.crossed(n, col).wait_send()
            if self.mode in ("sum", "twin"):
                self.crossed(n, self.z).wait_recv()
                self.cross(n, self.z, own=True).wait_send()


class Swap:
    def __init__(self, array, pieces, out):
        self.arrays, self.pieces = [array], pieces
        self.outs = [jax.ShapeDtypeStruct(out, array.dtype)]
        self.scratch = [DMA((len(pieces),))] * 2

    def bind(self, ins, outs, sems):
        self.i, self.o, self.sems = ins[0], outs[0], sems
        self.g, self.r, self.z = place()[:3]

    def copy(self, n):
        src, dst = self.pieces[n]
        return pltpu.make_async_remote_copy(
            src_ref=self.i.at[src(1 - self.g)],
            dst_ref=self.o.at[dst],
            send_sem=self.sems[0].at[n],
            recv_sem=self.sems[1].at[n],
            device_id=(1 - self.g, self.r, self.z),
            device_id_type=MESH,
        )

    def start(self, nz):
        for n in range(len(self.pieces)):
            self.copy(n).start()

    def step(self, k, nz):
        pass

    def finish(self, nz):
        for n in range(len(self.pieces)):
            self.copy(n).wait()


def bind_extras(extras, ins, outs, sems):
    for extra in extras:
        n, m, k = len(extra.arrays), len(extra.outs), len(extra.scratch)
        extra.bind(ins[:n], outs[:m], sems[:k])
        ins, outs, sems = ins[n:], outs[m:], sems[k:]


def greetings(extras, nz, devices):
    g, r, z = place()[:3]
    if any(isinstance(extra, Spread) for extra in extras):
        devices = devices[:2] + [(g, r, lax.rem(z + k, nz)) for k in range(1, nz)]
    if any(isinstance(extra, Swap) or extra.mode != "plain" for extra in extras):
        devices = devices + [(1 - g, r, z)]
    return devices


class Gather:
    def __init__(self, nz, units, ins, outs, sems):
        self.nz, self.units, self.ins, self.outs, self.sems = nz, units, ins, outs, sems
        self.at = place()
        z = self.at[2]
        self.has_left, self.has_right = z > 0, z < nz - 1
        self.right, self.left, self.over_x, self.to_core = 0, nz - 1, 2 * (nz - 1), 3 * nz - 2

    def own_part(self, u):
        i, start, size = self.units[u]
        return self.ins[i].at[pl.ds(start, size), :]

    def slot(self, u, row, col):
        i, start, size = self.units[u]
        b0, b1 = self.ins[i].shape
        return self.outs[i].at[
            pl.ds(pl.multiple_of(row * b0 + start, size), size),
            pl.ds(pl.multiple_of(col * b1, b1), b1),
        ]

    def copy(self, u, src, row, col, where, device):
        return pltpu.make_async_remote_copy(
            src_ref=src,
            dst_ref=self.slot(u, row, col),
            send_sem=self.sems[1].at[u, where],
            recv_sem=self.sems[2].at[u, row, col],
            device_id=device,
            device_id_type=MESH,
        )

    def own(self, u, where, device):
        g, r, z, rc, rx, rxc = self.at
        return self.copy(u, self.own_part(u), r, z, where, device)

    def forward(self, u, row, col, where, device):
        return self.copy(u, self.slot(u, row, col), row, col, where, device)

    def rank(self, col):
        return col - (col > self.at[2]).astype(jnp.int32)

    def local(self, u):
        g, r, z, rc, rx, rxc = self.at
        return pltpu.make_async_copy(self.own_part(u), self.slot(u, r, z), self.sems[0].at[u])

    def begin(self):
        g, r, z, rc, rx, rxc = self.at
        every = range(len(self.units))
        for u in every:

            @pl.when(self.has_right)
            def _():
                self.own(u, self.right, (g, r, z + 1)).start()

            @pl.when(self.has_left)
            def _():
                self.own(u, self.left, (g, r, z - 1)).start()

            self.own(u, self.over_x, (g, rx, z)).start()
        for u in every:
            self.own(u, self.to_core, (g, rc, z)).start()
            self.local(u).start()

    def from_x(self, u, k):
        g, r, z, rc, rx, rxc = self.at
        to_core, nz = self.to_core, self.nz
        for near, col, where in (
            (z - k >= 0, z - k, to_core + 1 if k == 0 else to_core + nz + 1 + z - k),
            (z + k < nz, z + k, to_core + nz + z + k),
        )[: 1 if k == 0 else 2]:

            @pl.when(near)
            def _():
                self.forward(u, rx, col, where, (g, rx, z)).wait_recv()
                self.forward(u, rx, col, where, (g, rc, z)).start()

    def from_z(self, u, k):
        g, r, z, rc, rx, rxc = self.at
        for near, more, col, device, flow in (
            (z - k >= 0, self.has_right, z - k, (g, r, z + 1), self.right),
            (z + k < self.nz, self.has_left, z + k, (g, r, z - 1), self.left),
        ):

            @pl.when(near)
            def _():
                self.forward(u, r, col, flow, (g, rc, z)).wait_recv()
                if k < self.nz - 1:

                    @pl.when(more)
                    def _():
                        self.forward(u, r, col, flow + k, device).start()

                self.forward(u, r, col, self.over_x + 1 + self.rank(col), (g, rx, z)).start()
                self.forward(u, r, col, self.to_core + 2 + self.rank(col), (g, rc, z)).start()

    def finish(self, u):
        g, r, z, rc, rx, rxc = self.at
        for col in range(self.nz):
            self.forward(u, rc, col, self.to_core, (g, rc, z)).wait_recv()
            self.forward(u, rxc, col, self.to_core, (g, rc, z)).wait_recv()
        self.local(u).wait()

    def sent(self, u):
        g, r, z, rc, rx, rxc = self.at
        for where in range(self.to_core + 2 * self.nz):

            def wait(where=where):
                self.own(u, where, (g, rc, z)).wait_send()

            if where < self.left:
                pl.when(self.has_right & (z - where >= 0))(wait)
            elif where < self.over_x:
                pl.when(self.has_left & (z + (where - self.left) < self.nz))(wait)
            else:
                wait()


def gather_sems(units, nz):
    return [DMA((units,)), DMA((units, 5 * nz - 2)), DMA((units, NR, nz))]


def gather_kernel(n, nz, units, extras, *refs):
    n_in, n_out = n + sum(len(e.arrays) for e in extras), n + sum(len(e.outs) for e in extras)
    ins, outs, sems = refs[:n], refs[n_in : n_in + n], refs[n_in + n_out :]
    bind_extras(extras, refs[n:n_in], refs[n_in + n : n_in + n_out], sems[3:])
    work = Gather(nz, units, ins, outs, sems[:3])
    g, r, z, rc, rx, rxc = place()
    devices = greetings(extras, nz, [(g, rc, z), (g, rx, z)])
    barrier = greet(devices)
    if any(isinstance(extra, Spread) for extra in extras):
        pl.semaphore_wait(barrier, len(devices))
    else:

        @pl.when(z > 0)
        def _():
            pl.semaphore_signal(barrier, inc=1, device_id=(g, r, z - 1), device_id_type=MESH)

        @pl.when(z < nz - 1)
        def _():
            pl.semaphore_signal(barrier, inc=1, device_id=(g, r, z + 1), device_id_type=MESH)

        count = (z > 0).astype(jnp.int32) + (z < nz - 1).astype(jnp.int32)
        pl.semaphore_wait(barrier, len(devices) + count)

    every = range(len(units))
    work.begin()
    for extra in extras:
        extra.start(nz)
    for k in range(1, nz):
        for u in every:
            work.from_z(u, k)
            work.from_x(u, k - 1)
        if k > 1:
            for extra in extras:
                extra.step(k - 1, nz)
    for u in every:
        work.from_x(u, nz - 1)
    for extra in extras:
        extra.step(nz - 1, nz)
    for u in every:
        work.finish(u)
        work.sent(u)
    for extra in extras:
        extra.finish(nz)


def flat(lists):
    return [item for some in lists for item in some]


def gather(arrays, collective_id, extras=()):
    n, nz = len(arrays), lax.axis_size("col")
    units = []
    for i, a in enumerate(arrays):
        parts = 2 if a.shape[0] % 256 == 0 else 1
        units += [(i, m * (a.shape[0] // parts), a.shape[0] // parts) for m in range(parts)]
    anywhere = pl.BlockSpec(memory_space=pl.ANY)
    extra_in, extra_out = flat(e.arrays for e in extras), flat(e.outs for e in extras)
    outs = pl.pallas_call(
        functools.partial(gather_kernel, n, nz, units, extras),
        out_shape=[
            jax.ShapeDtypeStruct((a.shape[0] * NR, a.shape[1] * nz), a.dtype) for a in arrays
        ]
        + extra_out,
        in_specs=[anywhere] * (n + len(extra_in)),
        out_specs=[anywhere] * (n + len(extra_out)),
        scratch_shapes=gather_sems(len(units), nz) + flat(e.scratch for e in extras),
        compiler_params=pltpu.CompilerParams(collective_id=collective_id, has_side_effects=True),
        cost_estimate=SHORT,
        name="gather",
    )(*arrays, *extra_in)
    return outs[:n], outs[n:]


def in_rows(total, step, body):
    step = min(step, total)
    if total == step:
        body(pl.ds(0, step))
    else:

        def one(i, carry):
            body(pl.ds(pl.multiple_of(i * step, step), step))
            return carry

        lax.fori_loop(0, total // step, one, 0)


class Scatter:
    def __init__(self, nz, source, out, bufs, sems, load):
        self.nz, self.source, self.out, self.load_it = nz, source, out, load
        self.own = bufs[0] if load else None
        self.from_core, self.half, self.from_x, self.mine, self.from_z = bufs[-5:]
        self.core_send, self.core_recv, self.x_send, self.x_recv, self.z_send, self.z_recv = sems[:6]
        self.load_sem = sems[6] if load else None
        self.at = g, r, z, rc, rx, rxc = place()
        self.pair = z + 1 - 2 * lax.rem(z, 2)
        self.far = lax.rem(z + 2, nz)
        self.order = (lax.rem(self.pair + 2, nz), self.pair, self.far, z)

    def partners(self):
        g, r, z, rc, rx, rxc = self.at
        return [(g, rc, z), (g, rx, z), (g, r, self.pair), (g, r, self.far)]

    def shape(self):
        return self.source.shape[0] // NR, self.source.shape[1] // self.nz

    def block(self, row, step):
        return block_at(self.source, row, self.order[step], self.shape())

    def load(self, way, step):
        g, r, z, rc, rx, rxc = self.at
        return pltpu.make_async_copy(
            self.block((rx, r)[way], step), self.own.at[way, step], self.load_sem.at[way, step]
        )

    def part(self, way, step, rows):
        g, r, z, rc, rx, rxc = self.at
        if self.load_it:
            return self.own[way, step, rows, :].astype(F32)
        return self.block((rx, r)[way], step)[rows, :].astype(F32)

    def remote(self, src, dst, send, recv, device):
        return pltpu.make_async_remote_copy(
            src_ref=src,
            dst_ref=dst,
            send_sem=send,
            recv_sem=recv,
            device_id=device,
            device_id_type=MESH,
        )

    def core(self, way, step):
        g, r, z, rc, rx, rxc = self.at
        return self.remote(
            self.block((rxc, rc)[way], step),
            self.from_core.at[way, step],
            self.core_send.at[way, step],
            self.core_recv.at[way, step],
            (g, rc, z),
        )

    def over_x(self, step):
        g, r, z, rc, rx, rxc = self.at
        return self.remote(
            self.half.at[step],
            self.from_x.at[step],
            self.x_send.at[step],
            self.x_recv.at[step],
            (g, rx, z),
        )

    def along_z(self, step):
        g, r, z, rc, rx, rxc = self.at
        return self.remote(
            self.mine.at[step],
            self.from_z.at[step],
            self.z_send.at[step],
            self.z_recv.at[step],
            (g, r, self.far if step == 2 else self.pair),
        )

    def begin(self):
        for way in range(2):
            for step in range(4):
                self.core(way, step).start()
                if self.load_it:
                    self.load(way, step).start()

    def to_x(self, step):
        if self.load_it:
            self.load(0, step).wait()
        self.core(0, step).wait_recv()

        def add(rows):
            self.half[step, rows, :] = (
                self.part(0, step, rows) + self.from_core[0, step, rows, :].astype(F32)
            ).astype(self.half.dtype)

        in_rows(self.shape()[0], 64, add)
        self.over_x(step).start()

    def to_z(self, step):
        if self.load_it:
            self.load(1, step).wait()
        self.core(1, step).wait_recv()
        self.over_x(step).wait_recv()
        for earlier in {2: (0,), 3: (1, 2)}.get(step, ()):
            self.along_z(earlier).wait_recv()

        def add(rows):
            total = (
                self.part(1, step, rows)
                + self.from_core[1, step, rows, :].astype(F32)
                + self.from_x[step, rows, :].astype(F32)
            )
            for earlier in {2: (0,), 3: (1, 2)}.get(step, ()):
                total = total + self.from_z[earlier, rows, :].astype(F32)
            if step == 3:
                self.out[rows, :] = total
            else:
                self.mine[step, rows, :] = total.astype(self.mine.dtype)

        in_rows(self.shape()[0], 64, add)
        if step < 3:
            self.along_z(step).start()

    def finish(self):
        for step in range(4):
            self.core(0, step).wait_send()
            self.core(1, step).wait_send()
            self.over_x(step).wait_send()
            if step < 3:
                self.along_z(step).wait_send()


def scatter_scratch(shape, dtype, nz, load):
    block = (shape[0] // NR, shape[1] // nz)
    leads = [(2, nz)] * (2 if load else 1) + [(nz,), (nz,), (nz - 1,), (nz - 1,)]
    sems = [DMA((2, nz))] * 2 + [DMA((nz,))] * 4 + ([DMA((2, nz))] if load else [])
    return [pltpu.VMEM(lead + block, dtype) for lead in leads], sems


def scatter_kernel(n, nz, extras, *refs):
    n_in, n_out = n + sum(len(e.arrays) for e in extras), n + sum(len(e.outs) for e in extras)
    ins, outs, rest = refs[:n], refs[n_in : n_in + n], refs[n_in + n_out :]
    works = [
        Scatter(nz, ins[i], outs[i], rest[13 * i : 13 * i + 6], rest[13 * i + 6 : 13 * i + 13], True)
        for i in range(n)
    ]
    bind_extras(extras, refs[n:n_in], refs[n_in + n : n_in + n_out], rest[13 * n :])
    devices = greetings(extras, nz, works[0].partners())
    barrier = greet(devices)
    pl.semaphore_wait(barrier, len(devices))
    for work in works:
        work.begin()
    for work in works:
        for step in range(4):
            work.to_x(step)
        if work is works[0]:
            for extra in extras:
                extra.start(nz)
    for work in works:
        for step in range(4):
            work.to_z(step)
            if work is works[0] and 1 <= step:
                for extra in extras:
                    extra.step(step, nz)
    for work in works:
        work.finish()
    for extra in extras:
        extra.finish(nz)


def reduce_scatter(arrays, collective_id, extras=()):
    n, nz = len(arrays), lax.axis_size("col")
    scratch = []
    for a in arrays:
        scratch += flat(scatter_scratch(a.shape, a.dtype, nz, True))
    anywhere = pl.BlockSpec(memory_space=pl.ANY)
    extra_in, extra_out = flat(e.arrays for e in extras), flat(e.outs for e in extras)
    outs = pl.pallas_call(
        functools.partial(scatter_kernel, n, nz, extras),
        out_shape=[
            jax.ShapeDtypeStruct((a.shape[0] // NR, a.shape[1] // nz), F32) for a in arrays
        ]
        + extra_out,
        in_specs=[anywhere] * (n + len(extra_in)),
        out_specs=[pl.BlockSpec(memory_space=pltpu.VMEM)] * n + [anywhere] * len(extra_out),
        scratch_shapes=scratch + flat(e.scratch for e in extras),
        compiler_params=pltpu.CompilerParams(
            collective_id=collective_id, has_side_effects=True, vmem_limit_bytes=48 * 2**20
        ),
        cost_estimate=SHORT,
        name="reduce_scatter",
    )(*arrays, *extra_in)
    return outs[:n], outs[n:]


def feed_forward_kernel(
    nz,
    early,
    late,
    raw_ref,
    inverse_ref,
    gate_up_ref,
    grad_ref,
    *refs,
):
    n_in, n_out = sum(len(e.arrays) for e in early), sum(len(e.outs) for e in early + late)
    raw_all, down_out, scale_out, grad_two_a, grad_two_b, inner_out, pair_grad, down_grad = refs[
        n_in : n_in + 8
    ]
    down_ref = refs[n_in + 8]
    rest = refs[n_in + 8 + n_out :]
    gate_up, down, x_buf, g_buf, d_buf, unit_a, unit_b, inner, hidden_t, scaled = rest[:10]
    left_buf, right_buf, pair_buf, down_buf = rest[10:14]
    load_sem, in_sem, out_sem, tile_sem, done_sem = rest[14:19]
    sems, rest = rest[19:22], rest[22:]
    units = [(0, 0, raw_ref.shape[0] // 2), (0, raw_ref.shape[0] // 2, raw_ref.shape[0] // 2)]
    size = units[0][2]
    gather_work = Gather(nz, units, [raw_ref], [raw_all], sems)
    works = []
    for source, out in ((unit_a, grad_two_a), (unit_b, grad_two_b), (inner, inner_out)):
        works.append(Scatter(nz, source, out, rest[:5], rest[5:11], False))
        rest = rest[11:]
    bind_extras(
        early + late,
        list(refs[:n_in]) + [down_grad] * len(late),
        refs[n_in + 8 : n_in + 8 + n_out],
        rest,
    )
    g, r, z, rc, rx, rxc = place()
    devices = greetings(early + late, nz, [(g, rc, z), (g, rx, z)])
    barrier = greet(devices)
    pl.semaphore_wait(barrier, len(devices))

    gather_work.begin()
    load_gate_up = pltpu.make_async_copy(gate_up_ref, gate_up, load_sem.at[0])
    load_gate_up.start()
    load_down = pltpu.make_async_copy(down_ref, down, load_sem.at[1])
    for extra in early:
        extra.start(nz)
    inner[...] = jnp.zeros_like(inner)
    for k in range(1, nz):
        for u in range(2):
            gather_work.from_z(u, k)
            gather_work.from_x(u, k - 1)
        if k > 1:
            for extra in early:
                extra.step(k - 1, nz)
    gather_work.from_x(0, nz - 1)
    for extra in early:
        extra.step(nz - 1, nz)
    ffn, width = down.shape
    tile, block = left_buf.shape[2], raw_ref.shape[1]
    tiles = width // tile
    parts = pair_grad.shape[0]

    def tokens_of(u, row):
        return pl.ds(row * 2 * size + u * size, size)

    def fetch(u, row):
        slot = (u * NR + row) % 2
        return [
            pltpu.make_async_copy(
                raw_all.at[tokens_of(u, row), :], x_buf.at[slot], in_sem.at[0, slot]
            ),
        ] + [
            pltpu.make_async_copy(
                grad_ref.at[row * nz + col, pl.ds(u * size, size), :],
                g_buf.at[slot, :, pl.ds(col * block, block)],
                in_sem.at[1 + col, slot],
            )
            for col in range(nz)
        ]

    def put(u, row):
        slot = (u * NR + row) % 2
        same_core, same_x = lax.rem(r + row, 2), lax.rem(r // 2 + row // 2, 2)
        return [
            pltpu.make_async_copy(
                d_buf.at[slot, :, pl.ds(pl.multiple_of(col * block, block), block)],
                down_out.at[same_core, same_x, step, pl.ds(u * size, size), :],
                out_sem.at[step, slot],
            )
            for step, col in enumerate(works[0].order)
        ]

    def chunk(u, row):
        slot = (u * NR + row) % 2
        for copy in fetch(u, row):
            copy.wait()
        if row + 1 < NR:
            for copy in fetch(u, row + 1):
                copy.start()
        if u * NR + row >= 2:
            before = u * NR + row - 2
            for copy in put(before // NR, before % NR):
                copy.wait()
        here = tokens_of(u, row)
        unit = (unit_a, unit_b)[u]
        x = x_buf[slot]
        plain = x.astype(F32) * inverse_ref[...]
        scale = lax.rsqrt(jnp.sum(plain * plain, axis=1, keepdims=True) / width + NORM_EPS)
        scale_out[here, :] = jnp.broadcast_to(scale, (size, 128))
        gate = dot(x, gate_up[:, :ffn], ((1,), (0,))) * scale
        up = dot(x, gate_up[:, ffn:], ((1,), (0,))) * scale
        sig = jax.nn.sigmoid(gate)
        act = gate * sig
        hidden = (act * up).astype(BF16)
        hidden_t[:, here] = hidden.T
        d_buf[slot] = dot(hidden, down[...], ((1,), (0,))).astype(BF16)
        for copy in put(u, row):
            copy.start()
        grad_hidden = dot(g_buf[slot], down[...], ((1,), (1,)))
        grad_gate = grad_hidden * up * sig * (1.0 + gate * (1.0 - sig))
        grad_up = grad_hidden * act
        total = jnp.sum(grad_gate * gate + grad_up * up, axis=1, keepdims=True)
        turned = jnp.broadcast_to(total, (size, 128)).T
        for m in range(size // 128):
            line = turned[:8, m * 128 : (m + 1) * 128]
            at_line = u * (size // 128) + m
            pick = lax.broadcasted_iota(jnp.int32, line.shape, 0) == at_line
            for col in range(nz):
                part = (slice(row * 8, row * 8 + 8), slice(col * 128, col * 128 + 128))
                inner[part] = jnp.where(pick, line, inner[part])
        scaled[here, :ffn] = (grad_gate * scale).astype(BF16)
        scaled[here, ffn:] = (grad_up * scale).astype(BF16)
        back = dot(grad_gate.astype(BF16), gate_up[:, :ffn], ((1,), (1,)))
        back = back + dot(grad_up.astype(BF16), gate_up[:, ffn:], ((1,), (1,)))
        unit[row * size : (row + 1) * size, :] = back.astype(BF16)

    def tile_in(kind, n):
        slot = lax.rem(n, 2)
        if kind == 1:
            return [
                pltpu.make_async_copy(
                    raw_all.at[:, pl.ds(pl.multiple_of(n * tile, tile), tile)],
                    left_buf.at[slot],
                    tile_sem.at[NR, slot],
                )
            ]
        col, inside = n // (block // tile), lax.rem(n, block // tile)
        return [
            pltpu.make_async_copy(
                grad_ref.at[row * nz + col, :, pl.ds(pl.multiple_of(inside * tile, tile), tile)],
                right_buf.at[slot, pl.ds(row * 2 * size, 2 * size), :],
                tile_sem.at[row, slot],
            )
            for row in range(NR)
        ]

    def tile_out(kind, n):
        slot = lax.rem(n, 2)
        where = pl.ds(pl.multiple_of(n * tile, tile), tile)
        half = ffn // parts
        copies = []
        for h in range(parts):
            part = lax.rem(h + g, 2) if parts == 2 else 0
            if kind == 0:
                copies.append((down_buf.at[slot, pl.ds(h * half, half), :], down_grad.at[part, :, where]))
            else:
                for m in range(2):
                    copies.append(
                        (
                            pair_buf.at[slot, :, pl.ds(m * ffn + h * half, half)],
                            pair_grad.at[part, where, pl.ds(m * half, half)],
                        )
                    )
        return [
            pltpu.make_async_copy(src, dst, done_sem.at[kind, m, slot])
            for m, (src, dst) in enumerate(copies)
        ]

    def weight_tiles(kind, low, high):
        def one(n, carry):
            slot = lax.rem(n, 2)
            for copy in tile_in(kind, n):
                copy.wait()

            @pl.when(n + 1 < tiles)
            def _():
                for copy in tile_in(kind, n + 1):
                    copy.start()

            @pl.when(n >= 2)
            def _():
                for copy in tile_out(kind, n - 2):
                    copy.wait()

            if kind == 0:
                down_buf[slot] = dot(hidden_t[...], right_buf[slot], ((1,), (0,))).astype(BF16)
            else:
                pair_buf[slot] = dot(left_buf[slot], scaled[...], ((0,), (0,))).astype(BF16)
            for copy in tile_out(kind, n):
                copy.start()
            return carry

        lax.fori_loop(low, high, one, 0)

    gather_work.finish(0)
    for copy in fetch(0, 0):
        copy.start()
    for extra in early:
        extra.finish(nz)
    load_down.start()
    gather_work.from_x(1, nz - 1)
    load_gate_up.wait()
    load_down.wait()
    for row in range(NR):
        chunk(0, row)
    first, second, third = works
    first.begin()
    gather_work.finish(1)
    for copy in fetch(1, 0):
        copy.start()
    for step in range(4):
        first.to_x(step)
    chunk(1, 0)
    chunk(1, 1)
    first.to_z(0)
    chunk(1, 2)
    first.to_z(1)
    for copy in tile_in(0, 0) + tile_in(1, 0):
        copy.start()
    chunk(1, 3)
    second.begin()
    third.begin()
    first.to_z(2)
    for step in range(4):
        second.to_x(step)
    for step in range(4):
        third.to_x(step)
    first.to_z(3)
    third.to_z(0)
    third.to_z(1)
    weight_tiles(0, 0, tiles)
    third.to_z(2)
    for n in (tiles - 2, tiles - 1):
        for copy in tile_out(0, n):
            copy.wait()
    for extra in late:
        extra.start(nz)
    second.to_z(0)
    weight_tiles(1, 0, tiles // 4)
    second.to_z(1)
    weight_tiles(1, tiles // 4, tiles // 2)
    second.to_z(2)
    weight_tiles(1, tiles // 2, 3 * tiles // 4)
    weight_tiles(1, 3 * tiles // 4, tiles)
    second.to_z(3)
    third.to_z(3)
    for u in range(2):
        gather_work.sent(u)
    for work in works:
        work.finish()
    for row in (NR - 2, NR - 1):
        for copy in put(1, row):
            copy.wait()
    for n in (tiles - 2, tiles - 1):
        for copy in tile_out(1, n):
            copy.wait()
    for extra in late:
        extra.finish(nz)


def feed_forward(raw, inverse, gate_up, grad, collective_id, early, late):
    nz = lax.axis_size("col")
    width, ffn = gate_up.shape[0], gate_up.shape[1] // 2
    tokens, size, tile = raw.shape[0] * NR, raw.shape[0] // 2, 256
    parts = 2 if lax.axis_size("group") == 2 else 1
    anywhere, vmem = pl.BlockSpec(memory_space=pl.ANY), pl.BlockSpec(memory_space=pltpu.VMEM)
    shape = jax.ShapeDtypeStruct
    scatters = [((NR * size, width), BF16)] * 2 + [((NR * 8, nz * 128), F32)]
    extra_in, extra_out = flat(e.arrays for e in early), flat(e.outs for e in early + late)
    outs = pl.pallas_call(
        functools.partial(feed_forward_kernel, nz, early, late),
        out_shape=[
            shape((tokens, width), BF16),
            shape((2, 2, nz) + raw.shape, BF16),
            shape((tokens, 128), F32),
            shape((size, raw.shape[1]), F32),
            shape((size, raw.shape[1]), F32),
            shape((8, 128), F32),
            shape((parts, width, 2 * ffn // parts), BF16),
            shape((parts, ffn // parts, width), BF16),
        ]
        + extra_out,
        in_specs=[anywhere, vmem, anywhere, anywhere] + [anywhere] * len(extra_in),
        out_specs=[anywhere] * 2 + [vmem] * 4 + [anywhere] * (2 + len(extra_out)),
        scratch_shapes=[
            pltpu.VMEM(gate_up.shape, BF16),
            pltpu.VMEM((ffn, width), BF16),
            pltpu.VMEM((2, size, width), BF16),
            pltpu.VMEM((2, size, width), BF16),
            pltpu.VMEM((2, size, width), BF16),
            pltpu.VMEM((NR * size, width), BF16),
            pltpu.VMEM((NR * size, width), BF16),
            pltpu.VMEM((NR * 8, nz * 128), F32),
            pltpu.VMEM((ffn, tokens), BF16),
            pltpu.VMEM((tokens, 2 * ffn), BF16),
            pltpu.VMEM((2, tokens, tile), BF16),
            pltpu.VMEM((2, tokens, tile), BF16),
            pltpu.VMEM((2, tile, 2 * ffn), BF16),
            pltpu.VMEM((2, ffn, tile), BF16),
            DMA((2,)),
            DMA((1 + nz, 2)),
            DMA((nz, 2)),
            DMA((NR + 1, 2)),
            DMA((2, 2 * parts, 2)),
        ]
        + gather_sems(2, nz)
        + flat(flat(scatter_scratch(s, t, nz, False)) for s, t in scatters)
        + flat(e.scratch for e in early + late),
        compiler_params=pltpu.CompilerParams(
            collective_id=collective_id, has_side_effects=True, vmem_limit_bytes=58 * 2**20
        ),
        cost_estimate=SHORT,
        name="feed_forward",
    )(raw, inverse, gate_up, grad, *extra_in)
    return outs[:8], outs[8:]


def swap64(v):
    parts = []
    for i in range(0, v.shape[1], 128):
        parts += [v[:, i + 64 : i + 128], v[:, i : i + 64]]
    return jnp.concatenate(parts, axis=1)


def lane_in(shape, low, high):
    lane = lax.rem(lax.broadcasted_iota(jnp.int32, shape, 1), 128)
    return (lane >= low) & (lane < high)


def stack_heads(v, half):
    zero = jnp.zeros_like(v)
    return jnp.concatenate(
        [
            jnp.where(lane_in(v.shape, 0, half), v, zero),
            jnp.where(lane_in(v.shape, half, 2 * half), v, zero),
        ],
        axis=0,
    )


def live(first, i, j):
    shape = (BQ, 2 * BQ)
    key = lax.broadcasted_iota(jnp.int32, shape, 0) + j * BQ
    query = lax.rem(lax.broadcasted_iota(jnp.int32, shape, 1), BQ) + i * BQ
    return (key <= query) & (key >= first)


def attend_forward_kernel(low_ref, rot_ref, val_ref, first_ref, out_ref, log_ref, keys_ref):
    i = pl.program_id(0)

    @pl.when(i == 0)
    def _():
        keys_ref[...] = swap64(rot_ref[...])

    query = stack_heads(rot_ref[pl.ds(pl.multiple_of(i * BQ, BQ), BQ), :], 32)
    first = jnp.concatenate([first_ref[0], first_ref[0]], axis=1)

    def step(j, state):
        top, total, acc = state
        rows = pl.ds(pl.multiple_of(j * BQ, BQ), BQ)
        scores = dot(keys_ref[rows, :], query, ((1,), (1,))) * SCORE_SCALE
        scores = jnp.where(live(first, i, j), scores, NEG)
        new_top = jnp.maximum(top, jnp.max(scores, axis=0, keepdims=True))
        weights = jnp.exp(scores - new_top)
        fade = jnp.exp(top - new_top)
        total = total * fade + jnp.sum(weights, axis=0, keepdims=True)
        acc = acc * fade + dot(val_ref[rows, :], weights.astype(BF16), ((0,), (0,)))
        return new_top, total, acc

    state = (
        jnp.full((1, 2 * BQ), NEG, F32),
        jnp.zeros((1, 2 * BQ), F32),
        jnp.zeros((128, 2 * BQ), F32),
    )
    top, total, acc = lax.fori_loop(low_ref[i], i, step, step(i, state))
    acc = (acc / total).T
    out_ref[...] = jnp.where(lane_in((BQ, 128), 0, 64), acc[:BQ], acc[BQ:]).astype(BF16)
    log_ref[0] = top + jnp.log(total)


def attend_backward_kernel(
    low_ref,
    rot_ref,
    val_ref,
    first_ref,
    log_ref,
    out_ref,
    grad_ref,
    grot_ref,
    gval_ref,
    keys_ref,
    gkey_ref,
):
    i, n = pl.program_id(0), pl.num_programs(0)

    @pl.when(i == 0)
    def _():
        keys_ref[...] = swap64(rot_ref[...])
        gkey_ref[...] = jnp.zeros_like(gkey_ref)
        gval_ref[...] = jnp.zeros_like(gval_ref)

    here = pl.ds(pl.multiple_of(i * BQ, BQ), BQ)
    query = stack_heads(rot_ref[here, :], 32)
    grad = grad_ref[...]
    grads = stack_heads(grad, 64)
    first = jnp.concatenate([first_ref[0], first_ref[0]], axis=1)
    log_row = log_ref[0]
    product = (grad.astype(F32) * out_ref[...].astype(F32)).T
    center = jnp.concatenate(
        [
            jnp.sum(product[:64], axis=0, keepdims=True),
            jnp.sum(product[64:], axis=0, keepdims=True),
        ],
        axis=1,
    )

    def step(j, acc):
        rows = pl.ds(pl.multiple_of(j * BQ, BQ), BQ)
        key = keys_ref[rows, :]
        scores = dot(key, query, ((1,), (1,))) * SCORE_SCALE
        weights = jnp.where(live(first, i, j), jnp.exp(scores - log_row), 0.0)
        grad_weights = dot(val_ref[rows, :], grads, ((1,), (1,)))
        grad_scores = (weights * (grad_weights - center)).astype(BF16)
        gval_ref[rows, :] += dot(weights.astype(BF16), grads, ((1,), (0,)))
        gkey_ref[rows, :] += dot(grad_scores, query, ((1,), (0,)))
        return acc + dot(grad_scores, key, ((0,), (0,)))

    acc = lax.fori_loop(low_ref[i], i + 1, step, jnp.zeros((2 * BQ, 256), F32))
    grot_ref[here, :] = jnp.where(lane_in((BQ, 256), 0, 32), acc[:BQ], acc[BQ:]) * SCORE_SCALE

    @pl.when(i == n - 1)
    def _():
        def put(rows):
            moved = swap64(gkey_ref[rows, :] * SCORE_SCALE)
            grot_ref[rows, :] = jnp.where(lane_in((BQ, 256), 0, 64), grot_ref[rows, :], moved)

        in_rows(grot_ref.shape[0], BQ, put)


def attend_forward(low, rot, val, first):
    t = rot.shape[0]
    n = t // BQ
    whole = lambda i, low: (0, 0)
    row = lambda i, low: (i, 0, 0)
    return pl.pallas_call(
        attend_forward_kernel,
        grid_spec=pltpu.PrefetchScalarGridSpec(
            num_scalar_prefetch=1,
            grid=(n,),
            in_specs=[
                pl.BlockSpec((t, 256), whole),
                pl.BlockSpec((t, 128), whole),
                pl.BlockSpec((1, 1, BQ), row),
            ],
            out_specs=[
                pl.BlockSpec((BQ, 128), lambda i, low: (i, 0)),
                pl.BlockSpec((1, 1, 2 * BQ), row),
            ],
            scratch_shapes=[pltpu.VMEM((t, 256), BF16)],
        ),
        out_shape=[
            jax.ShapeDtypeStruct((t, 128), BF16),
            jax.ShapeDtypeStruct((n, 1, 2 * BQ), F32),
        ],
        compiler_params=pltpu.CompilerParams(vmem_limit_bytes=40 * 2**20),
        cost_estimate=SHORT,
        name="attend_forward",
    )(low, rot, val, first)


def attend_backward(low, rot, val, first, log_all, out, grad):
    t = rot.shape[0]
    n = t // BQ
    whole = lambda i, low: (0, 0)
    row = lambda i, low: (i, 0, 0)
    some = lambda i, low: (i, 0)
    return pl.pallas_call(
        attend_backward_kernel,
        grid_spec=pltpu.PrefetchScalarGridSpec(
            num_scalar_prefetch=1,
            grid=(n,),
            in_specs=[
                pl.BlockSpec((t, 256), whole),
                pl.BlockSpec((t, 128), whole),
                pl.BlockSpec((1, 1, BQ), row),
                pl.BlockSpec((1, 1, 2 * BQ), row),
                pl.BlockSpec((BQ, 128), some),
                pl.BlockSpec((BQ, 128), some),
            ],
            out_specs=[pl.BlockSpec((t, 256), whole), pl.BlockSpec((t, 128), whole)],
            scratch_shapes=[pltpu.VMEM((t, 256), BF16), pltpu.VMEM((t, 256), F32)],
        ),
        out_shape=[jax.ShapeDtypeStruct((t, 256), F32), jax.ShapeDtypeStruct((t, 128), F32)],
        compiler_params=pltpu.CompilerParams(vmem_limit_bytes=40 * 2**20),
        cost_estimate=SHORT,
        name="attend_backward",
    )(low, rot, val, first, log_all, out, grad)


def assemble_kernel(mine_ref, other_ref, gate_ref, up_ref):
    part = gate_ref.shape[1]
    is_mine = pl.program_id(1) == lax.axis_index("group")

    @pl.when(is_mine)
    def _():
        gate_ref[...] = mine_ref[0, :, :part].astype(F32)
        up_ref[...] = mine_ref[0, :, part:].astype(F32)

    @pl.when(jnp.logical_not(is_mine))
    def _():
        gate_ref[...] = other_ref[0, :, :part].astype(F32)
        up_ref[...] = other_ref[0, :, part:].astype(F32)


def assemble(mine, other):
    nz, depth, part = mine.shape[0], mine.shape[1], mine.shape[2] // 2
    block = pl.BlockSpec((1, depth, 2 * part), lambda c, h: (c, 0, 0))
    out = pl.BlockSpec((depth, part), lambda c, h: (0, 2 * c + h))
    return pl.pallas_call(
        assemble_kernel,
        grid=(nz, 2),
        in_specs=[block, block],
        out_specs=[out, out],
        out_shape=[jax.ShapeDtypeStruct((depth, 2 * nz * part), F32)] * 2,
        compiler_params=pltpu.CompilerParams(vmem_limit_bytes=40 * 2**20),
        cost_estimate=SHORT,
        name="assemble",
    )(mine, other)


def pack(values, rows=8):
    lines = values.reshape(-1, 128)
    return jnp.pad(lines, ((0, rows - lines.shape[0]), (0, 0)))


def by_row(values):
    return values.reshape(NR, -1, 128)


def by_col(values, nz):
    return values.reshape(nz, -1, 128)


def sum_over_group(operand):
    if lax.axis_size("group") == 2:
        other = lax.ppermute(operand, "group", [(0, 1), (1, 0)])
        return operand.astype(F32) + other.astype(F32)
    return lax.psum(operand, "group").astype(F32)


def at(start, size):
    return pl.ds(pl.multiple_of(start, size), size)


def on_device(
    hidden_in,
    segments,
    attn_gain,
    query_weight,
    key_matrix,
    value_matrix,
    out_weight,
    ffn_gain,
    gate_weight,
    up_weight,
    down_weight,
    cotangent,
):
    row, col = lax.axis_index("row"), lax.axis_index("col")
    nz, groups = lax.axis_size("col"), lax.axis_size("group")
    two = groups == 2
    share = "share" if two else "plain"
    parts = 2 if two else 1
    rows_dev, cols_dev = hidden_in.shape
    tokens = rows_dev * NR
    width = cols_dev * nz
    ffn = gate_weight.shape[1] // nz
    ffn_part = ffn // parts
    depth = cols_dev // parts
    heads = query_weight.shape[1] // nz
    head_part = heads // parts
    every = slice(None)

    seg = segments.reshape(-1)
    numbers = jnp.arange(8, dtype=jnp.int32)
    sizes = jnp.sum((seg[None, :] == numbers[:, None]).astype(jnp.int32), axis=1)
    first = jnp.sum(jnp.where(numbers[:, None] < seg[None, :], sizes[:, None], 0), axis=0)
    places = jnp.arange(tokens, dtype=jnp.int32)
    low = first[::BQ] // BQ
    first_rows = first.reshape(-1, 1, BQ)
    offset = (places - first).astype(F32)
    half_width = HEAD_SIZE // 2
    inverse = ROPE_BASE ** (-(2.0 * jnp.arange(half_width, dtype=F32)) / HEAD_SIZE)
    angles = offset[:, None] * inverse[None, :]
    cosine = jnp.tile(jnp.cos(angles), (1, 4))
    sine = jnp.tile(jnp.sin(angles), (1, 4))

    names = jnp.arange(4 * HEAD_SIZE).reshape(4, 2, half_width)
    order = jnp.concatenate(
        [names[(0, 1, 2, 2), 0].reshape(-1), names[(0, 1, 2, 2), 1].reshape(-1)]
        + [names[3].reshape(-1)] * 2
    )
    permutation = (jnp.arange(4 * HEAD_SIZE)[:, None] == order[None, :]).astype(BF16)

    residual = hidden_in.astype(F32)
    grad_top = cotangent.astype(F32)
    grad_ffn = (RES_SCALE * grad_top).astype(BF16)
    joint_kv = jnp.concatenate(
        [
            key_matrix[:, :HEAD_SIZE],
            value_matrix[:, :HEAD_SIZE],
            key_matrix[:, HEAD_SIZE:],
            value_matrix[:, HEAD_SIZE:],
        ],
        axis=1,
    )
    kv = 2 * HEAD_SIZE
    spread_heads = Spread(
        [query_weight, joint_kv],
        [
            (
                0,
                lambda c, h: (at(h * depth, depth), at(c * heads, heads)),
                0,
                lambda c, h: (at(c * cols_dev + h * depth, depth), pl.ds(0, heads)),
            ),
            (
                1,
                lambda c, h: (at(h * depth, depth), at(c * 2 // nz * kv, kv)),
                0,
                lambda c, h: (at(c * cols_dev + h * depth, depth), pl.ds(heads, kv)),
            ),
        ],
        [(width, heads + kv)],
        share,
    )
    spread_out = Spread(
        [out_weight],
        [
            (
                0,
                lambda c, h: (at(c * heads + h * head_part, head_part), every),
                0,
                lambda c, h: (at(h * head_part, head_part), at(c * cols_dev, cols_dev)),
            )
        ],
        [(heads, width)],
        share,
    )
    (x_all, gain_all), (natural, out_rows) = gather(
        [
            hidden_in,
            jnp.concatenate([jnp.broadcast_to(a[None, :], (8, cols_dev)) for a in (attn_gain, ffn_gain)]),
        ],
        0,
        [spread_heads, spread_out],
    )
    joint = dot(natural, permutation, ((1,), (0,))).astype(BF16)
    gain_two_all = gain_all[8:]
    grad_ffn, x_all = lax.optimization_barrier((grad_ffn, x_all))
    grad_ffn_all = lax.all_gather(grad_ffn, ("row", "col"), axis=0, tiled=False)

    wide = x_all.astype(F32)
    scale_one = lax.rsqrt(jnp.mean(wide * wide, axis=1) + NORM_EPS)
    normed_one = (wide * scale_one[:, None] * gain_all[:1]).astype(BF16)

    pre = dot(normed_one, joint, ((1,), (0,)))
    pre_one, pre_two = pre[:, :128], pre[:, 128:256]
    rot = jnp.concatenate(
        [pre_one * cosine - pre_two * sine, pre_two * cosine + pre_one * sine], axis=1
    ).astype(BF16)
    val = pre[:, 256:].astype(BF16)
    heads_out, log_all = attend_forward(low, rot, val, first_rows)
    attn_part = dot(heads_out, out_rows, ((1,), (0,))).astype(BF16)

    def units_piece(which):
        return (
            which,
            lambda c, h: (at(h * depth, depth), at(c * ffn, ffn)),
            0,
            lambda c, h: (at(c * cols_dev + h * depth, depth), pl.ds(which * ffn, ffn)),
        )

    spread_gate_up = Spread(
        [gate_weight, up_weight], [units_piece(0), units_piece(1)], [(width, 2 * ffn)], share
    )
    spread_down = Spread(
        [down_weight],
        [
            (
                0,
                lambda c, h: (at(c * ffn + h * ffn_part, ffn_part), every),
                0,
                lambda c, h: (at(h * ffn_part, ffn_part), at(c * cols_dev, cols_dev)),
            )
        ],
        [(ffn, width)],
        share,
    )
    (attn_sum,), (gate_up,) = reduce_scatter([attn_part], 1, [spread_gate_up])
    resid_mid = residual + RES_SCALE * attn_sum

    late = []
    if two:
        late = [
            Swap(
                jax.ShapeDtypeStruct((parts, ffn_part, width), BF16),
                [(lambda h: (1, every, every), (every, every))],
                (ffn_part, width),
            )
        ]
    (_, down_part_sum, scale_wide, grad_a, grad_b, inner_two_sum, pair_grad_part, down_grad_part), others = (
        feed_forward(
            (resid_mid * ffn_gain[None, :]).astype(BF16),
            1.0 / gain_two_all[:1],
            gate_up,
            grad_ffn_all,
            2,
            [spread_down],
            late,
        )
    )
    grad_two = jnp.concatenate([grad_a, grad_b], axis=0)
    scale_two_own = lax.dynamic_slice_in_dim(scale_wide, row * rows_dev, rows_dev)[:, :1]
    inner_two_own = inner_two_sum[: rows_dev // 128].reshape(rows_dev, 1)
    grad_mid = (
        grad_top
        + scale_two_own * ffn_gain[None, :] * grad_two
        - resid_mid * (scale_two_own * scale_two_own * inner_two_own / width)
    )
    ffn_gain_part = jnp.sum(grad_two * resid_mid * scale_two_own, axis=0)
    grad_attn = (RES_SCALE * grad_mid).astype(BF16)

    def plus(a, b):
        return (a.astype(F32) + b.astype(F32)).astype(BF16)

    if two:
        down_half = plus(down_grad_part[0], others[-1])
    else:
        down_half = down_grad_part[0]
    spread_down_grad = Spread(
        [down_half],
        [
            (
                0,
                lambda c, h: (every, at(c * cols_dev, cols_dev)),
                0,
                lambda c, h: (at(c * ffn + h * ffn_part, ffn_part), every),
            )
        ],
        [(ffn * nz, cols_dev)],
        "sum" if two else "plain",
    )

    (grad_attn_all,), (down_grad,) = gather([grad_attn], 5, [spread_down_grad])

    pair_half = pair_grad_part[0]
    if two:
        pair_half = plus(pair_half, lax.ppermute(pair_grad_part[1], "group", [(0, 1), (1, 0)]))

    pair_half = lax.all_to_all(
        pair_half.reshape(nz, cols_dev, 2 * ffn_part), "col", 0, 0, tiled=True
    )
    pair_other = lax.ppermute(pair_half, "group", [(0, 1), (1, 0)]) if two else pair_half

    def step_over(a, axis, jump):
        count = lax.axis_size(axis)
        if jump == 2:
            pairs = [(m, (m + 2) % count) for m in range(count)]
        else:
            pairs = [(m, m + 1 - 2 * (m % 2)) for m in range(count)]
        return lax.ppermute(a, axis, pairs)

    down_x = plus(down_part_sum[0], step_over(down_part_sum[1], "row", 1))
    down_x, grad_attn_all = lax.optimization_barrier((down_x, grad_attn_all))
    down_z = plus(down_x[0], step_over(down_x[1], "row", 2))
    down_got = step_over(down_z[:2], "col", 1)
    down_far = step_over(plus(down_z[2], down_got[0]), "col", 2)
    down_sum = down_z[3].astype(F32) + down_got[1].astype(F32) + down_far.astype(F32)
    layer_out = (resid_mid + RES_SCALE * down_sum).astype(BF16)

    grad_heads = dot(grad_attn_all, out_rows, ((1,), (1,))).astype(BF16)
    out_grad_part = dot(heads_out, grad_attn_all, ((0,), (0,))).astype(BF16)
    grad_rot, grad_val = attend_backward(
        low, rot, val, first_rows, log_all, heads_out, grad_heads
    )
    inner_one = jnp.sum(grad_rot * rot.astype(F32), axis=1) + jnp.sum(
        grad_val * val.astype(F32), axis=1
    )
    grot_one, grot_two = grad_rot[:, :128], grad_rot[:, 128:]
    grad_pre = jnp.concatenate(
        [grot_one * cosine + grot_two * sine, grot_two * cosine - grot_one * sine, grad_val], axis=1
    ).astype(BF16)
    grad_natural = dot(grad_pre, permutation, ((1,), (1,))).astype(BF16)
    grad_one_part = dot(grad_natural, natural, ((1,), (1,))).astype(BF16)
    natural_grad = dot(normed_one, grad_natural, ((0,), (0,)))
    attn_gain_part = jnp.sum(natural_grad * natural.astype(F32), axis=1) / gain_all[0]
    natural_grad = natural_grad.astype(BF16)
    mine = (jnp.arange(nz) == col)[:, None, None]
    gain_lines = jnp.concatenate(
        [by_col(attn_gain_part, nz), jnp.where(mine, pack(ffn_gain_part, 4)[None], 0.0)], axis=1
    )
    lines = jnp.concatenate(
        [
            jnp.broadcast_to(by_row(inner_one)[:, None], (NR, nz, 4, 128)),
            jnp.broadcast_to(gain_lines[None], (NR, nz, 8, 128)),
            jnp.zeros((NR, nz, 4, 128), F32),
        ],
        axis=2,
    )
    stats = jnp.transpose(lines, (0, 2, 1, 3)).reshape(NR * 16, nz * 128)
    spread_small = Spread(
        [out_grad_part, natural_grad],
        [
            (
                0,
                lambda c, h: (every, at(c * cols_dev, cols_dev)),
                0,
                lambda c, h: (at(c * heads, heads), every),
            ),
            (
                1,
                lambda c, h: (at(c * cols_dev, cols_dev), pl.ds(0, heads)),
                1,
                lambda c, h: (every, at(c * heads, heads)),
            ),
            (
                1,
                lambda c, h: (at(c * cols_dev, cols_dev), pl.ds(heads, kv)),
                2,
                lambda c, h: (every, at(c * kv, kv)),
            ),
        ],
        [(heads * nz, cols_dev), (cols_dev, heads * nz), (cols_dev, kv * nz)],
        "twin" if two else "plain",
    )
    (grad_one, last), small = reduce_scatter(
        [grad_one_part, stats], 6, [spread_small]
    )
    scale_one_own = lax.dynamic_slice_in_dim(scale_one, row * rows_dev, rows_dev)[:, None]
    inner_one_own = last[:4].reshape(rows_dev, 1)
    input_grad = (
        grad_mid
        + scale_one_own * attn_gain[None, :] * grad_one
        - residual * (scale_one_own * scale_one_own * inner_one_own / width)
    )
    gain_grads = sum_over_group(last[4:12])
    if two:
        out_grad, query_grad, kv_grad = (
            small[m].astype(F32) + small[m + 3].astype(F32) for m in range(3)
        )
        down_grad = down_grad.astype(F32)
        gate_grad, up_grad = assemble(pair_half, pair_other)
    else:
        out_grad, query_grad, kv_grad, down_grad, pair_grad = (
            lax.psum(a, "group").astype(F32) for a in (*small, down_grad, pair_half)
        )
        gate_grad, up_grad = (
            jnp.transpose(pair_grad[:, :, m * ffn : (m + 1) * ffn], (1, 0, 2)).reshape(
                cols_dev, nz * ffn
            )
            for m in range(2)
        )
    kv_grad = jnp.sum(kv_grad.reshape(cols_dev, 2, nz // 2, 2, HEAD_SIZE), axis=2)
    key_grad = kv_grad[:, :, 0].reshape(cols_dev, 2 * HEAD_SIZE)
    value_grad = kv_grad[:, :, 1].reshape(cols_dev, 2 * HEAD_SIZE)
    return (
        layer_out,
        input_grad,
        gain_grads[:4].reshape(cols_dev),
        query_grad,
        key_grad,
        value_grad,
        out_grad,
        gain_grads[4:].reshape(cols_dev),
        gate_grad,
        up_grad,
        down_grad,
    )


def solution(mesh):
    return jax.shard_map(
        on_device,
        mesh=mesh,
        in_specs=(
            P(("group", "row"), "col"),
            P("group", None),
            P("col"),
            P("col", "row"),
            P("col", "row"),
            P("col", "row"),
            P("row", "col"),
            P("col"),
            P("col", "row"),
            P("col", "row"),
            P("row", "col"),
            P(("group", "row"), "col"),
        ),
        out_specs=(
            P(("group", "row"), "col"),
            P(("group", "row"), "col"),
            P("col"),
            P("col", "row"),
            P("col", "row"),
            P("col", "row"),
            P("row", "col"),
            P("col"),
            P("col", "row"),
            P("col", "row"),
            P("row", "col"),
        ),
        check_vma=False,
    )
```

```python
import functools

import jax
import jax.numpy as jnp
from jax import lax
from jax.experimental import pallas as pl
from jax.experimental.pallas import tpu as pltpu
from jax.sharding import PartitionSpec as P

F32, BF16 = jnp.float32, jnp.bfloat16
MESH = pl.DeviceIdType.MESH
DMA = pltpu.SemaphoreType.DMA

MODEL_WIDTH = 2048
HEAD_SIZE = 64
NORM_EPS = 1e-05
ROPE_BASE = 10000000.0
RES_SCALE = 0.22
SCORE_SCALE = 0.015625

NR = 4
BQ = 256
NEG = -1e30
SHORT = pl.CostEstimate(flops=0, bytes_accessed=2**20, transcendentals=0)


def dot(a, b, dims):
    return lax.dot_general(a, b, (dims, ((), ())), preferred_element_type=F32)


def place():
    group, row, col = lax.axis_index("group"), lax.axis_index("row"), lax.axis_index("col")
    other_core = row + 1 - 2 * lax.rem(row, 2)
    other_x = lax.rem(row + 2, NR)
    both = other_x + 1 - 2 * lax.rem(row, 2)
    return group, row, col, other_core, other_x, both


def greet(devices):
    barrier = pltpu.get_barrier_semaphore()
    for device in devices:
        pl.semaphore_signal(barrier, inc=1, device_id=device, device_id_type=MESH)
    return barrier


def block_at(ref, row, col, shape):
    b0, b1 = shape
    return ref.at[pl.ds(pl.multiple_of(row * b0, b0), b0), pl.ds(pl.multiple_of(col * b1, b1), b1)]


class Spread:
    def __init__(self, arrays, pieces, outs, mode):
        self.arrays, self.pieces, self.mode = list(arrays), pieces, mode
        self.base = [jax.ShapeDtypeStruct(o, arrays[0].dtype) for o in outs]
        self.outs = self.base + (self.base if mode == "twin" else [])
        n, nz = len(pieces), lax.axis_size("col")
        self.scratch = [DMA((n, 2))] + [DMA((n, nz))] * (2 if mode == "plain" else 4)

    def bind(self, ins, outs, sems):
        self.i, self.o, self.sems = ins, outs, sems
        self.g, self.r, self.z = place()[:3]

    def src(self, n, col, half):
        which, src, _, _ = self.pieces[n]
        return self.i[which].at[src(col, half)]

    def dst(self, n, col, half, twin=False):
        _, _, which, dst = self.pieces[n]
        return self.o[which + (len(self.base) if twin else 0)].at[dst(col, half)]

    def half(self):
        return self.g if self.mode in ("share", "sum") else 0

    def send(self, n, col):
        return pltpu.make_async_remote_copy(
            src_ref=self.src(n, col, self.half()),
            dst_ref=self.dst(n, self.z, self.half()),
            send_sem=self.sems[1].at[n, col],
            recv_sem=self.sems[2].at[n, self.z],
            device_id=(self.g, self.r, col),
            device_id_type=MESH,
        )

    def arrived(self, n, col):
        return pltpu.make_async_remote_copy(
            src_ref=self.src(n, col, self.half()),
            dst_ref=self.dst(n, col, self.half()),
            send_sem=self.sems[1].at[n, col],
            recv_sem=self.sems[2].at[n, col],
            device_id=(self.g, self.r, col),
            device_id_type=MESH,
        )

    def cross(self, n, col, own=False):
        src = self.src(n, self.z, self.half()) if own else self.dst(n, col, self.half())
        return pltpu.make_async_remote_copy(
            src_ref=src,
            dst_ref=self.dst(n, col, self.half(), self.mode == "twin"),
            send_sem=self.sems[3].at[n, col],
            recv_sem=self.sems[4].at[n, col],
            device_id=(1 - self.g, self.r, self.z),
            device_id_type=MESH,
        )

    def crossed(self, n, col):
        half = 1 - self.g if self.mode in ("share", "sum") else 0
        place_there = self.dst(n, col, half, self.mode == "twin")
        return pltpu.make_async_remote_copy(
            src_ref=place_there,
            dst_ref=place_there,
            send_sem=self.sems[3].at[n, col],
            recv_sem=self.sems[4].at[n, col],
            device_id=(1 - self.g, self.r, self.z),
            device_id_type=MESH,
        )

    def local(self, n):
        halves = (0, 1) if self.mode == "share" else (self.half(),)
        return [
            pltpu.make_async_copy(
                self.src(n, self.z, h), self.dst(n, self.z, h), self.sems[0].at[n, m]
            )
            for m, h in enumerate(halves)
        ]

    def start(self, nz):
        for k in range(1, nz):
            for n in range(len(self.pieces)):
                self.send(n, lax.rem(self.z + k, nz)).start()
        for n in range(len(self.pieces)):
            for copy in self.local(n):
                copy.start()
            if self.mode in ("sum", "twin"):
                self.cross(n, self.z, own=True).start()

    def step(self, k, nz):
        for n in range(len(self.pieces)):
            for near, col in ((self.z - k >= 0, self.z - k), (self.z + k < nz, self.z + k)):

                @pl.when(near)
                def _():
                    self.arrived(n, col).wait_recv()
                    if self.mode != "plain":
                        self.cross(n, col).start()

    def finish(self, nz):
        for n in range(len(self.pieces)):
            for copy in self.local(n):
                copy.wait()
            for k in range(1, nz):
                col = lax.rem(self.z + k, nz)
                self.send(n, col).wait_send()
                if self.mode != "plain":
                    self.crossed(n, col).wait_recv()
                    self.crossed(n, col).wait_send()
            if self.mode in ("sum", "twin"):
                self.crossed(n, self.z).wait_recv()
                self.cross(n, self.z, own=True).wait_send()


class Swap:
    def __init__(self, array, pieces, out):
        self.arrays, self.pieces = [array], pieces
        self.outs = [jax.ShapeDtypeStruct(out, array.dtype)]
        self.scratch = [DMA((len(pieces),))] * 2

    def bind(self, ins, outs, sems):
        self.i, self.o, self.sems = ins[0], outs[0], sems
        self.g, self.r, self.z = place()[:3]

    def copy(self, n):
        src, dst = self.pieces[n]
        return pltpu.make_async_remote_copy(
            src_ref=self.i.at[src(1 - self.g)],
            dst_ref=self.o.at[dst],
            send_sem=self.sems[0].at[n],
            recv_sem=self.sems[1].at[n],
            device_id=(1 - self.g, self.r, self.z),
            device_id_type=MESH,
        )

    def start(self, nz):
        for n in range(len(self.pieces)):
            self.copy(n).start()

    def step(self, k, nz):
        pass

    def finish(self, nz):
        for n in range(len(self.pieces)):
            self.copy(n).wait()


def bind_extras(extras, ins, outs, sems):
    for extra in extras:
        n, m, k = len(extra.arrays), len(extra.outs), len(extra.scratch)
        extra.bind(ins[:n], outs[:m], sems[:k])
        ins, outs, sems = ins[n:], outs[m:], sems[k:]


def greetings(extras, nz, devices):
    g, r, z = place()[:3]
    if any(isinstance(extra, Spread) for extra in extras):
        devices = devices[:2] + [(g, r, lax.rem(z + k, nz)) for k in range(1, nz)]
    if any(isinstance(extra, Swap) or extra.mode != "plain" for extra in extras):
        devices = devices + [(1 - g, r, z)]
    return devices


class Gather:
    def __init__(self, nz, units, ins, outs, sems):
        self.nz, self.units, self.ins, self.outs, self.sems = nz, units, ins, outs, sems
        self.at = place()
        z = self.at[2]
        self.has_left, self.has_right = z > 0, z < nz - 1
        self.right, self.left, self.over_x, self.to_core = 0, nz - 1, 2 * (nz - 1), 3 * nz - 2

    def own_part(self, u):
        i, start, size, reach = self.units[u]
        return self.ins[i].at[pl.ds(start, size), :]

    def slot(self, u, row, col):
        i, start, size, reach = self.units[u]
        b0, b1 = self.ins[i].shape
        return self.outs[i].at[
            pl.ds(pl.multiple_of((row if reach else 0) * b0 + start, size), size),
            pl.ds(pl.multiple_of(col * b1, b1), b1),
        ]

    def reaches(self, u):
        return self.units[u][3]

    def copy(self, u, src, row, col, where, device):
        return pltpu.make_async_remote_copy(
            src_ref=src,
            dst_ref=self.slot(u, row, col),
            send_sem=self.sems[1].at[u, where],
            recv_sem=self.sems[2].at[u, row, col],
            device_id=device,
            device_id_type=MESH,
        )

    def own(self, u, where, device):
        g, r, z, rc, rx, rxc = self.at
        return self.copy(u, self.own_part(u), r, z, where, device)

    def forward(self, u, row, col, where, device):
        return self.copy(u, self.slot(u, row, col), row, col, where, device)

    def rank(self, col):
        return col - (col > self.at[2]).astype(jnp.int32)

    def local(self, u):
        g, r, z, rc, rx, rxc = self.at
        return pltpu.make_async_copy(self.own_part(u), self.slot(u, r, z), self.sems[0].at[u])

    def begin(self):
        g, r, z, rc, rx, rxc = self.at
        every = range(len(self.units))
        for u in every:

            @pl.when(self.has_right)
            def _():
                self.own(u, self.right, (g, r, z + 1)).start()

            @pl.when(self.has_left)
            def _():
                self.own(u, self.left, (g, r, z - 1)).start()

            if self.reaches(u):
                self.own(u, self.over_x, (g, rx, z)).start()
        for u in every:
            if self.reaches(u):
                self.own(u, self.to_core, (g, rc, z)).start()
            self.local(u).start()

    def from_x(self, u, k):
        if not self.reaches(u):
            return
        g, r, z, rc, rx, rxc = self.at
        to_core, nz = self.to_core, self.nz
        for near, col, where in (
            (z - k >= 0, z - k, to_core + 1 if k == 0 else to_core + nz + 1 + z - k),
            (z + k < nz, z + k, to_core + nz + z + k),
        )[: 1 if k == 0 else 2]:

            @pl.when(near)
            def _():
                self.forward(u, rx, col, where, (g, rx, z)).wait_recv()
                self.forward(u, rx, col, where, (g, rc, z)).start()

    def from_z(self, u, k):
        g, r, z, rc, rx, rxc = self.at
        for near, more, col, device, flow in (
            (z - k >= 0, self.has_right, z - k, (g, r, z + 1), self.right),
            (z + k < self.nz, self.has_left, z + k, (g, r, z - 1), self.left),
        ):

            @pl.when(near)
            def _():
                self.forward(u, r, col, flow, (g, rc, z)).wait_recv()
                if k < self.nz - 1:

                    @pl.when(more)
                    def _():
                        self.forward(u, r, col, flow + k, device).start()

                if self.reaches(u):
                    self.forward(u, r, col, self.over_x + 1 + self.rank(col), (g, rx, z)).start()
                    self.forward(u, r, col, self.to_core + 2 + self.rank(col), (g, rc, z)).start()

    def from_core(self, u, row):
        g, r, z, rc, rx, rxc = self.at
        for col in range(self.nz):
            self.forward(u, row, col, self.to_core, (g, rc, z)).wait_recv()

    def finish(self, u):
        g, r, z, rc, rx, rxc = self.at
        if self.reaches(u):
            self.from_core(u, rc)
            self.from_core(u, rxc)
        self.local(u).wait()

    def sent(self, u):
        g, r, z, rc, rx, rxc = self.at
        for where in range(self.to_core + 2 * self.nz):

            def wait(where=where):
                self.own(u, where, (g, rc, z)).wait_send()

            if where < self.left:
                pl.when(self.has_right & (z - where >= 0))(wait)
            elif where < self.over_x:
                pl.when(self.has_left & (z + (where - self.left) < self.nz))(wait)
            elif self.reaches(u):
                wait()


def gather_sems(units, nz):
    return [DMA((units,)), DMA((units, 5 * nz - 2)), DMA((units, NR, nz))]


def gather_kernel(n, nz, units, extras, *refs):
    n_in, n_out = n + sum(len(e.arrays) for e in extras), n + sum(len(e.outs) for e in extras)
    ins, outs, sems = refs[:n], refs[n_in : n_in + n], refs[n_in + n_out :]
    bind_extras(extras, refs[n:n_in], refs[n_in + n : n_in + n_out], sems[3:])
    work = Gather(nz, units, ins, outs, sems[:3])
    g, r, z, rc, rx, rxc = place()
    devices = greetings(extras, nz, [(g, rc, z), (g, rx, z)])
    barrier = greet(devices)
    if any(isinstance(extra, Spread) for extra in extras):
        pl.semaphore_wait(barrier, len(devices))
    else:

        @pl.when(z > 0)
        def _():
            pl.semaphore_signal(barrier, inc=1, device_id=(g, r, z - 1), device_id_type=MESH)

        @pl.when(z < nz - 1)
        def _():
            pl.semaphore_signal(barrier, inc=1, device_id=(g, r, z + 1), device_id_type=MESH)

        count = (z > 0).astype(jnp.int32) + (z < nz - 1).astype(jnp.int32)
        pl.semaphore_wait(barrier, len(devices) + count)

    every = range(len(units))
    work.begin()
    for extra in extras:
        extra.start(nz)
    for k in range(1, nz):
        for u in every:
            work.from_z(u, k)
            work.from_x(u, k - 1)
        if k > 1:
            for extra in extras:
                extra.step(k - 1, nz)
    for u in every:
        work.from_x(u, nz - 1)
    for extra in extras:
        extra.step(nz - 1, nz)
    for u in every:
        work.finish(u)
        work.sent(u)
    for extra in extras:
        extra.finish(nz)


def flat(lists):
    return [item for some in lists for item in some]


def gather(arrays, collective_id, extras=(), along_col=()):
    reach = [True] * len(arrays) + [False] * len(along_col)
    arrays = list(arrays) + list(along_col)
    n, nz = len(arrays), lax.axis_size("col")
    units = []
    for i, a in enumerate(arrays):
        parts = 2 if a.shape[0] % 256 == 0 else 1
        size = a.shape[0] // parts
        units += [(i, m * size, size, reach[i]) for m in range(parts)]
    anywhere = pl.BlockSpec(memory_space=pl.ANY)
    extra_in, extra_out = flat(e.arrays for e in extras), flat(e.outs for e in extras)
    outs = pl.pallas_call(
        functools.partial(gather_kernel, n, nz, units, extras),
        out_shape=[
            jax.ShapeDtypeStruct((a.shape[0] * (NR if far else 1), a.shape[1] * nz), a.dtype)
            for a, far in zip(arrays, reach)
        ]
        + extra_out,
        in_specs=[anywhere] * (n + len(extra_in)),
        out_specs=[anywhere] * (n + len(extra_out)),
        scratch_shapes=gather_sems(len(units), nz) + flat(e.scratch for e in extras),
        compiler_params=pltpu.CompilerParams(collective_id=collective_id, has_side_effects=True),
        cost_estimate=SHORT,
        name="gather",
    )(*arrays, *extra_in)
    return outs[:n], outs[n:]


def in_rows(total, step, body):
    step = min(step, total)
    if total == step:
        body(pl.ds(0, step))
    else:

        def one(i, carry):
            body(pl.ds(pl.multiple_of(i * step, step), step))
            return carry

        lax.fori_loop(0, total // step, one, 0)


class Scatter:
    def __init__(self, nz, source, out, bufs, sems, load):
        self.nz, self.source, self.out, self.load_it = nz, source, out, load
        self.own = bufs[0] if load else None
        self.from_core, self.half, self.from_x, self.mine, self.from_z = bufs[-5:]
        self.core_send, self.core_recv, self.x_send, self.x_recv, self.z_send, self.z_recv = sems[:6]
        self.load_sem = sems[6] if load else None
        self.at = g, r, z, rc, rx, rxc = place()
        self.pair = z + 1 - 2 * lax.rem(z, 2)
        self.far = lax.rem(z + 2, nz)
        self.order = (lax.rem(self.pair + 2, nz), self.pair, self.far, z)

    def partners(self):
        g, r, z, rc, rx, rxc = self.at
        return [(g, rc, z), (g, rx, z), (g, r, self.pair), (g, r, self.far)]

    def shape(self):
        return self.source.shape[0] // NR, self.source.shape[1] // self.nz

    def block(self, row, step):
        return block_at(self.source, row, self.order[step], self.shape())

    def load(self, way, step):
        g, r, z, rc, rx, rxc = self.at
        return pltpu.make_async_copy(
            self.block((rx, r)[way], step), self.own.at[way, step], self.load_sem.at[way, step]
        )

    def part(self, way, step, rows):
        g, r, z, rc, rx, rxc = self.at
        if self.load_it:
            return self.own[way, step, rows, :].astype(F32)
        return self.block((rx, r)[way], step)[rows, :].astype(F32)

    def remote(self, src, dst, send, recv, device):
        return pltpu.make_async_remote_copy(
            src_ref=src,
            dst_ref=dst,
            send_sem=send,
            recv_sem=recv,
            device_id=device,
            device_id_type=MESH,
        )

    def core(self, way, step):
        g, r, z, rc, rx, rxc = self.at
        return self.remote(
            self.block((rxc, rc)[way], step),
            self.from_core.at[way, step],
            self.core_send.at[way, step],
            self.core_recv.at[way, step],
            (g, rc, z),
        )

    def over_x(self, step):
        g, r, z, rc, rx, rxc = self.at
        return self.remote(
            self.half.at[step],
            self.from_x.at[step],
            self.x_send.at[step],
            self.x_recv.at[step],
            (g, rx, z),
        )

    def along_z(self, step):
        g, r, z, rc, rx, rxc = self.at
        return self.remote(
            self.mine.at[step],
            self.from_z.at[step],
            self.z_send.at[step],
            self.z_recv.at[step],
            (g, r, self.far if step == 2 else self.pair),
        )

    def begin(self):
        for way in range(2):
            for step in range(4):
                self.core(way, step).start()
                if self.load_it:
                    self.load(way, step).start()

    def to_x(self, step):
        if self.load_it:
            self.load(0, step).wait()
        self.core(0, step).wait_recv()

        def add(rows):
            self.half[step, rows, :] = (
                self.part(0, step, rows) + self.from_core[0, step, rows, :].astype(F32)
            ).astype(self.half.dtype)

        in_rows(self.shape()[0], 64, add)
        self.over_x(step).start()

    def to_z(self, step):
        if self.load_it:
            self.load(1, step).wait()
        self.core(1, step).wait_recv()
        self.over_x(step).wait_recv()
        for earlier in {2: (0,), 3: (1, 2)}.get(step, ()):
            self.along_z(earlier).wait_recv()

        def add(rows):
            total = (
                self.part(1, step, rows)
                + self.from_core[1, step, rows, :].astype(F32)
                + self.from_x[step, rows, :].astype(F32)
            )
            for earlier in {2: (0,), 3: (1, 2)}.get(step, ()):
                total = total + self.from_z[earlier, rows, :].astype(F32)
            if step == 3:
                self.out[rows, :] = total
            else:
                self.mine[step, rows, :] = total.astype(self.mine.dtype)

        in_rows(self.shape()[0], 64, add)
        if step < 3:
            self.along_z(step).start()

    def finish(self):
        for step in range(4):
            self.core(0, step).wait_send()
            self.core(1, step).wait_send()
            self.over_x(step).wait_send()
            if step < 3:
                self.along_z(step).wait_send()


def scatter_scratch(shape, dtype, nz, load):
    block = (shape[0] // NR, shape[1] // nz)
    leads = [(2, nz)] * (2 if load else 1) + [(nz,), (nz,), (nz - 1,), (nz - 1,)]
    sems = [DMA((2, nz))] * 2 + [DMA((nz,))] * 4 + ([DMA((2, nz))] if load else [])
    return [pltpu.VMEM(lead + block, dtype) for lead in leads], sems


def scatter_kernel(n, nz, extras, *refs):
    n_in, n_out = n + sum(len(e.arrays) for e in extras), n + sum(len(e.outs) for e in extras)
    ins, outs, rest = refs[:n], refs[n_in : n_in + n], refs[n_in + n_out :]
    works = [
        Scatter(nz, ins[i], outs[i], rest[13 * i : 13 * i + 6], rest[13 * i + 6 : 13 * i + 13], True)
        for i in range(n)
    ]
    bind_extras(extras, refs[n:n_in], refs[n_in + n : n_in + n_out], rest[13 * n :])
    devices = greetings(extras, nz, works[0].partners())
    barrier = greet(devices)
    pl.semaphore_wait(barrier, len(devices))
    for work in works:
        work.begin()
    for work in works:
        for step in range(4):
            work.to_x(step)
        if work is works[0]:
            for extra in extras:
                extra.start(nz)
    for work in works:
        for step in range(4):
            work.to_z(step)
            if work is works[0] and 1 <= step:
                for extra in extras:
                    extra.step(step, nz)
    for work in works:
        work.finish()
    for extra in extras:
        extra.finish(nz)


def reduce_scatter(arrays, collective_id, extras=()):
    n, nz = len(arrays), lax.axis_size("col")
    scratch = []
    for a in arrays:
        scratch += flat(scatter_scratch(a.shape, a.dtype, nz, True))
    anywhere = pl.BlockSpec(memory_space=pl.ANY)
    extra_in, extra_out = flat(e.arrays for e in extras), flat(e.outs for e in extras)
    outs = pl.pallas_call(
        functools.partial(scatter_kernel, n, nz, extras),
        out_shape=[
            jax.ShapeDtypeStruct((a.shape[0] // NR, a.shape[1] // nz), F32) for a in arrays
        ]
        + extra_out,
        in_specs=[anywhere] * (n + len(extra_in)),
        out_specs=[pl.BlockSpec(memory_space=pltpu.VMEM)] * n + [anywhere] * len(extra_out),
        scratch_shapes=scratch + flat(e.scratch for e in extras),
        compiler_params=pltpu.CompilerParams(
            collective_id=collective_id, has_side_effects=True, vmem_limit_bytes=48 * 2**20
        ),
        cost_estimate=SHORT,
        name="reduce_scatter",
    )(*arrays, *extra_in)
    return outs[:n], outs[n:]


def feed_forward_kernel(
    nz,
    late,
    raw_ref,
    inverse_ref,
    gate_up_ref,
    down_ref,
    grad_ref,
    *refs,
):
    n_out = sum(len(e.outs) for e in late)
    raw_all, scale_out, grad_two_a, grad_two_b, inner_out, down_grad = refs[:6]
    down_outs, pair_grads = refs[6:8], refs[8 : 8 + (2 if late else 1)]
    n_own = 8 + len(pair_grads)
    rest = refs[n_own + n_out :]
    gate_up, down, x_buf, g_buf, d_buf, unit_a, unit_b, inner, hidden_t, scaled = rest[:10]
    left_buf, right_buf, pair_buf, down_buf = rest[10:14]
    load_sem, in_sem, out_sem, tile_sem, done_sem = rest[14:19]
    sems, rest = rest[19:22], rest[22:]
    size = raw_ref.shape[0] // 2
    units = [(0, 0, size, True), (0, size, size, True)]
    gather_work = Gather(nz, units, [raw_ref], [raw_all], sems)
    works = []
    for source, out in ((unit_a, grad_two_a), (unit_b, grad_two_b), (inner, inner_out)):
        works.append(Scatter(nz, source, out, rest[:5], rest[5:11], False))
        rest = rest[11:]
    bind_extras(late, [down_grad] * len(late), refs[n_own : n_own + n_out], rest)
    g, r, z, rc, rx, rxc = place()
    devices = [(g, rc, z), (g, rx, z)] + [(g, r, lax.rem(z + k, nz)) for k in range(1, nz)]
    devices = greetings(late, nz, devices)
    barrier = greet(devices)
    pl.semaphore_wait(barrier, len(devices))

    gather_work.begin()
    load_gate_up = pltpu.make_async_copy(gate_up_ref, gate_up, load_sem.at[0])
    load_gate_up.start()
    load_down = [
        pltpu.make_async_copy(
            down_ref.at[col],
            down.at[:, pl.ds(col * raw_ref.shape[1], raw_ref.shape[1])],
            load_sem.at[1 + col],
        )
        for col in range(nz)
    ]
    for copy in load_down:
        copy.start()
    inner[...] = jnp.zeros_like(inner)
    for k in range(1, nz - 1):
        for u in range(2):
            gather_work.from_z(u, k)
            gather_work.from_x(u, k - 1)
    ffn, width = down.shape
    tile, block = left_buf.shape[2], raw_ref.shape[1]
    tiles = width // tile
    parts = len(pair_grads)
    turns = [
        (0, 0, 0),
        (0, 1, 0),
        (1, 0, 0),
        (1, 1, 0),
        (0, 0, 1),
        (0, 1, 1),
        (1, 0, 1),
        (1, 1, 1),
    ]

    def row_of(turn):
        return ((r, rx), (rc, rxc))[turns[turn][1]][turns[turn][2]]

    def tokens_of(u, row):
        return pl.ds(pl.multiple_of(row * 2 * size + u * size, size), size)

    def fetch(turn):
        slot, u, row = turn % 2, turns[turn][0], row_of(turn)
        return [
            pltpu.make_async_copy(
                raw_all.at[tokens_of(u, row), :], x_buf.at[slot], in_sem.at[0, slot]
            ),
            pltpu.make_async_copy(
                grad_ref.at[tokens_of(u, row), :], g_buf.at[slot], in_sem.at[1, slot]
            ),
        ]

    def put(turn):
        slot, (u, core, side) = turn % 2, turns[turn]
        return [
            pltpu.make_async_copy(
                d_buf.at[slot, :, pl.ds(pl.multiple_of(col * block, block), block)],
                down_outs[core].at[side, step, pl.ds(u * size, size), :],
                out_sem.at[step, slot],
            )
            for step, col in enumerate(works[0].order)
        ]

    def begin(turn):
        u, core, side = turns[turn]
        if core == 1:
            gather_work.from_core(u, row_of(turn))
        elif side == 0:
            gather_work.local(u).wait()
        for copy in fetch(turn):
            copy.start()

    def chunk(turn):
        slot, (u, core, side), row = turn % 2, turns[turn], row_of(turn)
        for copy in fetch(turn):
            copy.wait()
        if turn + 1 < len(turns):
            begin(turn + 1)
        if turn >= 2:
            for copy in put(turn - 2):
                copy.wait()
        here = tokens_of(u, row)
        unit = (unit_a, unit_b)[u]
        x = x_buf[slot]
        plain = x.astype(F32) * inverse_ref[...]
        scale = lax.rsqrt(jnp.sum(plain * plain, axis=1, keepdims=True) / width + NORM_EPS)
        scale_out[here, :] = jnp.broadcast_to(scale, (size, 128))
        gate = dot(x, gate_up[:, :ffn], ((1,), (0,))) * scale
        up = dot(x, gate_up[:, ffn:], ((1,), (0,))) * scale
        sig = jax.nn.sigmoid(gate)
        act = gate * sig
        hidden = (act * up).astype(BF16)
        hidden_t[:, here] = hidden.T
        d_buf[slot] = dot(hidden, down[...], ((1,), (0,))).astype(BF16)
        for copy in put(turn):
            copy.start()
        grad_hidden = dot(g_buf[slot], down[...], ((1,), (1,)))
        grad_gate = grad_hidden * up * sig * (1.0 + gate * (1.0 - sig))
        grad_up = grad_hidden * act
        total = jnp.sum(grad_gate * gate + grad_up * up, axis=1, keepdims=True)
        turned = jnp.broadcast_to(total, (size, 128)).T
        for m in range(size // 128):
            line = turned[:8, m * 128 : (m + 1) * 128]
            at_line = u * (size // 128) + m
            pick = lax.broadcasted_iota(jnp.int32, line.shape, 0) == at_line
            for col in range(nz):
                part = (pl.ds(pl.multiple_of(row * 8, 8), 8), pl.ds(col * 128, 128))
                inner[part] = jnp.where(pick, line, inner[part])
        scaled[here, :ffn] = (grad_gate * scale).astype(BF16)
        scaled[here, ffn:] = (grad_up * scale).astype(BF16)
        back = dot(grad_gate.astype(BF16), gate_up[:, :ffn], ((1,), (1,)))
        back = back + dot(grad_up.astype(BF16), gate_up[:, ffn:], ((1,), (1,)))
        unit[pl.ds(pl.multiple_of(row * size, size), size), :] = back.astype(BF16)

    def tile_in(kind, n):
        slot = lax.rem(n, 2)
        source, buf = ((grad_ref, right_buf), (raw_all, left_buf))[kind]
        return [
            pltpu.make_async_copy(
                source.at[:, pl.ds(pl.multiple_of(n * tile, tile), tile)],
                buf.at[slot],
                tile_sem.at[kind, slot],
            )
        ]

    def tile_out(kind, n):
        slot = lax.rem(n, 2)
        where = pl.ds(pl.multiple_of(n * tile, tile), tile)
        half = ffn // parts
        copies = []
        for part in range(parts):
            h = lax.rem(part + g, 2) if parts == 2 else 0
            if kind == 0:
                copies.append(
                    (
                        down_buf.at[slot, pl.ds(pl.multiple_of(h * half, half), half), :],
                        down_grad.at[part, :, where],
                    )
                )
            else:
                for m in range(2):
                    start = pl.multiple_of(m * ffn + h * half, half)
                    copies.append(
                        (
                            pair_buf.at[slot, :, pl.ds(start, half)],
                            pair_grads[part].at[where, pl.ds(m * half, half)],
                        )
                    )
        return [
            pltpu.make_async_copy(src, dst, done_sem.at[kind, m, slot])
            for m, (src, dst) in enumerate(copies)
        ]

    def weight_tiles(kind, low, high):
        def one(n, carry):
            slot = lax.rem(n, 2)
            for copy in tile_in(kind, n):
                copy.wait()

            @pl.when(n + 1 < tiles)
            def _():
                for copy in tile_in(kind, n + 1):
                    copy.start()

            @pl.when(n >= 2)
            def _():
                for copy in tile_out(kind, n - 2):
                    copy.wait()

            if kind == 0:
                down_buf[slot] = dot(hidden_t[...], right_buf[slot], ((1,), (0,))).astype(BF16)
            else:
                pair_buf[slot] = dot(left_buf[slot], scaled[...], ((0,), (0,))).astype(BF16)
            for copy in tile_out(kind, n):
                copy.start()
            return carry

        lax.fori_loop(low, high, one, 0)

    first, second, third = works
    gather_work.from_z(0, nz - 1)
    gather_work.from_x(0, nz - 2)
    load_gate_up.wait()
    for copy in load_down:
        copy.wait()
    begin(0)
    chunk(0)
    gather_work.from_z(1, nz - 1)
    gather_work.from_x(1, nz - 2)
    chunk(1)
    gather_work.from_x(0, nz - 1)
    chunk(2)
    gather_work.from_x(1, nz - 1)
    chunk(3)
    chunk(4)
    chunk(5)
    first.begin()
    chunk(6)
    for step in range(4):
        first.to_x(step)
    for copy in tile_in(0, 0) + tile_in(1, 0):
        copy.start()
    chunk(7)
    second.begin()
    third.begin()
    first.to_z(0)
    for step in range(4):
        second.to_x(step)
    for step in range(4):
        third.to_x(step)
    first.to_z(1)
    first.to_z(2)
    first.to_z(3)
    third.to_z(0)
    third.to_z(1)
    weight_tiles(0, 0, tiles)
    third.to_z(2)
    for n in (tiles - 2, tiles - 1):
        for copy in tile_out(0, n):
            copy.wait()
    for extra in late:
        extra.start(nz)
    second.to_z(0)
    weight_tiles(1, 0, tiles // 4)
    second.to_z(1)
    weight_tiles(1, tiles // 4, tiles // 2)
    second.to_z(2)
    weight_tiles(1, tiles // 2, 3 * tiles // 4)
    weight_tiles(1, 3 * tiles // 4, tiles)
    second.to_z(3)
    third.to_z(3)
    for u in range(2):
        gather_work.sent(u)
    for work in works:
        work.finish()
    for turn in (len(turns) - 2, len(turns) - 1):
        for copy in put(turn):
            copy.wait()
    for n in (tiles - 2, tiles - 1):
        for copy in tile_out(1, n):
            copy.wait()
    for extra in late:
        extra.finish(nz)


def feed_forward(raw, inverse, gate_up, down, grad, collective_id, late):
    nz = lax.axis_size("col")
    width, ffn = gate_up.shape[0], gate_up.shape[1] // 2
    tokens, size, tile = raw.shape[0] * NR, raw.shape[0] // 2, 256
    parts = 2 if lax.axis_size("group") == 2 else 1
    anywhere, vmem = pl.BlockSpec(memory_space=pl.ANY), pl.BlockSpec(memory_space=pltpu.VMEM)
    shape = jax.ShapeDtypeStruct
    scatters = [((NR * size, width), BF16)] * 2 + [((NR * 8, nz * 128), F32)]
    extra_out = flat(e.outs for e in late)
    outs = pl.pallas_call(
        functools.partial(feed_forward_kernel, nz, late),
        out_shape=[
            shape((tokens, width), BF16),
            shape((tokens, 128), F32),
            shape((size, raw.shape[1]), F32),
            shape((size, raw.shape[1]), F32),
            shape((8, 128), F32),
            shape((parts, ffn // parts, width), BF16),
        ]
        + [shape((2, nz) + raw.shape, BF16)] * 2
        + [shape((width, 2 * ffn // parts), BF16)] * parts
        + extra_out,
        in_specs=[anywhere, vmem] + [anywhere] * 3,
        out_specs=[anywhere] + [vmem] * 4 + [anywhere] * (3 + parts + len(extra_out)),
        scratch_shapes=[
            pltpu.VMEM(gate_up.shape, BF16),
            pltpu.VMEM((ffn, width), BF16),
            pltpu.VMEM((2, size, width), BF16),
            pltpu.VMEM((2, size, width), BF16),
            pltpu.VMEM((2, size, width), BF16),
            pltpu.VMEM((NR * size, width), BF16),
            pltpu.VMEM((NR * size, width), BF16),
            pltpu.VMEM((NR * 8, nz * 128), F32),
            pltpu.VMEM((ffn, tokens), BF16),
            pltpu.VMEM((tokens, 2 * ffn), BF16),
            pltpu.VMEM((2, tokens, tile), BF16),
            pltpu.VMEM((2, tokens, tile), BF16),
            pltpu.VMEM((2, tile, 2 * ffn), BF16),
            pltpu.VMEM((2, ffn, tile), BF16),
            DMA((1 + nz,)),
            DMA((2, 2)),
            DMA((nz, 2)),
            DMA((2, 2)),
            DMA((2, 2 * parts, 2)),
        ]
        + gather_sems(2, nz)
        + flat(flat(scatter_scratch(s, t, nz, False)) for s, t in scatters)
        + flat(e.scratch for e in late),
        compiler_params=pltpu.CompilerParams(
            collective_id=collective_id, has_side_effects=True, vmem_limit_bytes=58 * 2**20
        ),
        cost_estimate=SHORT,
        name="feed_forward",
    )(raw, inverse, gate_up, down, grad)
    return outs[1:6], outs[6:8], outs[8 : 8 + parts], outs[8 + parts :]


def swap64(v):
    parts = []
    for i in range(0, v.shape[1], 128):
        parts += [v[:, i + 64 : i + 128], v[:, i : i + 64]]
    return jnp.concatenate(parts, axis=1)


def lane_in(shape, low, high):
    lane = lax.rem(lax.broadcasted_iota(jnp.int32, shape, 1), 128)
    return (lane >= low) & (lane < high)


def stack_heads(v, half):
    zero = jnp.zeros_like(v)
    return jnp.concatenate(
        [
            jnp.where(lane_in(v.shape, 0, half), v, zero),
            jnp.where(lane_in(v.shape, half, 2 * half), v, zero),
        ],
        axis=0,
    )


def live(first, i, j):
    shape = (BQ, 2 * BQ)
    key = lax.broadcasted_iota(jnp.int32, shape, 0) + j * BQ
    query = lax.rem(lax.broadcasted_iota(jnp.int32, shape, 1), BQ) + i * BQ
    return (key <= query) & (key >= first)


def attend_forward_kernel(
    low_ref,
    x_ref,
    gain_ref,
    natural_ref,
    permutation_ref,
    weight_ref,
    cosine_ref,
    sine_ref,
    first_ref,
    normed_ref,
    scale_ref,
    rot_ref,
    val_ref,
    out_ref,
    log_ref,
    part_ref,
    joint_ref,
    keys_ref,
):
    i = pl.program_id(0)

    @pl.when(i == 0)
    def _():
        joint_ref[...] = dot(natural_ref[...], permutation_ref[...], ((1,), (0,))).astype(BF16)

    here = pl.ds(pl.multiple_of(i * BQ, BQ), BQ)
    x = x_ref[...].astype(F32)
    scale = lax.rsqrt(jnp.sum(x * x, axis=1, keepdims=True) / x.shape[1] + NORM_EPS)
    normed = (x * scale * gain_ref[...]).astype(BF16)
    normed_ref[...] = normed
    scale_ref[...] = jnp.broadcast_to(scale, scale_ref.shape)
    pre = dot(normed, joint_ref[...], ((1,), (0,)))
    one, two = pre[:, :128], pre[:, 128:256]
    cosine, sine = cosine_ref[...], sine_ref[...]
    rot = jnp.concatenate([one * cosine - two * sine, two * cosine + one * sine], axis=1)
    rot = rot.astype(BF16)
    rot_ref[here, :] = rot
    keys_ref[here, :] = swap64(rot)
    val_ref[here, :] = pre[:, 256:].astype(BF16)

    query = stack_heads(rot, 32)
    first = jnp.concatenate([first_ref[0], first_ref[0]], axis=1)

    def step(j, state):
        top, total, acc = state
        rows = pl.ds(pl.multiple_of(j * BQ, BQ), BQ)
        scores = dot(keys_ref[rows, :], query, ((1,), (1,))) * SCORE_SCALE
        scores = jnp.where(live(first, i, j), scores, NEG)
        new_top = jnp.maximum(top, jnp.max(scores, axis=0, keepdims=True))
        weights = jnp.exp(scores - new_top)
        fade = jnp.exp(top - new_top)
        total = total * fade + jnp.sum(weights, axis=0, keepdims=True)
        acc = acc * fade + dot(val_ref[rows, :], weights.astype(BF16), ((0,), (0,)))
        return new_top, total, acc

    state = (
        jnp.full((1, 2 * BQ), NEG, F32),
        jnp.zeros((1, 2 * BQ), F32),
        jnp.zeros((128, 2 * BQ), F32),
    )
    top, total, acc = lax.fori_loop(low_ref[i], i, step, step(i, state))
    acc = (acc / total).T
    out = jnp.where(lane_in((BQ, 128), 0, 64), acc[:BQ], acc[BQ:]).astype(BF16)
    out_ref[...] = out
    log_ref[0] = top + jnp.log(total)
    part_ref[...] = dot(out, weight_ref[...], ((1,), (0,))).astype(BF16)


def attend_backward_kernel(
    low_ref,
    incoming_ref,
    normed_ref,
    natural_ref,
    permutation_ref,
    weight_ref,
    cosine_ref,
    sine_ref,
    rot_ref,
    val_ref,
    first_ref,
    log_ref,
    out_ref,
    part_ref,
    natural_grad_ref,
    weight_grad_ref,
    inner_ref,
    keys_ref,
    gkey_ref,
    gval_ref,
    wgrad_ref,
):
    n = pl.num_programs(0)
    i = n - 1 - pl.program_id(0)

    @pl.when(i == n - 1)
    def _():
        keys_ref[...] = swap64(rot_ref[...])
        gkey_ref[...] = jnp.zeros_like(gkey_ref)
        gval_ref[...] = jnp.zeros_like(gval_ref)
        wgrad_ref[...] = jnp.zeros_like(wgrad_ref)
        natural_grad_ref[...] = jnp.zeros_like(natural_grad_ref)

    here = pl.ds(pl.multiple_of(i * BQ, BQ), BQ)
    incoming, out = incoming_ref[...], out_ref[...]
    grad = dot(incoming, weight_ref[...], ((1,), (1,))).astype(BF16)
    wgrad_ref[...] += dot(out, incoming, ((0,), (0,)))
    query = stack_heads(rot_ref[here, :], 32)
    grads = stack_heads(grad, 64)
    first = jnp.concatenate([first_ref[0], first_ref[0]], axis=1)
    log_row = log_ref[0]
    product = (grad.astype(F32) * out.astype(F32)).T
    center = jnp.concatenate(
        [
            jnp.sum(product[:64], axis=0, keepdims=True),
            jnp.sum(product[64:], axis=0, keepdims=True),
        ],
        axis=1,
    )

    def step(j, acc):
        rows = pl.ds(pl.multiple_of(j * BQ, BQ), BQ)
        key = keys_ref[rows, :]
        scores = dot(key, query, ((1,), (1,))) * SCORE_SCALE
        weights = jnp.where(live(first, i, j), jnp.exp(scores - log_row), 0.0)
        grad_weights = dot(val_ref[rows, :], grads, ((1,), (1,)))
        grad_scores = (weights * (grad_weights - center)).astype(BF16)
        gval_ref[rows, :] += dot(weights.astype(BF16), grads, ((1,), (0,)))
        gkey_ref[rows, :] += dot(grad_scores, query, ((1,), (0,)))
        return acc + dot(grad_scores, key, ((0,), (0,)))

    acc = lax.fori_loop(low_ref[i], i + 1, step, jnp.zeros((2 * BQ, 256), F32))
    own = jnp.where(lane_in((BQ, 256), 0, 32), acc[:BQ], acc[BQ:])
    grot = jnp.where(lane_in((BQ, 256), 0, 64), own, swap64(gkey_ref[here, :])) * SCORE_SCALE
    gval = gval_ref[here, :]
    total = jnp.sum(grot * rot_ref[here, :].astype(F32), axis=1, keepdims=True)
    total = total + jnp.sum(gval * val_ref[here, :].astype(F32), axis=1, keepdims=True)
    turned = jnp.broadcast_to(total, (BQ, 128)).T
    for m in range(BQ // 128):
        inner_ref[pl.ds(i * (BQ // 128) + m, 1), :] = turned[:1, m * 128 : (m + 1) * 128]
    one, two = grot[:, :128], grot[:, 128:]
    cosine, sine = cosine_ref[...], sine_ref[...]
    pre = jnp.concatenate([one * cosine + two * sine, two * cosine - one * sine, gval], axis=1)
    natural = dot(pre.astype(BF16), permutation_ref[...], ((1,), (1,))).astype(BF16)
    part_ref[...] = dot(natural, natural_ref[...], ((1,), (1,))).astype(BF16)
    natural_grad_ref[...] += dot(normed_ref[...], natural, ((0,), (0,)))

    @pl.when(i == 0)
    def _():
        weight_grad_ref[...] = wgrad_ref[...].astype(BF16)


def attend_forward(low, x, gain, natural, permutation, weight, cosine, sine, first):
    t, width = x.shape
    n = t // BQ
    some = lambda i, low: (i, 0)
    row = lambda i, low: (i, 0, 0)
    whole = lambda a: pl.BlockSpec(a.shape, lambda i, low: (0, 0))
    shape = jax.ShapeDtypeStruct
    return pl.pallas_call(
        attend_forward_kernel,
        grid_spec=pltpu.PrefetchScalarGridSpec(
            num_scalar_prefetch=1,
            grid=(n,),
            in_specs=[
                pl.BlockSpec((BQ, width), some),
                whole(gain),
                whole(natural),
                whole(permutation),
                whole(weight),
                pl.BlockSpec((BQ, 128), some),
                pl.BlockSpec((BQ, 128), some),
                pl.BlockSpec((1, 1, BQ), row),
            ],
            out_specs=[
                pl.BlockSpec((BQ, width), some),
                pl.BlockSpec((BQ, 128), some),
                pl.BlockSpec((t, 256), lambda i, low: (0, 0)),
                pl.BlockSpec((t, 128), lambda i, low: (0, 0)),
                pl.BlockSpec((BQ, 128), some),
                pl.BlockSpec((1, 1, 2 * BQ), row),
                pl.BlockSpec((BQ, width), some),
            ],
            scratch_shapes=[
                pltpu.VMEM((width, permutation.shape[1]), BF16),
                pltpu.VMEM((t, 256), BF16),
            ],
        ),
        out_shape=[
            shape((t, width), BF16),
            shape((t, 128), F32),
            shape((t, 256), BF16),
            shape((t, 128), BF16),
            shape((t, 128), BF16),
            shape((n, 1, 2 * BQ), F32),
            shape((t, width), BF16),
        ],
        compiler_params=pltpu.CompilerParams(vmem_limit_bytes=48 * 2**20),
        cost_estimate=SHORT,
        name="attend_forward",
    )(low, x, gain, natural, permutation, weight, cosine, sine, first)


def attend_backward(
    low, incoming, normed, natural, permutation, weight, cosine, sine, rot, val, first, log_all, out
):
    t, width = incoming.shape
    n = t // BQ
    some = lambda s, low: (n - 1 - s, 0)
    row = lambda s, low: (n - 1 - s, 0, 0)
    whole = lambda a: pl.BlockSpec(a.shape, lambda s, low: (0, 0))
    shape = jax.ShapeDtypeStruct
    outs = [
        shape((t, width), BF16),
        shape(natural.shape, F32),
        shape(weight.shape, BF16),
        shape((t // 128, 128), F32),
    ]
    return pl.pallas_call(
        attend_backward_kernel,
        grid_spec=pltpu.PrefetchScalarGridSpec(
            num_scalar_prefetch=1,
            grid=(n,),
            in_specs=[
                pl.BlockSpec((BQ, width), some),
                pl.BlockSpec((BQ, width), some),
                whole(natural),
                whole(permutation),
                whole(weight),
                pl.BlockSpec((BQ, 128), some),
                pl.BlockSpec((BQ, 128), some),
                whole(rot),
                whole(val),
                pl.BlockSpec((1, 1, BQ), row),
                pl.BlockSpec((1, 1, 2 * BQ), row),
                pl.BlockSpec((BQ, 128), some),
            ],
            out_specs=[pl.BlockSpec((BQ, width), some)] + [whole(o) for o in outs[1:]],
            scratch_shapes=[
                pltpu.VMEM((t, 256), BF16),
                pltpu.VMEM((t, 256), F32),
                pltpu.VMEM((t, 128), F32),
                pltpu.VMEM(weight.shape, F32),
            ],
        ),
        out_shape=outs,
        compiler_params=pltpu.CompilerParams(vmem_limit_bytes=48 * 2**20),
        cost_estimate=SHORT,
        name="attend_backward",
    )(low, incoming, normed, natural, permutation, weight, cosine, sine, rot, val, first, log_all, out)


def assemble_kernel(mine_ref, other_ref, gate_ref, up_ref):
    part = gate_ref.shape[1]
    is_mine = pl.program_id(1) == lax.axis_index("group")

    @pl.when(is_mine)
    def _():
        gate_ref[...] = mine_ref[0, :, :part].astype(F32)
        up_ref[...] = mine_ref[0, :, part:].astype(F32)

    @pl.when(jnp.logical_not(is_mine))
    def _():
        gate_ref[...] = other_ref[0, :, :part].astype(F32)
        up_ref[...] = other_ref[0, :, part:].astype(F32)


def assemble(mine, other):
    nz, depth, part = mine.shape[0], mine.shape[1], mine.shape[2] // 2
    block = pl.BlockSpec((1, depth, 2 * part), lambda c, h: (c, 0, 0))
    out = pl.BlockSpec((depth, part), lambda c, h: (0, 2 * c + h))
    return pl.pallas_call(
        assemble_kernel,
        grid=(nz, 2),
        in_specs=[block, block],
        out_specs=[out, out],
        out_shape=[jax.ShapeDtypeStruct((depth, 2 * nz * part), F32)] * 2,
        compiler_params=pltpu.CompilerParams(vmem_limit_bytes=40 * 2**20),
        cost_estimate=pl.CostEstimate(flops=0, bytes_accessed=24 * 2**20, transcendentals=0),
        name="assemble",
    )(mine, other)


def pack(values, rows=8):
    lines = values.reshape(-1, 128)
    return jnp.pad(lines, ((0, rows - lines.shape[0]), (0, 0)))


def by_row(values):
    return values.reshape(NR, -1, 128)


def by_col(values, nz):
    return values.reshape(nz, -1, 128)


def sum_over_group(operand):
    if lax.axis_size("group") == 2:
        other = lax.ppermute(operand, "group", [(0, 1), (1, 0)])
        return operand.astype(F32) + other.astype(F32)
    return lax.psum(operand, "group").astype(F32)


def at(start, size):
    return pl.ds(pl.multiple_of(start, size), size)


def on_device(
    hidden_in,
    segments,
    attn_gain,
    query_weight,
    key_matrix,
    value_matrix,
    out_weight,
    ffn_gain,
    gate_weight,
    up_weight,
    down_weight,
    cotangent,
):
    row, col = lax.axis_index("row"), lax.axis_index("col")
    nz, groups = lax.axis_size("col"), lax.axis_size("group")
    two = groups == 2
    share = "share" if two else "plain"
    parts = 2 if two else 1
    rows_dev, cols_dev = hidden_in.shape
    tokens = rows_dev * NR
    width = cols_dev * nz
    ffn = gate_weight.shape[1] // nz
    ffn_part = ffn // parts
    depth = cols_dev // parts
    heads = query_weight.shape[1] // nz
    head_part = heads // parts
    every = slice(None)

    seg = segments.reshape(-1)
    numbers = jnp.arange(8, dtype=jnp.int32)
    sizes = jnp.sum((seg[None, :] == numbers[:, None]).astype(jnp.int32), axis=1)
    first = jnp.sum(jnp.where(numbers[:, None] < seg[None, :], sizes[:, None], 0), axis=0)
    places = jnp.arange(tokens, dtype=jnp.int32)
    low = first[::BQ] // BQ
    first_rows = first.reshape(-1, 1, BQ)
    offset = (places - first).astype(F32)
    half_width = HEAD_SIZE // 2
    inverse = ROPE_BASE ** (-(2.0 * jnp.arange(half_width, dtype=F32)) / HEAD_SIZE)
    angles = offset[:, None] * jnp.tile(inverse, 4)[None, :]
    cosine, sine = jnp.cos(angles), jnp.sin(angles)

    names = jnp.arange(4 * HEAD_SIZE).reshape(4, 2, half_width)
    order = jnp.concatenate(
        [names[(0, 1, 2, 2), 0].reshape(-1), names[(0, 1, 2, 2), 1].reshape(-1)]
        + [names[3].reshape(-1)] * 2
    )
    permutation = (jnp.arange(4 * HEAD_SIZE)[:, None] == order[None, :]).astype(BF16)

    residual = hidden_in.astype(F32)
    grad_top = cotangent.astype(F32)
    grad_ffn = (RES_SCALE * grad_top).astype(BF16)
    joint_kv = jnp.concatenate(
        [
            key_matrix[:, :HEAD_SIZE],
            value_matrix[:, :HEAD_SIZE],
            key_matrix[:, HEAD_SIZE:],
            value_matrix[:, HEAD_SIZE:],
        ],
        axis=1,
    )
    kv = 2 * HEAD_SIZE
    spread_heads = Spread(
        [query_weight, joint_kv],
        [
            (
                0,
                lambda c, h: (at(h * depth, depth), at(c * heads, heads)),
                0,
                lambda c, h: (at(c * cols_dev + h * depth, depth), pl.ds(0, heads)),
            ),
            (
                1,
                lambda c, h: (at(h * depth, depth), at(c * 2 // nz * kv, kv)),
                0,
                lambda c, h: (at(c * cols_dev + h * depth, depth), pl.ds(heads, kv)),
            ),
        ],
        [(width, heads + kv)],
        share,
    )
    spread_out = Spread(
        [out_weight],
        [
            (
                0,
                lambda c, h: (at(c * heads + h * head_part, head_part), every),
                0,
                lambda c, h: (at(h * head_part, head_part), at(c * cols_dev, cols_dev)),
            )
        ],
        [(heads, width)],
        share,
    )
    (x_all, gain_all, grad_col), (natural, out_rows) = gather(
        [
            hidden_in,
            jnp.concatenate([jnp.broadcast_to(a[None, :], (8, cols_dev)) for a in (attn_gain, ffn_gain)]),
        ],
        0,
        [spread_heads, spread_out],
        [grad_ffn],
    )
    gain_two_all = gain_all[8:]
    down_weight, x_all = lax.optimization_barrier((down_weight, x_all))
    down = lax.all_to_all(down_weight.reshape(nz, ffn, cols_dev), "col", 0, 0, tiled=True)
    grad_ffn_all = lax.all_gather(grad_col, "row", axis=0, tiled=True)

    normed_one, scale_one, rot, val, heads_out, log_all, attn_part = attend_forward(
        low, x_all, gain_all[:1], natural, permutation, out_rows, cosine, sine, first_rows
    )

    def units_piece(which):
        return (
            which,
            lambda c, h: (at(h * depth, depth), at(c * ffn, ffn)),
            0,
            lambda c, h: (at(c * cols_dev + h * depth, depth), pl.ds(which * ffn, ffn)),
        )

    spread_gate_up = Spread(
        [gate_weight, up_weight], [units_piece(0), units_piece(1)], [(width, 2 * ffn)], share
    )
    (attn_sum,), (gate_up,) = reduce_scatter([attn_part], 1, [spread_gate_up])
    resid_mid = residual + RES_SCALE * attn_sum

    late = []
    if two:
        late = [
            Swap(
                jax.ShapeDtypeStruct((parts, ffn_part, width), BF16),
                [(lambda h: (1, every, every), (every, every))],
                (ffn_part, width),
            )
        ]
    (scale_wide, grad_a, grad_b, inner_two_sum, down_grad_part), down_parts, pair_parts, others = (
        feed_forward(
            (resid_mid * ffn_gain[None, :]).astype(BF16),
            1.0 / gain_two_all[:1],
            gate_up,
            down,
            grad_ffn_all,
            2,
            late,
        )
    )
    grad_two = jnp.concatenate([grad_a, grad_b], axis=0)
    scale_two_own = lax.dynamic_slice_in_dim(scale_wide, row * rows_dev, rows_dev)[:, :1]
    inner_two_own = inner_two_sum[: rows_dev // 128].reshape(rows_dev, 1)
    grad_mid = (
        grad_top
        + scale_two_own * ffn_gain[None, :] * grad_two
        - resid_mid * (scale_two_own * scale_two_own * inner_two_own / width)
    )
    ffn_gain_part = jnp.sum(grad_two * resid_mid * scale_two_own, axis=0)
    grad_attn = (RES_SCALE * grad_mid).astype(BF16)

    def plus(a, b):
        return (a.astype(F32) + b.astype(F32)).astype(BF16)

    if two:
        down_half = plus(down_grad_part[0], others[-1])
    else:
        down_half = down_grad_part[0]
    spread_down_grad = Spread(
        [down_half],
        [
            (
                0,
                lambda c, h: (every, at(c * cols_dev, cols_dev)),
                0,
                lambda c, h: (at(c * ffn + h * ffn_part, ffn_part), every),
            )
        ],
        [(ffn * nz, cols_dev)],
        "sum" if two else "plain",
    )

    (grad_attn_all,), (down_grad,) = gather([grad_attn], 5, [spread_down_grad])

    pair_half = pair_parts[0]
    if two:
        swapped = lax.ppermute(pair_parts[1], "group", [(0, 1), (1, 0)])
        swapped, grad_attn_all = lax.optimization_barrier((swapped, grad_attn_all))
        pair_half = plus(pair_half, swapped)
    pair_half = lax.all_to_all(
        pair_half.reshape(nz, cols_dev, 2 * ffn_part), "col", 0, 0, tiled=True
    )

    def step_over(a, axis, jump):
        count = lax.axis_size(axis)
        near = [m + 1 - 2 * (m % 2) for m in range(count)]
        goal = [(m + 2) % count if jump == 2 else (near[m] + jump - 1) % count for m in range(count)]
        return lax.ppermute(a, axis, list(enumerate(goal)))

    from_core = step_over(down_parts[1], "row", 1)
    from_core, grad_attn_all = lax.optimization_barrier((from_core, grad_attn_all))
    down_away = plus(down_parts[0][1], from_core[1])
    from_x = step_over(down_away, "row", 2)

    grad_one_part, natural_grad, out_grad_part, inner_one = attend_backward(
        low,
        grad_attn_all,
        normed_one,
        natural,
        permutation,
        out_rows,
        cosine,
        sine,
        rot,
        val,
        first_rows,
        log_all,
        heads_out,
    )
    grad_one_part, from_x, pair_half = lax.optimization_barrier((grad_one_part, from_x, pair_half))
    pair_other = lax.ppermute(pair_half, "group", [(0, 1), (1, 0)]) if two else pair_half
    down_z = (
        down_parts[0][0].astype(F32) + from_core[0].astype(F32) + from_x.astype(F32)
    ).astype(BF16)
    down_got = [step_over(down_z[m], "col", jump) for m, jump in enumerate((3, 1, 2))]
    attn_gain_part = jnp.sum(natural_grad * natural.astype(F32), axis=1) / gain_all[0]
    natural_grad = natural_grad.astype(BF16)
    mine = (jnp.arange(nz) == col)[:, None, None]
    gain_lines = jnp.concatenate(
        [by_col(attn_gain_part, nz), jnp.where(mine, pack(ffn_gain_part, 4)[None], 0.0)], axis=1
    )
    lines = jnp.concatenate(
        [
            jnp.broadcast_to(by_row(inner_one)[:, None], (NR, nz, 4, 128)),
            jnp.broadcast_to(gain_lines[None], (NR, nz, 8, 128)),
            jnp.zeros((NR, nz, 4, 128), F32),
        ],
        axis=2,
    )
    stats = jnp.transpose(lines, (0, 2, 1, 3)).reshape(NR * 16, nz * 128)
    spread_small = Spread(
        [out_grad_part, natural_grad],
        [
            (
                0,
                lambda c, h: (every, at(c * cols_dev, cols_dev)),
                0,
                lambda c, h: (at(c * heads, heads), every),
            ),
            (
                1,
                lambda c, h: (at(c * cols_dev, cols_dev), pl.ds(0, heads)),
                1,
                lambda c, h: (every, at(c * heads, heads)),
            ),
            (
                1,
                lambda c, h: (at(c * cols_dev, cols_dev), pl.ds(heads, kv)),
                2,
                lambda c, h: (every, at(c * kv, kv)),
            ),
        ],
        [(heads * nz, cols_dev), (cols_dev, heads * nz), (cols_dev, kv * nz)],
        "twin" if two else "plain",
    )
    (grad_one, last), small = reduce_scatter(
        [grad_one_part, stats], 6, [spread_small]
    )
    scale_one_own = lax.dynamic_slice_in_dim(scale_one, row * rows_dev, rows_dev)[:, :1]
    inner_one_own = last[:4].reshape(rows_dev, 1)
    input_grad = (
        grad_mid
        + scale_one_own * attn_gain[None, :] * grad_one
        - residual * (scale_one_own * scale_one_own * inner_one_own / width)
    )
    gain_grads = sum_over_group(last[4:12])
    if two:
        out_grad, query_grad, kv_grad = (
            small[m].astype(F32) + small[m + 3].astype(F32) for m in range(3)
        )
        down_grad = down_grad.astype(F32)
        gate_grad, up_grad = assemble(pair_half, pair_other)
        gate_grad, up_grad, out_grad, query_grad, kv_grad, down_z = lax.optimization_barrier(
            (gate_grad, up_grad, out_grad, query_grad, kv_grad, down_z)
        )
    else:
        out_grad, query_grad, kv_grad, down_grad, pair_grad = (
            lax.psum(a, "group").astype(F32) for a in (*small, down_grad, pair_half)
        )
        gate_grad, up_grad = (
            jnp.transpose(pair_grad[:, :, m * ffn : (m + 1) * ffn], (1, 0, 2)).reshape(
                cols_dev, nz * ffn
            )
            for m in range(2)
        )
    down_sum = down_z[3].astype(F32) + sum(a.astype(F32) for a in down_got)
    layer_out = (resid_mid + RES_SCALE * down_sum).astype(BF16)
    shared = [
        sum(kv_grad[:, c * kv : (c + 1) * kv] for c in range(m * nz // 2, (m + 1) * nz // 2))
        for m in range(2)
    ]
    key_grad = jnp.concatenate([a[:, :HEAD_SIZE] for a in shared], axis=1)
    value_grad = jnp.concatenate([a[:, HEAD_SIZE:] for a in shared], axis=1)
    return (
        layer_out,
        input_grad,
        gain_grads[:4].reshape(cols_dev),
        query_grad,
        key_grad,
        value_grad,
        out_grad,
        gain_grads[4:].reshape(cols_dev),
        gate_grad,
        up_grad,
        down_grad,
    )


def solution(mesh):
    return jax.shard_map(
        on_device,
        mesh=mesh,
        in_specs=(
            P(("group", "row"), "col"),
            P("group", None),
            P("col"),
            P("col", "row"),
            P("col", "row"),
            P("col", "row"),
            P("row", "col"),
            P("col"),
            P("col", "row"),
            P("col", "row"),
            P("row", "col"),
            P(("group", "row"), "col"),
        ),
        out_specs=(
            P(("group", "row"), "col"),
            P(("group", "row"), "col"),
            P("col"),
            P("col", "row"),
            P("col", "row"),
            P("col", "row"),
            P("row", "col"),
            P("col"),
            P("col", "row"),
            P("col", "row"),
            P("row", "col"),
        ),
        check_vma=False,
    )
```
